256 devices in a mesh: tensor: 16 (over z, core), context: 16 (over y, x).
Axes of the slice: x: 4, y: 4, z: 8, core: 2. Of those that a mesh axis runs over, the one named last changes fastest.
Arguments:
- hidden: bfloat16 [4096, 8192], P(('context', 'tensor')), may hold values from -6 to 6
- w_proj: bfloat16 [8192, 12288], P(None, 'tensor'), may hold values from -0.0625 to 0.0625
- w_dt: bfloat16 [128, 8192], P('tensor'), may hold values from -0.0625 to 0.0625
- dt_bias: float32 [128], P('tensor'), may hold values from -9 to -3
- a_log: float32 [128], P('tensor'), may hold values from 0 to 0.6
- d_skip: float32 [128], P('tensor'), may hold values from 0.5 to 1.5
- doc_lengths: int32 [8], replicated, may hold values from 1 to 1920, as said below
- grad_out: bfloat16 [4096, 8192], P('context', 'tensor'), may hold values from -3 to 3
Outputs:
- ssd_out: bfloat16 [4096, 8192], P('context', 'tensor')
- grad_hidden: bfloat16 [4096, 8192], P(('context', 'tensor'))
The draws below stay inside these ranges and needn't reach their ends.
Inputs may be any that keep to these rules, and one draw needn't show every extreme that they name: `doc_lengths`: the 8 lengths sum to 4096; the first document has exactly 1920 tokens and the second exactly 448.
All inputs are finite; a program needn't handle non-finite values.
Results may differ from the reference program's by a relative error of at most 0.029.
Values may be sent and summed in bfloat16 or wider, within the bound.
A program may use at most 128 MiB of HBM per device.

```python
import jax
import jax.numpy as jnp
from jax import lax

D = 8192
HEAD_DIM = 64
STATE = 128
HEADS_DEV = 8
BLOCK_LEN = 128
MX_BLOCK = 32
DOCS = 8
TOK_DEV = 256
HEADS = 128
GROUPS = 16
PROJ_DEV = 768
TOKENS = 4096


def draw_doc_lengths(key, part):
    key = jax.random.fold_in(key, 11)
    head_length = TOKENS // 2 - TOK_DEV // 2
    second_length = TOK_DEV + TOK_DEV // 2 + TOK_DEV // 4
    middle_total = TOKENS - head_length - second_length
    shuffled = jax.random.permutation(key, middle_total - 1)
    cuts = jnp.sort(shuffled[:DOCS - 3] + 1).astype(jnp.int32)
    bounds = jnp.concatenate([jnp.zeros((1,), jnp.int32), cuts, jnp.full((1,), middle_total, jnp.int32)])
    middle = (bounds[1:] - bounds[:-1]).astype(jnp.int32)
    first = jnp.full((1,), head_length, jnp.int32)
    second = jnp.full((1,), second_length, jnp.int32)
    return jnp.concatenate([first, second, middle]).astype(jnp.int32)


def draw_dt_bias(key, part):
    key = jax.random.fold_in(key, 23)
    pick_key, slow_key, fast_key = jax.random.split(key, 3)
    slow_share = 0.5
    picks = jax.random.uniform(pick_key, (HEADS,), jnp.float32)
    slow_values = jax.random.uniform(slow_key, (HEADS,), jnp.float32, -9.0, -8.0)
    fast_values = jax.random.uniform(fast_key, (HEADS,), jnp.float32, -4.5, -3.0)
    return jnp.where(picks < slow_share, slow_values, fast_values).astype(jnp.float32)


def draw_grad_out(key, part):
    key = jax.random.fold_in(key, 29)
    mean_key, noise_key = jax.random.split(key)
    column_mean = jax.random.uniform(mean_key, (1, HEADS * HEAD_DIM), jnp.float32, -0.6, 0.6)
    noise = 0.9 * jax.random.normal(noise_key, (TOKENS, HEADS * HEAD_DIM), jnp.float32)
    return jnp.clip(column_mean + noise, -3.0, 3.0).astype(jnp.bfloat16)


def shard_levels(stream_key, shape, shards, smallest, high):
    factor_of = 1.0
    for axis_at, blocks in shards:
        steps = jax.random.uniform(jax.random.fold_in(jax.random.fold_in(stream_key, 6), axis_at), (blocks,), jnp.float32, smallest / len(shards), high / len(shards))
        factor_of = factor_of * jnp.repeat(jnp.exp(steps), shape[axis_at] // blocks).reshape((-1,) + (1,) * (len(shape) - 1 - axis_at))
    return factor_of


def centred(rng, dims, spread, bound, cuts=(), held_as=jnp.bfloat16):
    values = spread * jax.random.normal(rng, dims, jnp.float32)
    if cuts:
        values = values * shard_levels(rng, dims, cuts, -0.22, 0.18)
    return jnp.clip(values, -bound, bound).astype(held_as)


def setup_inputs(seed: int = 0) -> dict:
    streams_of = jax.random.split(jax.random.key(seed), 9)
    hidden = centred(streams_of[0], (TOKENS, D), 1.0, 6.0, ((0, 256),))
    w_proj = centred(streams_of[1], (D, GROUPS * PROJ_DEV), D ** -0.5, 0.0625, ((1, 16),))
    w_dt = centred(streams_of[2], (HEADS, D), D ** -0.5, 0.0625, ((0, 16),))
    dt_bias = draw_dt_bias(jax.random.fold_in(streams_of[8], 71), 0)
    a_log = jnp.clip(0.6 * jax.random.uniform(streams_of[4], (HEADS,), jnp.float32) ** shard_levels(streams_of[4], (HEADS,), ((0, 16),), -0.2, 0.2), 0.0, 0.6)
    d_skip = jnp.clip(0.5 + 1.0 * jax.random.uniform(streams_of[5], (HEADS,), jnp.float32) ** shard_levels(streams_of[5], (HEADS,), ((0, 16),), -0.2, 0.2), 0.5, 1.5)
    doc_lengths = draw_doc_lengths(jax.random.fold_in(streams_of[8], 71), 0)
    grad_out = draw_grad_out(jax.random.fold_in(streams_of[8], 71), 0)
    return {"hidden": hidden, "w_proj": w_proj, "w_dt": w_dt, "dt_bias": dt_bias, "a_log": a_log, "d_skip": d_skip, "doc_lengths": doc_lengths, "grad_out": grad_out}


PRECISE = lax.Precision.HIGHEST

def block_encode(rows):
    row_total = rows.shape[0]
    feat_width = rows.shape[1]
    values = rows.astype(jnp.float32).reshape(row_total, feat_width // MX_BLOCK, MX_BLOCK)
    largest = lax.optimization_barrier(jnp.max(jnp.abs(values), axis=2))
    scale_power = jnp.full(largest.shape, 2.0 ** (-48), jnp.float32)
    for exponent in range(-39, 40):
        scale_power = jnp.where(largest >= 2.0 ** exponent, 2.0 ** (exponent - 8), scale_power)
    scaled = values / scale_power[:, :, None]
    magnitude = jnp.abs(scaled)
    quantum = jnp.full(scaled.shape, 2.0 ** (-9), jnp.float32)
    for exponent in range(-5, 9):
        quantum = jnp.where(magnitude >= 2.0 ** exponent, 2.0 ** (exponent - 3), quantum)
    step_ratio = scaled / quantum
    floored = jnp.floor(step_ratio)
    remainder = step_ratio - floored
    parity = floored - 2.0 * jnp.floor(0.5 * floored)
    upward = (remainder > 0.5) | (remainder == 0.5) & (parity == 1.0)
    snapped = (floored + jnp.where(upward, 1.0, 0.0)) * quantum
    snapped = jnp.clip(snapped, -448.0, 448.0)
    return (snapped.reshape(row_total, feat_width).astype(jnp.bfloat16), scale_power.astype(jnp.bfloat16))

def dequantize(elements, scale_power):
    row_total = elements.shape[0]
    feat_width = elements.shape[1]
    blocks_view = elements.astype(jnp.float32).reshape(row_total, feat_width // MX_BLOCK, MX_BLOCK)
    restored = blocks_view * scale_power.astype(jnp.float32)[:, :, None]
    return restored.reshape(row_total, feat_width).astype(jnp.bfloat16)

def segment_index(positions, doc_lengths):
    lengths = doc_lengths.astype(jnp.int32)
    starts = (jnp.cumsum(lengths) - lengths).astype(jnp.int32)
    inside = (starts[None, :] <= positions[:, None]).astype(jnp.int32)
    return (lax.optimization_barrier(jnp.sum(inside, axis=1)) - 1).astype(jnp.int32)

def block_parts(x_heads, b_rows, c_rows, dt_rows, decay_rates, segments, previous):
    cumulative = jnp.cumsum(dt_rows * decay_rates[None], axis=0)
    positions = jnp.arange(segments.shape[0])
    allowed = (positions[:, None] >= positions[None, :]) & (segments[:, None] == segments[None, :])
    allowed_grid = allowed[:, :, None, None]
    log_gap = cumulative[:, None] - cumulative[None, :]
    decay_grid = jnp.where(allowed_grid, jnp.exp(jnp.where(allowed_grid, log_gap, 0.0)), 0.0)
    scores = jnp.einsum('tgn,sgn->tsg', c_rows, b_rows, precision=PRECISE)
    mixing = scores[:, :, :, None] * decay_grid * dt_rows[None]
    inner_out = jnp.einsum('tsge,sgep->tgep', mixing, x_heads, precision=PRECISE)
    continues = (segments == previous).astype(jnp.float32)
    carry_weight = jnp.exp(cumulative) * continues[:, None, None]
    in_last = (segments == segments[-1]).astype(jnp.float32)
    keep_weight = jnp.exp(cumulative[-1][None] - cumulative) * dt_rows * in_last[:, None, None]
    end_state = jnp.einsum('sge,sgep,sgn->gepn', keep_weight, x_heads, b_rows, precision=PRECISE)
    block_decay = jnp.exp(cumulative[-1]) * continues[-1]
    return (inner_out, carry_weight, block_decay, end_state)

def ssd_output(proj_values, dt_values, dt_bias, a_log, d_skip, segments, previous_segs):
    token_total = proj_values.shape[0]
    x_width = HEADS_DEV * HEAD_DIM
    lane_values = proj_values.reshape(token_total, GROUPS, x_width + 2 * STATE)
    x_heads = jax.nn.silu(lane_values[:, :, :x_width]).reshape(token_total, GROUPS, HEADS_DEV, HEAD_DIM)
    b_rows = jax.nn.silu(lane_values[:, :, x_width:x_width + STATE])
    c_rows = jax.nn.silu(lane_values[:, :, x_width + STATE:])
    dt_rows = jax.nn.softplus(dt_values + dt_bias[None]).reshape(token_total, GROUPS, HEADS_DEV)
    decay_rates = (-jnp.exp(a_log)).reshape(GROUPS, HEADS_DEV)
    skip_gain = d_skip.reshape(GROUPS, HEADS_DEV)
    blocks = token_total // BLOCK_LEN

    def advance(state_in, inputs):
        x_blk, b_blk, c_blk, dt_blk, seg_blk, prev_blk = inputs
        inner_out, carry_weight, block_decay, end_state = block_parts(x_blk, b_blk, c_blk, dt_blk, decay_rates, seg_blk, prev_blk)
        carried = jnp.einsum('tgn,gepn->tgep', c_blk, state_in, precision=PRECISE) * carry_weight[:, :, :, None]
        result = inner_out + carried + skip_gain[None, :, :, None] * x_blk
        state_out = block_decay[:, :, None, None] * state_in + end_state
        return (state_out, result)
    initial = jnp.zeros((GROUPS, HEADS_DEV, HEAD_DIM, STATE), jnp.float32)
    scanned = (x_heads.reshape(blocks, BLOCK_LEN, GROUPS, HEADS_DEV, HEAD_DIM), b_rows.reshape(blocks, BLOCK_LEN, GROUPS, STATE), c_rows.reshape(blocks, BLOCK_LEN, GROUPS, STATE), dt_rows.reshape(blocks, BLOCK_LEN, GROUPS, HEADS_DEV), segments.reshape(blocks, BLOCK_LEN), previous_segs)
    final_state, results = lax.scan(advance, initial, scanned)
    return results.reshape(token_total, GROUPS * x_width)

def reference(hidden, w_proj, w_dt, dt_bias, a_log, d_skip, doc_lengths, grad_out):
    elements, scale_power = block_encode(hidden)
    quantized = dequantize(elements, scale_power)
    projected = jnp.dot(quantized, w_proj, preferred_element_type=jnp.float32).astype(jnp.bfloat16)
    dt_raw = lax.dot_general(quantized, w_dt, (((1,), (1,)), ((), ())), preferred_element_type=jnp.float32)
    positions = jnp.arange(TOKENS, dtype=jnp.int32)
    segments = segment_index(positions, doc_lengths)
    previous_segs = segment_index((positions[::BLOCK_LEN] - 1).astype(jnp.int32), doc_lengths)

    def forward(proj_values, dt_values):
        return ssd_output(proj_values, dt_values, dt_bias, a_log, d_skip, segments, previous_segs)
    ssd_y, backward = jax.vjp(forward, projected.astype(jnp.float32), dt_raw)
    proj_grad, dt_grad = backward(grad_out.astype(jnp.float32))
    proj_grad = proj_grad.astype(jnp.bfloat16)
    dt_grad = dt_grad.astype(jnp.bfloat16)
    grad_hidden = lax.dot_general(proj_grad, w_proj, (((1,), (1,)), ((), ())), preferred_element_type=jnp.float32)
    grad_hidden = grad_hidden + jnp.dot(dt_grad, w_dt, preferred_element_type=jnp.float32)
    return (ssd_y.astype(jnp.bfloat16), grad_hidden.astype(jnp.bfloat16))
```

```python
import jax
import jax.numpy as jnp
from jax import lax
from jax.experimental import pallas as pl
from jax.experimental.pallas import tpu as pltpu
from jax.sharding import PartitionSpec as P

BF = jnp.bfloat16
F32 = jnp.float32
MESH = pl.DeviceIdType.MESH

PLANES = 8
SPANS = 16
ROWS = 16
SPAN = 256
FEAT = 8192
HEADS = 8
HDIM = 64
XW = HEADS * HDIM
STATE = 128
PROJ = XW + 2 * STATE
PIECES = 4
PIECE = FEAT // PIECES
HALF = PIECES // 2
PART = XW // SPANS
SLOT = {0: 0, 1: 1, 7: 2, 2: 3, 6: 4, 3: 5, 5: 6, 4: 7}
NEAR = 5 * 32

NN = (((1,), (0,)), ((), ()))
NT = (((1,), (1,)), ((), ()))
TN = (((0,), (0,)), ((), ()))


def mm(a, b, dims=NN):
    return lax.dot_general(a, b, dims, preferred_element_type=F32)


def cols(piece):
    return pl.ds(piece * PIECE, PIECE)


def quantize(rows):
    lane = lax.broadcasted_iota(jnp.int32, rows.shape, 1)
    largest = jnp.abs(rows)
    for step in (1, 2, 4, 8, 16):
        below = pltpu.roll(largest, step, 1)
        above = pltpu.roll(largest, 128 - step, 1)
        largest = jnp.maximum(largest, jnp.where((lane & step) != 0, below, above))
    power = jnp.exp2(jnp.floor(jnp.log2(jnp.maximum(largest, 2.0**-39)))).astype(BF).astype(F32)
    power = jnp.where(power > largest, power * 0.5, power)
    power = jnp.where(power * 2.0 <= largest, power * 2.0, power)
    scale = jnp.where(largest >= 2.0**-39, power * 2.0**-8, 2.0**-48)
    lifted = rows * 2.0**20
    normal = (rows + lifted) - lifted
    anchor = scale * (1.5 * 2.0**14)
    small = (rows + anchor) - anchor
    snapped = jnp.where(jnp.abs(rows) < scale * 2.0**-6, small, normal)
    bound = scale * 448.0
    return jnp.clip(snapped, -bound, bound)


def split3(values):
    first = values.astype(BF)
    rest = values - first.astype(F32)
    second = rest.astype(BF)
    third = (rest - second.astype(F32)).astype(BF)
    return first, second, third


def sums(values, chosen):
    first, second, third = split3(values)
    stacked = jnp.concatenate(
        [first.astype(F32), second.astype(F32), third.astype(F32), jnp.zeros_like(values)], axis=0
    ).astype(BF)
    out = mm(stacked, chosen)
    return out[0:8] + out[8:16] + out[16:24]


def column(scalars):
    row = lax.broadcasted_iota(jnp.int32, (HEADS, SPAN), 0)
    out = jnp.zeros((HEADS, SPAN), F32)
    for head in range(HEADS):
        out = jnp.where(row == head, scalars[head], out)
    return out


def head_rows(head):
    return pl.ds(head * HDIM, HDIM)


def kernel(
    hid, w_hbm, wdt_ref, bias_ref, alog_ref, skip_ref, docs, go,
    y_out, gh_out,
    w, wdt, xb, acc, dacc, bias_m, gyt, pn, dn_, ptx, dst, ut, gyw, kut, yt, dut, ds_,
    xs, xr, os_, or_, pg, dg, pga, dga, own, sbs, sbr, ru_s, ru_r, rd_s, rd_r,
    wsem, au_s, au_r, ad_s, ad_r, ab_s, ab_r, x1s, x1r, x2s, x2r,
    bu_s, bu_r, bd_s, bd_r, bb_s, bb_r,
):
    me = lax.axis_index("tensor")
    span = lax.axis_index("context")
    z = me // 2
    core = me % 2
    up = lax.rem(z + 1, PLANES) * 2 + core
    down = lax.rem(z + PLANES - 1, PLANES) * 2 + core
    twin = z * 2 + (1 - core)

    w_copy = pltpu.make_async_copy(w_hbm, w, wsem)
    w_copy.start()

    barrier = pltpu.get_barrier_semaphore()
    for near in (up, down, twin):
        pl.semaphore_signal(barrier, inc=1, device_id={"tensor": near}, device_id_type=MESH)

    def greet(step, carry):
        pl.semaphore_signal(
            barrier, inc=1, device_id={"context": lax.rem(span + step, SPANS)}, device_id_type=MESH
        )
        return carry

    lax.fori_loop(1, SPANS, greet, 0)

    def block(place, half, piece):
        return xb.at[pl.ds(SLOT[place % PLANES] * 32 + half * 16, ROWS), cols(piece)]

    def to_up(step, piece):
        return pltpu.make_async_remote_copy(
            src_ref=block(-step, 0, piece), dst_ref=block(-step - 1, 0, piece),
            send_sem=au_s.at[step, piece], recv_sem=au_r.at[step, piece],
            device_id={"tensor": up}, device_id_type=MESH,
        )

    def to_down(step, piece):
        return pltpu.make_async_remote_copy(
            src_ref=block(step, 0, piece), dst_ref=block(step + 1, 0, piece),
            send_sem=ad_s.at[step, piece], recv_sem=ad_r.at[step, piece],
            device_id={"tensor": down}, device_id_type=MESH,
        )

    def to_twin(place, piece):
        place = place % PLANES
        return pltpu.make_async_remote_copy(
            src_ref=block(place, 0, piece), dst_ref=block(place, 1, piece),
            send_sem=ab_s.at[place, piece], recv_sem=ab_r.at[place, piece],
            device_id={"tensor": twin}, device_id_type=MESH,
        )

    tiles = PIECE // 128
    for piece in range(PIECES):
        part = hid[:, piece * PIECE : (piece + 1) * PIECE].astype(F32)
        stacked = jnp.concatenate(
            [part[:, i * 128 : (i + 1) * 128] for i in range(tiles)], axis=0
        )
        snapped = quantize(stacked)
        flat = jnp.concatenate(
            [snapped[i * ROWS : (i + 1) * ROWS] for i in range(tiles)], axis=1
        )
        xb[0:ROWS, piece * PIECE : (piece + 1) * PIECE] = flat.astype(BF)
        if piece == 0:
            pl.semaphore_wait(barrier, SPANS - 1 + 3)
        to_up(0, piece).start()
        to_down(0, piece).start()
        to_twin(0, piece).start()

    wdt[0:16, :] = jnp.concatenate(
        [wdt_ref[...].astype(F32), jnp.zeros((8, FEAT), F32)], axis=0
    ).astype(BF)
    wdt[16:128, :] = jnp.zeros((112, FEAT), BF)
    first_token = span * SPAN

    def segment(positions):
        out = jnp.full(positions.shape, -1, jnp.int32)
        begin = jnp.int32(0)
        for doc in range(8):
            out = out + jnp.where(positions >= begin, 1, 0)
            begin = begin + docs[doc]
        return out

    row_pos = first_token + lax.broadcasted_iota(jnp.int32, (SPAN, SPAN), 0)
    col_pos = first_token + lax.broadcasted_iota(jnp.int32, (SPAN, SPAN), 1)
    bias_m[...] = jnp.where(
        (row_pos >= col_pos) & (segment(row_pos) == segment(col_pos)), 0.0, -1e30
    )
    token = first_token + lax.broadcasted_iota(jnp.int32, (HEADS, SPAN), 1)
    seg = segment(token)
    seg_before = segment(jnp.zeros((HEADS, SPAN), jnp.int32) + (first_token - 1))
    seg_last = segment(jnp.zeros((HEADS, SPAN), jnp.int32) + (first_token + SPAN - 1))
    continues = jnp.where(seg == seg_before, 1.0, 0.0)
    in_last = jnp.where(seg == seg_last, 1.0, 0.0)
    through = jnp.where(seg_last == seg_before, 1.0, 0.0)
    gyt[...] = jnp.transpose(go[...].astype(F32)).astype(BF)

    def project(first, last):
        for piece in range(PIECES):
            rows = xb[first:last, piece * PIECE : (piece + 1) * PIECE]
            part = mm(rows, w[piece * PIECE : (piece + 1) * PIECE, :])
            dpart = mm(rows, wdt[:, piece * PIECE : (piece + 1) * PIECE], NT)
            if piece == 0:
                acc[first:last, :] = part
                dacc[first:last, :] = dpart
            else:
                acc[first:last, :] += part
                dacc[first:last, :] += dpart

    for step in range(3):
        for piece in range(PIECES):
            to_up(step, piece).wait_recv()
            if step < 2 or piece < HALF:
                to_up(step + 1, piece).start()
            to_twin(-step - 1, piece).start()
            to_down(step, piece).wait_recv()
            if step < 2 or piece >= HALF:
                to_down(step + 1, piece).start()
            to_twin(step + 1, piece).start()
        if step == 1:
            w_copy.wait()
            for place in (0, 1, 7, 2, 6):
                for piece in range(PIECES):
                    to_twin(place, piece).wait_recv()
            project(0, NEAR)
    for piece in range(HALF):
        to_up(3, piece).wait_recv()
        to_twin(4, piece).start()
        to_down(3, piece + HALF).wait_recv()
        to_twin(4, piece + HALF).start()
    for place in (3, 5, 4):
        for piece in range(PIECES):
            to_twin(place, piece).wait_recv()
    project(NEAR, SPAN)
    for piece in range(PIECES):
        for step in range(4):
            if step < 3 or piece < HALF:
                to_up(step, piece).wait_send()
            if step < 3 or piece >= HALF:
                to_down(step, piece).wait_send()
        for place in range(PLANES):
            to_twin(place, piece).wait_send()

    def home(place, half):
        owner = lax.rem(z + place, PLANES) * 2 + (core if half == 0 else 1 - core)
        return pl.ds(pl.multiple_of(owner * ROWS, ROWS), ROWS)

    for place in range(PLANES):
        for half in range(2):
            at = SLOT[place] * 32 + half * 16
            pn[home(place, half), :] = acc[at : at + 16, :].astype(BF).astype(F32)
            dn_[home(place, half), :] = dacc[at : at + 16, :]

    natural = pn[:, XW:PROJ]
    natural = (natural / (1.0 + jnp.exp(-natural))).astype(BF)
    b_nat = natural[:, 0:STATE]
    c_nat = natural[:, STATE : 2 * STATE]
    pt = jnp.transpose(pn[...])
    gate = 1.0 / (1.0 + jnp.exp(-pt))
    ptx[...] = pt * gate
    dst[...] = gate * (1.0 + pt * (1.0 - gate))
    b_t = ptx[XW : XW + STATE, :].astype(BF)
    c_t = ptx[XW + STATE : PROJ, :].astype(BF)

    dt_arg = jnp.transpose(dn_[...])[0:HEADS, :] + column(bias_ref)
    dt = jnp.maximum(dt_arg, 0.0) + jnp.log1p(jnp.exp(-jnp.abs(dt_arg)))
    dt_gate = 1.0 / (1.0 + jnp.exp(-dt_arg))
    rate = -jnp.exp(column(alog_ref))
    skip = column(skip_ref)
    line = lax.broadcasted_iota(jnp.int32, (SPAN, SPAN), 0)
    lane = lax.broadcasted_iota(jnp.int32, (SPAN, SPAN), 1)
    upto = jnp.where(line <= lane, 1.0, 0.0).astype(BF)
    since = jnp.where(line >= lane, 1.0, 0.0).astype(BF)
    before = jnp.where(line < lane, 1.0, 0.0).astype(BF)
    cum = sums(dt * rate, upto)
    cum_col = jnp.transpose(jnp.concatenate([cum, jnp.zeros((120, SPAN), F32)], axis=0))
    cum_last = jnp.broadcast_to(cum[:, SPAN - 1 : SPAN], (HEADS, SPAN))
    carry_w = jnp.exp(cum) * continues
    keep_w = jnp.exp(cum_last - cum) * in_last
    total = jnp.exp(cum_last) * through

    for head in range(HEADS):
        at = head_rows(head)
        u = ptx[at, :] * dt[head : head + 1, :]
        ut[at, :] = u.astype(BF)
        kut[at, :] = (u * keep_w[head : head + 1, :]).astype(BF)
        gyw[at, :] = (gyt[at, :].astype(F32) * carry_w[head : head + 1, :]).astype(BF)
    end_state = mm(kut[...], b_nat).astype(BF)
    from_out = mm(gyw[...], c_nat).astype(BF)
    note_row = lax.broadcasted_iota(jnp.int32, (16, 128), 0)
    for part in range(SPANS):
        at = slice(part * PART, (part + 1) * PART)
        xs[part, 0:PART, :] = end_state[at]
        xs[part, PART : 2 * PART, :] = from_out[at]
        head = part * PART // HDIM
        decay = total[head : head + 1, 0:128]
        high = decay.astype(BF).astype(F32)
        xs[part, 2 * PART : 2 * PART + 16, :] = jnp.where(
            note_row == 0, high, jnp.where(note_row == 1, decay - high, 0.0)
        ).astype(BF)

    def other(step):
        return lax.rem(span + step, SPANS)

    def out1(step):
        return pltpu.make_async_remote_copy(
            src_ref=xs.at[other(step)], dst_ref=xr.at[span],
            send_sem=x1s.at[other(step)], recv_sem=x1r.at[span],
            device_id={"context": other(step)}, device_id_type=MESH,
        )

    def in1(step):
        return pltpu.make_async_remote_copy(
            src_ref=xs.at[other(step)], dst_ref=xr.at[other(step)],
            send_sem=x1s.at[other(step)], recv_sem=x1r.at[other(step)],
            device_id={"context": other(step)}, device_id_type=MESH,
        )

    def out2(step):
        return pltpu.make_async_remote_copy(
            src_ref=os_.at[other(step)], dst_ref=or_.at[span],
            send_sem=x2s.at[other(step)], recv_sem=x2r.at[span],
            device_id={"context": other(step)}, device_id_type=MESH,
        )

    def in2(step):
        return pltpu.make_async_remote_copy(
            src_ref=os_.at[other(step)], dst_ref=or_.at[other(step)],
            send_sem=x2s.at[other(step)], recv_sem=x2r.at[other(step)],
            device_id={"context": other(step)}, device_id_type=MESH,
        )

    def every(action):
        def one(step, carry):
            action(step)
            return carry

        lax.fori_loop(1, SPANS, one, 0)

    every(lambda step: out1(step).start())
    xr[span] = xs[span]

    scores = mm(c_nat, b_t)
    low = jnp.where(lax.broadcasted_iota(jnp.int32, (1, 128), 1) < HDIM, 1.0, 0.0).astype(BF)
    high_half = jnp.where(lax.broadcasted_iota(jnp.int32, (1, 128), 1) < HDIM, 0.0, 1.0).astype(BF)

    def inner(head):
        at = head_rows(head)
        pair = head // 2 * 128
        gap = cum_col[:, head : head + 1] - cum[head : head + 1, :] + bias_m[...]
        decay = jnp.exp(gap)
        mixing = (scores * decay).astype(BF)
        yt[at, :] = mm(ut[at, :], mixing, NT)
        dut[at, :] = mm(gyt[at, :], mixing)
        picked = go[:, pair : pair + 128] * (low if head % 2 == 0 else high_half)
        products = mm(picked, ut[pair : pair + 128, :])
        if head == 0:
            ds_[...] = products * decay
        else:
            ds_[...] += products * decay

    for head in range(HEADS // 2):
        inner(head)

    every(lambda step: in1(step).wait_recv())
    running = jnp.zeros((PART, STATE), F32)
    for source in range(SPANS):
        os_[source, 0:PART, :] = running.astype(BF)
        note = xr[source, 2 * PART : 2 * PART + 16, :].astype(F32)
        decay = note[0:1] + note[1:2]
        running = decay * running + xr[source, 0:PART, :].astype(F32)
    running = jnp.zeros((PART, STATE), F32)
    for source in reversed(range(SPANS)):
        os_[source, PART : 2 * PART, :] = running.astype(BF)
        note = xr[source, 2 * PART : 2 * PART + 16, :].astype(F32)
        decay = note[0:1] + note[1:2]
        running = decay * running + xr[source, PART : 2 * PART, :].astype(F32)
    every(lambda step: out2(step).start())
    or_[span] = os_[span]

    for head in range(HEADS // 2, HEADS):
        inner(head)
    ds = ds_[...].astype(BF)
    dc_t = mm(b_t, ds, NT)
    db_t = mm(c_t, ds)

    every(lambda step: in2(step).wait_recv())
    state_in = or_[:, 0:PART, :].reshape(XW, STATE)
    state_grad = or_[:, PART : 2 * PART, :].reshape(XW, STATE)
    carried = mm(state_in, c_t)
    reach = mm(state_grad, b_t)
    dc_t = dc_t + mm(state_in, gyw[...], TN)
    db_t = db_t + mm(state_grad, kut[...], TN)

    from_rows, from_u, from_keep, direct, ends = [], [], [], [], []
    for head in range(HEADS):
        at = head_rows(head)
        rows = slice(head * HDIM, (head + 1) * HDIM)
        x = ptx[at, :]
        gy = gyt[at, :].astype(F32)
        u = ut[at, :].astype(F32)
        y = yt[at, :] + carried[rows] * carry_w[head : head + 1, :]
        late = reach[rows] * keep_w[head : head + 1, :]
        du_here = dut[at, :]
        du = du_here + late
        from_rows.append(jnp.sum(gy * y, axis=0, keepdims=True))
        from_u.append(jnp.sum(u * du_here, axis=0, keepdims=True))
        from_keep.append(jnp.sum(u * late, axis=0, keepdims=True))
        direct.append(jnp.sum(x * du, axis=0, keepdims=True))
        ends.append(
            jnp.sum(state_in[rows].astype(F32) * state_grad[rows].astype(F32), axis=0, keepdims=True)
        )
        dx = du * dt[head : head + 1, :] + gy * skip[head : head + 1, :]
        pg[at, :] = dx * dst[at, :]
        yt[at, :] = y + x * skip[head : head + 1, :]
    pg[XW : XW + STATE, :] = db_t * dst[XW : XW + STATE, :]
    pg[XW + STATE : PROJ, :] = dc_t * dst[XW + STATE : PROJ, :]
    gap_grad = jnp.concatenate(from_rows, axis=0) - jnp.concatenate(from_u, axis=0)
    end_grad = jnp.sum(jnp.concatenate(ends, axis=0), axis=1, keepdims=True)
    log_grad = (
        sums(gap_grad, since)
        + sums(jnp.concatenate(from_keep, axis=0), before)
        + total * end_grad
    )
    dt_grad = (jnp.concatenate(direct, axis=0) + rate * log_grad) * dt_gate

    pn[...] = jnp.transpose(pg[...])
    dn_[...] = jnp.transpose(jnp.concatenate([dt_grad, jnp.zeros((120, SPAN), F32)], axis=0))
    for place in range(PLANES):
        for half in range(2):
            at = half * 128 + SLOT[place] * 16
            pga[at : at + 16, :] = pn[home(place, half), :].astype(BF)
            dga[at : at + 16, :] = dn_[home(place, half), :].astype(BF)

    def multiply(piece):
        width = 512

        def one(step, carry):
            at = pl.multiple_of(piece * PIECE + step * width, width)
            term = mm(pga[...], w[pl.ds(at, width), :], NT)
            term = term + mm(dga[...], wdt[:, pl.ds(at, width)])
            own[:, pl.ds(at, width)] = term[0:128]
            sbs[:, pl.ds(at, width)] = term[128:256].astype(BF)
            return carry

        lax.fori_loop(0, PIECE // width, one, 0)

    def swap(piece):
        return pltpu.make_async_remote_copy(
            src_ref=sbs.at[:, cols(piece)], dst_ref=sbr.at[:, cols(piece)],
            send_sem=bb_s.at[piece], recv_sem=bb_r.at[piece],
            device_id={"tensor": twin}, device_id_type=MESH,
        )

    def pass_up(step, piece):
        return pltpu.make_async_remote_copy(
            src_ref=ru_s.at[step, :, cols(piece)], dst_ref=ru_r.at[step, :, cols(piece)],
            send_sem=bu_s.at[step, piece], recv_sem=bu_r.at[step, piece],
            device_id={"tensor": up}, device_id_type=MESH,
        )

    def pass_down(step, piece):
        return pltpu.make_async_remote_copy(
            src_ref=rd_s.at[step, :, cols(piece)], dst_ref=rd_r.at[step, :, cols(piece)],
            send_sem=bd_s.at[step, piece], recv_sem=bd_r.at[step, piece],
            device_id={"tensor": down}, device_id_type=MESH,
        )

    def pair_sum(place, piece):
        at = slice(SLOT[place % PLANES] * 16, SLOT[place % PLANES] * 16 + 16)
        return own[at, cols(piece)] + sbr[at, cols(piece)].astype(F32)

    def go_up(step, piece):
        value = pair_sum(4 - step, piece)
        if step > 1 or (step == 1 and piece < HALF):
            pass_up(step - 1, piece).wait_recv()
            value = value + ru_r[step - 1, :, cols(piece)].astype(F32)
        ru_s[step, :, cols(piece)] = value.astype(BF)
        pass_up(step, piece).start()

    def go_down(step, piece):
        value = pair_sum(4 + step, piece)
        if step > 1 or (step == 1 and piece >= HALF):
            pass_down(step - 1, piece).wait_recv()
            value = value + rd_r[step - 1, :, cols(piece)].astype(F32)
        rd_s[step, :, cols(piece)] = value.astype(BF)
        pass_down(step, piece).start()

    order = (0, 2, 1, 3)
    for at, piece in enumerate(order):
        multiply(piece)
        swap(piece).start()
        if at > 0:
            ready = order[at - 1]
            swap(ready).wait_recv()
            (go_up if ready < HALF else go_down)(0, ready)
    ready = order[-1]
    swap(ready).wait_recv()
    (go_up if ready < HALF else go_down)(0, ready)
    for step in range(1, 4):
        for up_piece, down_piece in ((2, 0), (3, 1), (0, 2), (1, 3)):
            go_up(step, up_piece)
            go_down(step, down_piece)
        if step == 1:
            y_out[...] = jnp.transpose(yt[...]).astype(BF)
    for piece in (2, 0, 3, 1):
        pass_up(3, piece).wait_recv()
        pass_down(3, piece).wait_recv()
        value = pair_sum(0, piece)
        value = value + ru_r[3, :, cols(piece)].astype(F32) + rd_r[3, :, cols(piece)].astype(F32)
        gh_out[:, cols(piece)] = value.astype(BF)
    for piece in range(PIECES):
        swap(piece).wait_send()
        for step in range(4):
            if step > 0 or piece < HALF:
                pass_up(step, piece).wait_send()
            if step > 0 or piece >= HALF:
                pass_down(step, piece).wait_send()
    every(lambda step: out1(step).wait_send())
    every(lambda step: out2(step).wait_send())


def per_device(hidden, w_proj, w_dt, dt_bias, a_log, d_skip, doc_lengths, grad_out):
    vmem = pl.BlockSpec(memory_space=pltpu.VMEM)
    smem = pl.BlockSpec(memory_space=pltpu.SMEM)
    dma = pltpu.SemaphoreType.DMA
    return pl.pallas_call(
        kernel,
        out_shape=(
            jax.ShapeDtypeStruct((SPAN, XW), BF),
            jax.ShapeDtypeStruct((ROWS, FEAT), BF),
        ),
        in_specs=[vmem, pl.BlockSpec(memory_space=pl.ANY), vmem, smem, smem, smem, smem, vmem],
        out_specs=(vmem, vmem),
        scratch_shapes=[
            pltpu.VMEM((FEAT, PROJ), BF),
            pltpu.VMEM((128, FEAT), BF),
            pltpu.VMEM((SPAN, FEAT), BF),
            pltpu.VMEM((SPAN, PROJ), F32),
            pltpu.VMEM((SPAN, 128), F32),
            pltpu.VMEM((SPAN, SPAN), F32),
            pltpu.VMEM((XW, SPAN), BF),
            pltpu.VMEM((SPAN, PROJ), F32),
            pltpu.VMEM((SPAN, 128), F32),
            pltpu.VMEM((PROJ, SPAN), F32),
            pltpu.VMEM((PROJ, SPAN), F32),
            pltpu.VMEM((XW, SPAN), BF),
            pltpu.VMEM((XW, SPAN), BF),
            pltpu.VMEM((XW, SPAN), BF),
            pltpu.VMEM((XW, SPAN), F32),
            pltpu.VMEM((XW, SPAN), F32),
            pltpu.VMEM((SPAN, SPAN), F32),
            pltpu.VMEM((SPANS, 2 * PART + 16, STATE), BF),
            pltpu.VMEM((SPANS, 2 * PART + 16, STATE), BF),
            pltpu.VMEM((SPANS, 2 * PART, STATE), BF),
            pltpu.VMEM((SPANS, 2 * PART, STATE), BF),
            pltpu.VMEM((PROJ, SPAN), F32),
            pltpu.VMEM((128, SPAN), F32),
            pltpu.VMEM((SPAN, PROJ), BF),
            pltpu.VMEM((SPAN, 128), BF),
            pltpu.VMEM((128, FEAT), F32),
            pltpu.VMEM((128, FEAT), BF),
            pltpu.VMEM((128, FEAT), BF),
            pltpu.VMEM((4, ROWS, FEAT), BF),
            pltpu.VMEM((4, ROWS, FEAT), BF),
            pltpu.VMEM((4, ROWS, FEAT), BF),
            pltpu.VMEM((4, ROWS, FEAT), BF),
            dma,
            dma((4, PIECES)), dma((4, PIECES)), dma((4, PIECES)), dma((4, PIECES)),
            dma((PLANES, PIECES)), dma((PLANES, PIECES)),
            dma((SPANS,)), dma((SPANS,)), dma((SPANS,)), dma((SPANS,)),
            dma((4, PIECES)), dma((4, PIECES)), dma((4, PIECES)), dma((4, PIECES)),
            dma((PIECES,)), dma((PIECES,)),
        ],
        compiler_params=pltpu.CompilerParams(
            collective_id=0, has_side_effects=True, vmem_limit_bytes=60 * 1024 * 1024
        ),
        name="layer",
    )(hidden, w_proj, w_dt, dt_bias, a_log, d_skip, doc_lengths, grad_out)


def solution(mesh):
    placed = (
        P(("context", "tensor"), None),
        P(None, "tensor"),
        P("tensor", None),
        P("tensor"),
        P("tensor"),
        P("tensor"),
        P(),
        P("context", "tensor"),
    )
    return jax.shard_map(
        per_device,
        mesh=mesh,
        in_specs=placed,
        out_specs=(P("context", "tensor"), P(("context", "tensor"), None)),
        check_vma=False,
    )
```

```python
import jax
import jax.numpy as jnp
from jax import lax
from jax.experimental import pallas as pl
from jax.experimental.pallas import tpu as pltpu
from jax.sharding import PartitionSpec as P

BF = jnp.bfloat16
F32 = jnp.float32
MESH = pl.DeviceIdType.MESH

PLANES = 8
SPANS = 16
ROWS = 16
SPAN = 256
FEAT = 8192
HEADS = 8
HDIM = 64
XW = HEADS * HDIM
STATE = 128
PROJ = XW + 2 * STATE
WIDE = PROJ + 128
QUARTER = FEAT // 4
PART = XW // SPANS
SLOT = {0: 0, 1: 1, 7: 2, 2: 3, 6: 4, 3: 5, 5: 6, 4: 7}
NEAR = 5 * 32

NN = (((1,), (0,)), ((), ()))
NT = (((1,), (1,)), ((), ()))
TN = (((0,), (0,)), ((), ()))


def mm(a, b, dims=NN):
    return lax.dot_general(a, b, dims, preferred_element_type=F32)


def cols(quarter, count=1):
    return pl.ds(quarter * QUARTER, count * QUARTER)


def quantize(rows):
    lane = lax.broadcasted_iota(jnp.int32, rows.shape, 1)
    largest = jnp.abs(rows)
    for step in (1, 2, 4, 8, 16):
        below = pltpu.roll(largest, step, 1)
        above = pltpu.roll(largest, 128 - step, 1)
        largest = jnp.maximum(largest, jnp.where((lane & step) != 0, below, above))
    power = jnp.exp2(jnp.floor(jnp.log2(jnp.maximum(largest, 2.0**-39)))).astype(BF).astype(F32)
    power = jnp.where(power > largest, power * 0.5, power)
    power = jnp.where(power * 2.0 <= largest, power * 2.0, power)
    scale = jnp.where(largest >= 2.0**-39, power * 2.0**-8, 2.0**-48)
    lifted = rows * 2.0**20
    normal = (rows + lifted) - lifted
    anchor = scale * (1.5 * 2.0**14)
    small = (rows + anchor) - anchor
    snapped = jnp.where(jnp.abs(rows) < scale * 2.0**-6, small, normal)
    bound = scale * 448.0
    return jnp.clip(snapped, -bound, bound)


def split3(values):
    first = values.astype(BF)
    rest = values - first.astype(F32)
    second = rest.astype(BF)
    third = (rest - second.astype(F32)).astype(BF)
    return first, second, third


def sums(values, chosen):
    first, second, third = split3(values)
    stacked = jnp.concatenate(
        [first.astype(F32), second.astype(F32), third.astype(F32), jnp.zeros_like(values)], axis=0
    ).astype(BF)
    out = mm(stacked, chosen)
    return out[0:8] + out[8:16] + out[16:24]


def column(scalars):
    row = lax.broadcasted_iota(jnp.int32, (HEADS, SPAN), 0)
    out = jnp.zeros((HEADS, SPAN), F32)
    for head in range(HEADS):
        out = jnp.where(row == head, scalars[head], out)
    return out


def head_rows(head):
    return pl.ds(head * HDIM, HDIM)


def kernel(
    hid, w_hbm, wdt_ref, bias_ref, alog_ref, skip_ref, docs, go,
    y_out, gh_out,
    w, xb, acc, bias_m, gyt, pn, ptx, dst, ut, gyw, kut, yt, dut, ds_,
    xs, xr, os_, or_, pg, pga, own, sbs, sbr, ru_s, ru_r, rd_s, rd_r,
    wsem, au_s, au_r, ad_s, ad_r, ab_s, ab_r, x1s, x1r, x2s, x2r,
    bu_s, bu_r, bd_s, bd_r, bb_s, bb_r, bf_s, bf_r,
):
    me = lax.axis_index("tensor")
    span = lax.axis_index("context")
    z = me // 2
    core = me % 2
    up = lax.rem(z + 1, PLANES) * 2 + core
    down = lax.rem(z + PLANES - 1, PLANES) * 2 + core
    twin = z * 2 + (1 - core)

    w_copy = pltpu.make_async_copy(w_hbm, w.at[:, 0:PROJ], wsem)
    w_copy.start()

    barrier = pltpu.get_barrier_semaphore()
    for near in (up, down, twin):
        pl.semaphore_signal(barrier, inc=1, device_id={"tensor": near}, device_id_type=MESH)

    def greet(step, carry):
        pl.semaphore_signal(
            barrier, inc=1, device_id={"context": lax.rem(span + step, SPANS)}, device_id_type=MESH
        )
        return carry

    lax.fori_loop(1, SPANS, greet, 0)

    def block(place, half, quarter, count):
        return xb.at[pl.ds(SLOT[place % PLANES] * 32 + half * 16, ROWS), cols(quarter, count)]

    def to_up(step, quarter, count):
        return pltpu.make_async_remote_copy(
            src_ref=block(-step, 0, quarter, count), dst_ref=block(-step - 1, 0, quarter, count),
            send_sem=au_s.at[step, quarter], recv_sem=au_r.at[step, quarter],
            device_id={"tensor": up}, device_id_type=MESH,
        )

    def to_down(step, quarter, count):
        return pltpu.make_async_remote_copy(
            src_ref=block(step, 0, quarter, count), dst_ref=block(step + 1, 0, quarter, count),
            send_sem=ad_s.at[step, quarter], recv_sem=ad_r.at[step, quarter],
            device_id={"tensor": down}, device_id_type=MESH,
        )

    def to_twin(place, quarter, count):
        place = place % PLANES
        return pltpu.make_async_remote_copy(
            src_ref=block(place, 0, quarter, count), dst_ref=block(place, 1, quarter, count),
            send_sem=ab_s.at[place, quarter], recv_sem=ab_r.at[place, quarter],
            device_id={"tensor": twin}, device_id_type=MESH,
        )

    quarters = ((0, 1), (1, 1), (2, 1), (3, 1))
    halves = ((0, 2), (2, 2))
    up_units = (quarters, halves, halves, quarters[:2])
    down_units = (quarters[2:] + quarters[:2], halves[::-1], halves[::-1], quarters[2:])
    twin_units = {0: ((0, 4),), 4: quarters}

    tiles = QUARTER // 128

    def encode(quarter):
        part = hid[:, quarter * QUARTER : (quarter + 1) * QUARTER].astype(F32)
        stacked = jnp.concatenate(
            [part[:, i * 128 : (i + 1) * 128] for i in range(tiles)], axis=0
        )
        snapped = quantize(stacked)
        flat = jnp.concatenate(
            [snapped[i * ROWS : (i + 1) * ROWS] for i in range(tiles)], axis=1
        )
        xb[0:ROWS, quarter * QUARTER : (quarter + 1) * QUARTER] = flat.astype(BF)

    encode(0)
    pl.semaphore_wait(barrier, SPANS - 1 + 3)
    to_up(0, 0, 1).start()
    encode(2)
    to_down(0, 2, 1).start()
    encode(1)
    to_up(0, 1, 1).start()
    encode(3)
    to_down(0, 3, 1).start()
    to_up(0, 2, 1).start()
    to_down(0, 0, 1).start()
    to_up(0, 3, 1).start()
    to_down(0, 1, 1).start()
    to_twin(0, 0, 4).start()

    first_token = span * SPAN

    def segment(positions):
        out = jnp.full(positions.shape, -1, jnp.int32)
        begin = jnp.int32(0)
        for doc in range(8):
            out = out + jnp.where(positions >= begin, 1, 0)
            begin = begin + docs[doc]
        return out

    row_pos = first_token + lax.broadcasted_iota(jnp.int32, (SPAN, SPAN), 0)
    col_pos = first_token + lax.broadcasted_iota(jnp.int32, (SPAN, SPAN), 1)
    bias_m[...] = jnp.where(
        (row_pos >= col_pos) & (segment(row_pos) == segment(col_pos)), 0.0, -1e30
    )
    token = first_token + lax.broadcasted_iota(jnp.int32, (HEADS, SPAN), 1)
    seg = segment(token)
    seg_before = segment(jnp.zeros((HEADS, SPAN), jnp.int32) + (first_token - 1))
    seg_last = segment(jnp.zeros((HEADS, SPAN), jnp.int32) + (first_token + SPAN - 1))
    continues = jnp.where(seg == seg_before, 1.0, 0.0)
    in_last = jnp.where(seg == seg_last, 1.0, 0.0)
    through = jnp.where(seg_last == seg_before, 1.0, 0.0)
    gyt[...] = jnp.transpose(go[...].astype(F32)).astype(BF)

    for quarter in range(4):
        steps_w = wdt_ref[:, quarter * QUARTER : (quarter + 1) * QUARTER].astype(F32)
        padded = jnp.concatenate([steps_w, jnp.zeros((120, QUARTER), F32)], axis=0)
        w[cols(quarter), PROJ:WIDE] = jnp.transpose(padded).astype(BF)

    def project(first, last, quarter, begin):
        at = slice(quarter * QUARTER, (quarter + 1) * QUARTER)
        part = mm(xb[first:last, at], w[at, :])
        if begin:
            acc[first:last, :] = part
        else:
            acc[first:last, :] += part

    def arrived_twin(place):
        for unit in twin_units.get(place, halves):
            to_twin(place, *unit).wait_recv()

    for step in range(3):
        for turn in range(2):
            unit = halves[turn]
            for got in quarters[2 * turn : 2 * turn + 2] if step == 0 else (unit,):
                to_up(step, *got).wait_recv()
            if step < 2:
                to_up(step + 1, *unit).start()
            elif turn == 0:
                for part in up_units[3]:
                    to_up(3, *part).start()
            to_twin(-step - 1, *unit).start()
            unit = halves[1 - turn]
            for got in quarters[2 - 2 * turn : 4 - 2 * turn] if step == 0 else (unit,):
                to_down(step, *got).wait_recv()
            if step < 2:
                to_down(step + 1, *unit).start()
            elif turn == 0:
                for part in down_units[3]:
                    to_down(3, *part).start()
            to_twin(step + 1, *unit).start()
        if step == 1:
            w_copy.wait()
            for place in (0, 1, 7, 2, 6):
                arrived_twin(place)
            for quarter in range(4):
                project(0, NEAR, quarter, quarter == 0)
    for at in range(2):
        to_up(3, *up_units[3][at]).wait_recv()
        to_twin(4, *up_units[3][at]).start()
        to_down(3, *down_units[3][at]).wait_recv()
        to_twin(4, *down_units[3][at]).start()
    arrived_twin(3)
    arrived_twin(5)
    for quarter in (0, 2, 1, 3):
        to_twin(4, quarter, 1).wait_recv()
        project(NEAR, SPAN, quarter, quarter == 0)

    def home(place, half):
        owner = lax.rem(z + place, PLANES) * 2 + (core if half == 0 else 1 - core)
        return pl.ds(pl.multiple_of(owner * ROWS, ROWS), ROWS)

    for place in range(PLANES):
        for half in range(2):
            at = SLOT[place] * 32 + half * 16
            pn[home(place, half), 0:PROJ] = acc[at : at + 16, 0:PROJ].astype(BF).astype(F32)
            pn[home(place, half), PROJ:WIDE] = acc[at : at + 16, PROJ:WIDE]

    natural = pn[:, XW:PROJ]
    natural = (natural / (1.0 + jnp.exp(-natural))).astype(BF)
    b_nat = natural[:, 0:STATE]
    c_nat = natural[:, STATE : 2 * STATE]
    all_t = jnp.transpose(pn[...])
    pt = all_t[0:PROJ]
    gate = 1.0 / (1.0 + jnp.exp(-pt))
    ptx[...] = pt * gate
    dst[...] = gate * (1.0 + pt * (1.0 - gate))
    b_t = ptx[XW : XW + STATE, :].astype(BF)
    c_t = ptx[XW + STATE : PROJ, :].astype(BF)

    dt_arg = all_t[PROJ : PROJ + HEADS] + column(bias_ref)
    dt = jnp.maximum(dt_arg, 0.0) + jnp.log1p(jnp.exp(-jnp.abs(dt_arg)))
    dt_gate = 1.0 / (1.0 + jnp.exp(-dt_arg))
    rate = -jnp.exp(column(alog_ref))
    skip = column(skip_ref)
    line = lax.broadcasted_iota(jnp.int32, (SPAN, SPAN), 0)
    lane = lax.broadcasted_iota(jnp.int32, (SPAN, SPAN), 1)
    upto = jnp.where(line <= lane, 1.0, 0.0).astype(BF)
    since = jnp.where(line >= lane, 1.0, 0.0).astype(BF)
    before = jnp.where(line < lane, 1.0, 0.0).astype(BF)
    cum = sums(dt * rate, upto)
    cum_col = jnp.transpose(jnp.concatenate([cum, jnp.zeros((120, SPAN), F32)], axis=0))
    cum_last = jnp.broadcast_to(cum[:, SPAN - 1 : SPAN], (HEADS, SPAN))
    carry_w = jnp.exp(cum) * continues
    keep_w = jnp.exp(cum_last - cum) * in_last
    total = jnp.exp(cum_last) * through

    for head in range(HEADS):
        at = head_rows(head)
        u = ptx[at, :] * dt[head : head + 1, :]
        ut[at, :] = u.astype(BF)
        kut[at, :] = (u * keep_w[head : head + 1, :]).astype(BF)
        gyw[at, :] = (gyt[at, :].astype(F32) * carry_w[head : head + 1, :]).astype(BF)
    end_state = mm(kut[...], b_nat).astype(BF)
    from_out = mm(gyw[...], c_nat).astype(BF)
    note_row = lax.broadcasted_iota(jnp.int32, (16, 128), 0)
    for part in range(SPANS):
        at = slice(part * PART, (part + 1) * PART)
        xs[part, 0:PART, :] = end_state[at]
        xs[part, PART : 2 * PART, :] = from_out[at]
        head = part * PART // HDIM
        decay = total[head : head + 1, 0:128]
        high = decay.astype(BF).astype(F32)
        xs[part, 2 * PART : 2 * PART + 16, :] = jnp.where(
            note_row == 0, high, jnp.where(note_row == 1, decay - high, 0.0)
        ).astype(BF)

    def other(step):
        return lax.rem(span + step, SPANS)

    def out1(step):
        return pltpu.make_async_remote_copy(
            src_ref=xs.at[other(step)], dst_ref=xr.at[span],
            send_sem=x1s.at[other(step)], recv_sem=x1r.at[span],
            device_id={"context": other(step)}, device_id_type=MESH,
        )

    def in1(step):
        return pltpu.make_async_remote_copy(
            src_ref=xs.at[other(step)], dst_ref=xr.at[other(step)],
            send_sem=x1s.at[other(step)], recv_sem=x1r.at[other(step)],
            device_id={"context": other(step)}, device_id_type=MESH,
        )

    def out2(step):
        return pltpu.make_async_remote_copy(
            src_ref=os_.at[other(step)], dst_ref=or_.at[span],
            send_sem=x2s.at[other(step)], recv_sem=x2r.at[span],
            device_id={"context": other(step)}, device_id_type=MESH,
        )

    def in2(step):
        return pltpu.make_async_remote_copy(
            src_ref=os_.at[other(step)], dst_ref=or_.at[other(step)],
            send_sem=x2s.at[other(step)], recv_sem=x2r.at[other(step)],
            device_id={"context": other(step)}, device_id_type=MESH,
        )

    def every(action):
        def one(step, carry):
            action(step)
            return carry

        lax.fori_loop(1, SPANS, one, 0)

    every(lambda step: out1(step).start())
    xr[span] = xs[span]

    scores = mm(c_nat, b_t)
    low = jnp.where(lax.broadcasted_iota(jnp.int32, (1, 128), 1) < HDIM, 1.0, 0.0).astype(BF)
    high_half = jnp.where(lax.broadcasted_iota(jnp.int32, (1, 128), 1) < HDIM, 0.0, 1.0).astype(BF)

    def inner(head):
        at = head_rows(head)
        pair = head // 2 * 128
        gap = cum_col[:, head : head + 1] - cum[head : head + 1, :] + bias_m[...]
        decay = jnp.exp(gap)
        mixing = (scores * decay).astype(BF)
        yt[at, :] = mm(ut[at, :], mixing, NT)
        dut[at, :] = mm(gyt[at, :], mixing)
        picked = go[:, pair : pair + 128] * (low if head % 2 == 0 else high_half)
        products = mm(picked, ut[pair : pair + 128, :])
        if head == 0:
            ds_[...] = products * decay
        else:
            ds_[...] += products * decay

    for head in range(HEADS // 2):
        inner(head)

    every(lambda step: in1(step).wait_recv())
    running = jnp.zeros((PART, STATE), F32)
    for source in range(SPANS):
        os_[source, 0:PART, :] = running.astype(BF)
        note = xr[source, 2 * PART : 2 * PART + 16, :].astype(F32)
        decay = note[0:1] + note[1:2]
        running = decay * running + xr[source, 0:PART, :].astype(F32)
    running = jnp.zeros((PART, STATE), F32)
    for source in reversed(range(SPANS)):
        os_[source, PART : 2 * PART, :] = running.astype(BF)
        note = xr[source, 2 * PART : 2 * PART + 16, :].astype(F32)
        decay = note[0:1] + note[1:2]
        running = decay * running + xr[source, PART : 2 * PART, :].astype(F32)
    every(lambda step: out2(step).start())
    or_[span] = os_[span]

    for head in range(HEADS // 2, HEADS):
        inner(head)
    ds = ds_[...].astype(BF)
    dc_t = mm(b_t, ds, NT)
    db_t = mm(c_t, ds)

    every(lambda step: in2(step).wait_recv())
    state_in = or_[:, 0:PART, :].reshape(XW, STATE)
    state_grad = or_[:, PART : 2 * PART, :].reshape(XW, STATE)
    carried = mm(state_in, c_t)
    reach = mm(state_grad, b_t)
    dc_t = dc_t + mm(state_in, gyw[...], TN)
    db_t = db_t + mm(state_grad, kut[...], TN)

    from_rows, from_u, from_keep, direct, ends = [], [], [], [], []
    for head in range(HEADS):
        at = head_rows(head)
        rows = slice(head * HDIM, (head + 1) * HDIM)
        x = ptx[at, :]
        gy = gyt[at, :].astype(F32)
        u = ut[at, :].astype(F32)
        y = yt[at, :] + carried[rows] * carry_w[head : head + 1, :]
        late = reach[rows] * keep_w[head : head + 1, :]
        du_here = dut[at, :]
        du = du_here + late
        from_rows.append(jnp.sum(gy * y, axis=0, keepdims=True))
        from_u.append(jnp.sum(u * du_here, axis=0, keepdims=True))
        from_keep.append(jnp.sum(u * late, axis=0, keepdims=True))
        direct.append(jnp.sum(x * du, axis=0, keepdims=True))
        ends.append(
            jnp.sum(state_in[rows].astype(F32) * state_grad[rows].astype(F32), axis=0, keepdims=True)
        )
        dx = du * dt[head : head + 1, :] + gy * skip[head : head + 1, :]
        pg[at, :] = dx * dst[at, :]
        yt[at, :] = y + x * skip[head : head + 1, :]
    pg[XW : XW + STATE, :] = db_t * dst[XW : XW + STATE, :]
    pg[XW + STATE : PROJ, :] = dc_t * dst[XW + STATE : PROJ, :]
    gap_grad = jnp.concatenate(from_rows, axis=0) - jnp.concatenate(from_u, axis=0)
    end_grad = jnp.sum(jnp.concatenate(ends, axis=0), axis=1, keepdims=True)
    log_grad = (
        sums(gap_grad, since)
        + sums(jnp.concatenate(from_keep, axis=0), before)
        + total * end_grad
    )
    dt_grad = (jnp.concatenate(direct, axis=0) + rate * log_grad) * dt_gate

    pg[PROJ : PROJ + HEADS, :] = dt_grad
    pg[PROJ + HEADS : WIDE, :] = jnp.zeros((128 - HEADS, SPAN), F32)
    pn[...] = jnp.transpose(pg[...])
    for place in range(PLANES):
        for half in range(2):
            at = half * 128 + SLOT[place] * 16
            pga[at : at + 16, :] = pn[home(place, half), :].astype(BF)

    def multiply(quarter):
        term = mm(pga[...], w[quarter * QUARTER : (quarter + 1) * QUARTER, :], NT)
        own[:, cols(quarter)] = term[0:128]
        sbs[:, cols(quarter)] = term[128:256].astype(BF)

    far = SLOT[4] * 16

    def swap_far(quarter):
        return pltpu.make_async_remote_copy(
            src_ref=sbs.at[far : far + 16, cols(quarter)], dst_ref=sbr.at[far : far + 16, cols(quarter)],
            send_sem=bf_s.at[quarter], recv_sem=bf_r.at[quarter],
            device_id={"tensor": twin}, device_id_type=MESH,
        )

    def swap(quarter):
        return pltpu.make_async_remote_copy(
            src_ref=sbs.at[0:far, cols(quarter)], dst_ref=sbr.at[0:far, cols(quarter)],
            send_sem=bb_s.at[quarter], recv_sem=bb_r.at[quarter],
            device_id={"tensor": twin}, device_id_type=MESH,
        )

    def pass_up(step, quarter, count):
        return pltpu.make_async_remote_copy(
            src_ref=ru_s.at[step, :, cols(quarter, count)], dst_ref=ru_r.at[step, :, cols(quarter, count)],
            send_sem=bu_s.at[step, quarter], recv_sem=bu_r.at[step, quarter],
            device_id={"tensor": up}, device_id_type=MESH,
        )

    def pass_down(step, quarter, count):
        return pltpu.make_async_remote_copy(
            src_ref=rd_s.at[step, :, cols(quarter, count)], dst_ref=rd_r.at[step, :, cols(quarter, count)],
            send_sem=bd_s.at[step, quarter], recv_sem=bd_r.at[step, quarter],
            device_id={"tensor": down}, device_id_type=MESH,
        )

    def pair_sum(place, quarter, count):
        at = slice(SLOT[place % PLANES] * 16, SLOT[place % PLANES] * 16 + 16)
        where = cols(quarter, count)
        return own[at, where] + sbr[at, where].astype(F32)

    def go_up(step, quarter, count):
        value = pair_sum(4 - step, quarter, count)
        if step > 1 or (step == 1 and quarter == 0):
            for unit in quarters[:2] if step == 1 else ((quarter, count),):
                pass_up(step - 1, *unit).wait_recv()
            value = value + ru_r[step - 1, :, cols(quarter, count)].astype(F32)
        ru_s[step, :, cols(quarter, count)] = value.astype(BF)
        pass_up(step, quarter, count).start()

    def go_down(step, quarter, count):
        value = pair_sum(4 + step, quarter, count)
        if step > 1 or (step == 1 and quarter == 2):
            for unit in quarters[2:] if step == 1 else ((quarter, count),):
                pass_down(step - 1, *unit).wait_recv()
            value = value + rd_r[step - 1, :, cols(quarter, count)].astype(F32)
        rd_s[step, :, cols(quarter, count)] = value.astype(BF)
        pass_down(step, quarter, count).start()

    def first_pass(quarter):
        swap_far(quarter).wait_recv()
        (go_up if quarter < 2 else go_down)(0, quarter, 1)

    ready = None
    for quarter in (0, 2, 1, 3):
        multiply(quarter)
        swap_far(quarter).start()
        swap(quarter).start()
        if ready is not None:
            first_pass(ready)
        ready = quarter
    first_pass(ready)
    for quarter in (2, 3):
        swap(quarter).wait_recv()
    go_up(1, 2, 2)
    for quarter in (0, 1):
        swap(quarter).wait_recv()
    go_down(1, 0, 2)
    go_up(1, 0, 2)
    go_down(1, 2, 2)
    y_out[...] = jnp.transpose(yt[...]).astype(BF)
    for step in (2, 3):
        go_up(step, 2, 2)
        go_down(step, 0, 2)
        go_up(step, 0, 2)
        go_down(step, 2, 2)

    def finish(quarter, up_here, down_here):
        value = pair_sum(0, quarter, 2)
        if up_here:
            pass_up(3, quarter, 2).wait_recv()
        if down_here:
            pass_down(3, quarter, 2).wait_recv()
        value = value + ru_r[3, :, cols(quarter, 2)].astype(F32)
        value = value + rd_r[3, :, cols(quarter, 2)].astype(F32)
        gh_out[:, cols(quarter, 2)] = value.astype(BF)

    finish(2, True, True)
    finish(0, True, True)

    for step in range(4):
        for unit in up_units[step]:
            to_up(step, *unit).wait_send()
        for unit in down_units[step]:
            to_down(step, *unit).wait_send()
    for place in range(PLANES):
        for unit in twin_units.get(place, halves):
            to_twin(place, *unit).wait_send()
    for quarter in range(4):
        swap_far(quarter).wait_send()
        swap(quarter).wait_send()
    for step in range(4):
        for unit in quarters[:2] if step == 0 else halves:
            pass_up(step, *unit).wait_send()
        for unit in quarters[2:] if step == 0 else halves:
            pass_down(step, *unit).wait_send()
    every(lambda step: out1(step).wait_send())
    every(lambda step: out2(step).wait_send())


def per_device(hidden, w_proj, w_dt, dt_bias, a_log, d_skip, doc_lengths, grad_out):
    vmem = pl.BlockSpec(memory_space=pltpu.VMEM)
    smem = pl.BlockSpec(memory_space=pltpu.SMEM)
    dma = pltpu.SemaphoreType.DMA
    whole = pl.BlockSpec(memory_space=pl.ANY)
    return pl.pallas_call(
        kernel,
        out_shape=(
            pltpu.VMEM((SPAN, XW), BF),
            pltpu.VMEM((ROWS, FEAT), BF),
        ),
        in_specs=[vmem, whole, vmem, smem, smem, smem, smem, vmem],
        out_specs=(vmem, vmem),
        scratch_shapes=[
            pltpu.VMEM((FEAT, WIDE), BF),
            pltpu.VMEM((SPAN, FEAT), BF),
            pltpu.VMEM((SPAN, WIDE), F32),
            pltpu.VMEM((SPAN, SPAN), F32),
            pltpu.VMEM((XW, SPAN), BF),
            pltpu.VMEM((SPAN, WIDE), F32),
            pltpu.VMEM((PROJ, SPAN), F32),
            pltpu.VMEM((PROJ, SPAN), F32),
            pltpu.VMEM((XW, SPAN), BF),
            pltpu.VMEM((XW, SPAN), BF),
            pltpu.VMEM((XW, SPAN), BF),
            pltpu.VMEM((XW, SPAN), F32),
            pltpu.VMEM((XW, SPAN), F32),
            pltpu.VMEM((SPAN, SPAN), F32),
            pltpu.VMEM((SPANS, 2 * PART + 16, STATE), BF),
            pltpu.VMEM((SPANS, 2 * PART + 16, STATE), BF),
            pltpu.VMEM((SPANS, 2 * PART, STATE), BF),
            pltpu.VMEM((SPANS, 2 * PART, STATE), BF),
            pltpu.VMEM((WIDE, SPAN), F32),
            pltpu.VMEM((SPAN, WIDE), BF),
            pltpu.VMEM((128, FEAT), F32),
            pltpu.VMEM((128, FEAT), BF),
            pltpu.VMEM((128, FEAT), BF),
            pltpu.VMEM((4, ROWS, FEAT), BF),
            pltpu.VMEM((4, ROWS, FEAT), BF),
            pltpu.VMEM((4, ROWS, FEAT), BF),
            pltpu.VMEM((4, ROWS, FEAT), BF),
            dma,
            dma((4, 4)), dma((4, 4)), dma((4, 4)), dma((4, 4)),
            dma((PLANES, 4)), dma((PLANES, 4)),
            dma((SPANS,)), dma((SPANS,)), dma((SPANS,)), dma((SPANS,)),
            dma((4, 4)), dma((4, 4)), dma((4, 4)), dma((4, 4)),
            dma((4,)), dma((4,)), dma((4,)), dma((4,)),
        ],
        compiler_params=pltpu.CompilerParams(
            collective_id=0, has_side_effects=True, vmem_limit_bytes=58 * 1024 * 1024
        ),
        name="layer",
    )(hidden, w_proj, w_dt, dt_bias, a_log, d_skip, doc_lengths, grad_out)


def solution(mesh):
    placed = (
        P(("context", "tensor"), None),
        P(None, "tensor"),
        P("tensor", None),
        P("tensor"),
        P("tensor"),
        P("tensor"),
        P(),
        P("context", "tensor"),
    )
    return jax.shard_map(
        per_device,
        mesh=mesh,
        in_specs=placed,
        out_specs=(P("context", "tensor"), P(("context", "tensor"), None)),
        check_vma=False,
    )
```

```python
import jax
import jax.numpy as jnp
from jax import lax
from jax.experimental import pallas as pl
from jax.experimental.pallas import tpu as pltpu
from jax.sharding import PartitionSpec as P

BF = jnp.bfloat16
F32 = jnp.float32
MESH = pl.DeviceIdType.MESH

PLANES = 8
SPANS = 16
ROWS = 16
SPAN = 256
FEAT = 8192
HEADS = 8
HDIM = 64
XW = HEADS * HDIM
STATE = 128
PROJ = XW + 2 * STATE
WIDE = PROJ + 128
QUARTER = FEAT // 4
PART = XW // SPANS
SLOT = {0: 0, 1: 1, 7: 2, 2: 3, 6: 4, 3: 5, 5: 6, 4: 7}
NEAR = 5 * 32

NN = (((1,), (0,)), ((), ()))
NT = (((1,), (1,)), ((), ()))
TN = (((0,), (0,)), ((), ()))


def mm(a, b, dims=NN):
    return lax.dot_general(a, b, dims, preferred_element_type=F32)


def cols(quarter, count=1):
    return pl.ds(quarter * QUARTER, count * QUARTER)


def quantize(rows):
    lane = lax.broadcasted_iota(jnp.int32, rows.shape, 1)
    largest = jnp.abs(rows)
    for step in (1, 2, 4, 8, 16):
        below = pltpu.roll(largest, step, 1)
        above = pltpu.roll(largest, 128 - step, 1)
        largest = jnp.maximum(largest, jnp.where((lane & step) != 0, below, above))
    power = jnp.exp2(jnp.floor(jnp.log2(jnp.maximum(largest, 2.0**-39)))).astype(BF).astype(F32)
    power = jnp.where(power > largest, power * 0.5, power)
    power = jnp.where(power * 2.0 <= largest, power * 2.0, power)
    scale = jnp.where(largest >= 2.0**-39, power * 2.0**-8, 2.0**-48)
    lifted = rows * 2.0**20
    normal = (rows + lifted) - lifted
    anchor = scale * (1.5 * 2.0**14)
    small = (rows + anchor) - anchor
    snapped = jnp.where(jnp.abs(rows) < scale * 2.0**-6, small, normal)
    bound = scale * 448.0
    return jnp.clip(snapped, -bound, bound)


def split3(values):
    first = values.astype(BF)
    rest = values - first.astype(F32)
    second = rest.astype(BF)
    third = (rest - second.astype(F32)).astype(BF)
    return first, second, third


def sums(values, chosen):
    first, second, third = split3(values)
    stacked = jnp.concatenate(
        [first.astype(F32), second.astype(F32), third.astype(F32), jnp.zeros_like(values)], axis=0
    ).astype(BF)
    out = mm(stacked, chosen)
    return out[0:8] + out[8:16] + out[16:24]


def head_lanes(scalars):
    lane = lax.broadcasted_iota(jnp.int32, (8, 128), 1)
    out = jnp.zeros((8, 128), F32)
    for head in range(HEADS):
        out = jnp.where(lane == head, scalars[head], out)
    return out


def split2(values):
    high = values.astype(BF)
    return high, (values - high.astype(F32)).astype(BF)


def spread(values, spreader):
    return mm(jnp.concatenate(split2(values), axis=1), spreader)


def head_rows(head):
    return pl.ds(head * HDIM, HDIM)


def kernel(
    hid, w_hbm, wdt_ref, bias_ref, alog_ref, skip_ref, docs, go,
    y_out, gh_out,
    w, wt, xb, acc, bias_m, masks, spreader, gyt, pn, dn_, xn, dstn, bc, dte, kdd, crw, xk, ku, gw,
    ut, yt, dut, ds_, yn, pre, dbc, xs, xr, os_, or_, pgn, pga, sbr, ru_r, rd_r,
    wsem, au_s, au_r, ad_s, ad_r, ab_s, ab_r, x1s, x1r, x2s, x2r,
    bu_s, bu_r, bd_s, bd_r, bb_s, bb_r, bf_s, bf_r, bn_s, bn_r, heard,
):
    me = lax.axis_index("tensor")
    span = lax.axis_index("context")
    z = me // 2
    core = me % 2
    up = lax.rem(z + 1, PLANES) * 2 + core
    down = lax.rem(z + PLANES - 1, PLANES) * 2 + core
    twin = z * 2 + (1 - core)

    w_copy = pltpu.make_async_copy(w_hbm, w.at[:, 0:PROJ], wsem)
    w_copy.start()

    barrier = pltpu.get_barrier_semaphore()
    for near in (up, down, twin):
        pl.semaphore_signal(barrier, inc=1, device_id={"tensor": near}, device_id_type=MESH)

    x, y = span % 4, span // 4
    beside = (y * 4 + lax.rem(x + 1, 4), y * 4 + lax.rem(x + 3, 4))
    across = (lax.rem(y + 1, 4) * 4 + x, lax.rem(y + 3, 4) * 4 + x)
    for near in beside + across:
        pl.semaphore_signal(barrier, inc=1, device_id={"context": near}, device_id_type=MESH)

    def tell(whom, sem):
        for near in whom:
            pl.semaphore_signal(sem, inc=1, device_id={"context": near}, device_id_type=MESH)

    def block(place, half, quarter, count):
        return xb.at[pl.ds(SLOT[place % PLANES] * 32 + half * 16, ROWS), cols(quarter, count)]

    def to_up(step, quarter, count):
        return pltpu.make_async_remote_copy(
            src_ref=block(-step, 0, quarter, count), dst_ref=block(-step - 1, 0, quarter, count),
            send_sem=au_s.at[step, quarter], recv_sem=au_r.at[step, quarter],
            device_id={"tensor": up}, device_id_type=MESH,
        )

    def to_down(step, quarter, count):
        return pltpu.make_async_remote_copy(
            src_ref=block(step, 0, quarter, count), dst_ref=block(step + 1, 0, quarter, count),
            send_sem=ad_s.at[step, quarter], recv_sem=ad_r.at[step, quarter],
            device_id={"tensor": down}, device_id_type=MESH,
        )

    def to_twin(place, quarter, count):
        place = place % PLANES
        return pltpu.make_async_remote_copy(
            src_ref=block(place, 0, quarter, count), dst_ref=block(place, 1, quarter, count),
            send_sem=ab_s.at[place, quarter], recv_sem=ab_r.at[place, quarter],
            device_id={"tensor": twin}, device_id_type=MESH,
        )

    quarters = ((0, 1), (1, 1), (2, 1), (3, 1))
    halves = ((0, 2), (2, 2))
    up_units = (quarters, halves, halves, quarters[:2])
    down_units = (quarters[2:] + quarters[:2], halves[::-1], halves[::-1], quarters[2:])
    twin_units = {0: ((0, 4),), 4: quarters}

    tiles = QUARTER // 128

    def encode(quarter):
        part = hid[:, quarter * QUARTER : (quarter + 1) * QUARTER].astype(F32)
        stacked = jnp.concatenate(
            [part[:, i * 128 : (i + 1) * 128] for i in range(tiles)], axis=0
        )
        snapped = quantize(stacked)
        flat = jnp.concatenate(
            [snapped[i * ROWS : (i + 1) * ROWS] for i in range(tiles)], axis=1
        )
        xb[0:ROWS, quarter * QUARTER : (quarter + 1) * QUARTER] = flat.astype(BF)

    encode(0)
    pl.semaphore_wait(barrier, 7)
    to_up(0, 0, 1).start()
    encode(2)
    to_down(0, 2, 1).start()
    encode(1)
    to_up(0, 1, 1).start()
    encode(3)
    to_down(0, 3, 1).start()
    to_up(0, 2, 1).start()
    to_down(0, 0, 1).start()
    to_up(0, 3, 1).start()
    to_down(0, 1, 1).start()
    to_twin(0, 0, 4).start()
    tell(beside, heard.at[0])

    first_token = span * SPAN

    def segment(positions):
        out = jnp.full(positions.shape, -1, jnp.int32)
        begin = jnp.int32(0)
        for doc in range(8):
            out = out + jnp.where(positions >= begin, 1, 0)
            begin = begin + docs[doc]
        return out

    row_pos = first_token + lax.broadcasted_iota(jnp.int32, (SPAN, SPAN), 0)
    col_pos = first_token + lax.broadcasted_iota(jnp.int32, (SPAN, SPAN), 1)
    bias_m[...] = jnp.where(
        (row_pos >= col_pos) & (segment(row_pos) == segment(col_pos)), 0.0, -1e30
    )
    token = first_token + lax.broadcasted_iota(jnp.int32, (SPAN, 128), 0)
    seg = segment(token)
    none = jnp.zeros((8, 128), jnp.int32)
    seg_before = segment(none + (first_token - 1))
    seg_last = segment(none + (first_token + SPAN - 1))
    masks[0] = jnp.where(seg == seg_before[0:1], 1.0, 0.0)
    masks[1] = jnp.where(seg == seg_last[0:1], 1.0, 0.0)
    through = jnp.where(seg_last == seg_before, 1.0, 0.0)
    head_of_row = lax.rem(lax.broadcasted_iota(jnp.int32, (256, XW), 0), 128)
    head_of_lane = lax.broadcasted_iota(jnp.int32, (256, XW), 1) // HDIM
    spreader[...] = jnp.where(head_of_row == head_of_lane, 1.0, 0.0).astype(BF)
    gyt[...] = jnp.transpose(go[...].astype(F32)).astype(BF)

    for quarter in range(4):
        steps_w = wdt_ref[:, quarter * QUARTER : (quarter + 1) * QUARTER].astype(F32)
        padded = jnp.concatenate([steps_w, jnp.zeros((120, QUARTER), F32)], axis=0)
        w[cols(quarter), PROJ:WIDE] = jnp.transpose(padded).astype(BF)
        wt[PROJ:WIDE, cols(quarter)] = padded.astype(BF)
    square_row = lax.broadcasted_iota(jnp.int32, (256, 256), 0)
    square_lane = lax.broadcasted_iota(jnp.int32, (256, 256), 1)
    same = jnp.where(square_row == square_lane, 1.0, 0.0).astype(BF)
    units = [(quarter, first) for quarter in (0, 2, 1, 3) for first in range(0, PROJ, 256)]

    def turn_weights(count):
        for _ in range(count):
            quarter, first = units.pop(0)
            at = slice(first, first + 256)
            wt[at, cols(quarter)] = mm(same, w[cols(quarter), at], NT).astype(BF)

    def project(first, last, quarter, begin):
        at = slice(quarter * QUARTER, (quarter + 1) * QUARTER)
        part = mm(xb[first:last, at], w[at, :])
        if begin:
            acc[first:last, :] = part
        else:
            acc[first:last, :] += part

    def arrived_twin(place):
        for unit in twin_units.get(place, halves):
            to_twin(place, *unit).wait_recv()

    def between(step, turn):
        if (step, turn) == (0, 0):
            pl.semaphore_wait(heard.at[0], 2)
            tell(across, heard.at[1])
            w_copy.wait()
            turn_weights(3)
        elif (step, turn) == (0, 1):
            pl.semaphore_wait(heard.at[1], 2)
            tell(across, heard.at[2])
            turn_weights(3)
        elif (step, turn) == (1, 0):
            pl.semaphore_wait(heard.at[2], 2)
            turn_weights(4)
        elif (step, turn) == (1, 1):
            turn_weights(2)
            for place in (0, 1, 7, 2, 6):
                arrived_twin(place)
            project(0, NEAR, 0, True)
            project(0, NEAR, 1, False)
        elif (step, turn) == (2, 0):
            project(0, NEAR, 2, False)
            project(0, NEAR, 3, False)

    for step in range(3):
        for turn in range(2):
            unit = halves[turn]
            for got in quarters[2 * turn : 2 * turn + 2] if step == 0 else (unit,):
                to_up(step, *got).wait_recv()
            if step < 2:
                to_up(step + 1, *unit).start()
            elif turn == 0:
                for part in up_units[3]:
                    to_up(3, *part).start()
            to_twin(-step - 1, *unit).start()
            unit = halves[1 - turn]
            for got in quarters[2 - 2 * turn : 4 - 2 * turn] if step == 0 else (unit,):
                to_down(step, *got).wait_recv()
            if step < 2:
                to_down(step + 1, *unit).start()
            elif turn == 0:
                for part in down_units[3]:
                    to_down(3, *part).start()
            to_twin(step + 1, *unit).start()
            between(step, turn)
    for at in range(2):
        to_up(3, *up_units[3][at]).wait_recv()
        to_twin(4, *up_units[3][at]).start()
        to_down(3, *down_units[3][at]).wait_recv()
        to_twin(4, *down_units[3][at]).start()
    arrived_twin(3)
    arrived_twin(5)
    for quarter in (0, 2, 1, 3):
        to_twin(4, quarter, 1).wait_recv()
        project(NEAR, SPAN, quarter, quarter == 0)

    def home(place, half):
        owner = lax.rem(z + place, PLANES) * 2 + (core if half == 0 else 1 - core)
        return pl.ds(pl.multiple_of(owner * ROWS, ROWS), ROWS)

    for place in range(PLANES):
        for half in range(2):
            at = SLOT[place] * 32 + half * 16
            pn[home(place, half), :] = acc[at : at + 16, 0:PROJ].astype(BF).astype(F32)
            dn_[home(place, half), :] = acc[at : at + 16, PROJ:WIDE]

    row = lax.broadcasted_iota(jnp.int32, (SPAN, SPAN), 0)
    lane = lax.broadcasted_iota(jnp.int32, (SPAN, SPAN), 1)
    rate = -jnp.exp(head_lanes(alog_ref))
    skip = head_lanes(skip_ref)
    dt_arg = dn_[...] + head_lanes(bias_ref)[0:1]
    dt = jnp.maximum(dt_arg, 0.0) + jnp.log1p(jnp.exp(-jnp.abs(dt_arg)))
    dt_gate = 1.0 / (1.0 + jnp.exp(-dt_arg))
    summed = mm(
        jnp.where(row >= lane, 1.0, 0.0).astype(BF),
        jnp.concatenate(split3(dt * rate[0:1]), axis=1),
    )
    cum = summed[:, 0:128] + summed[:, 128:256] + summed[:, 256:384]
    cum_last = cum[SPAN - 1 : SPAN]
    carry_w = jnp.exp(cum) * masks[0]
    keep_w = jnp.exp(cum_last - cum) * masks[1]
    total = jnp.exp(jnp.broadcast_to(cum_last, (8, 128))) * through
    keep_dt = spread(keep_w * dt, spreader[...])
    crw[...] = spread(carry_w, spreader[...])
    projected = pn[...]
    gate = 1.0 / (1.0 + jnp.exp(-projected))
    dstn[...] = gate * (1.0 + projected * (1.0 - gate))
    active = projected * gate
    xn[...] = active[:, 0:XW]
    bc[...] = active[:, XW:PROJ].astype(BF)
    b_nat = bc[:, 0:STATE]
    c_nat = bc[:, STATE : 2 * STATE]
    b_t = jnp.transpose(active[:, XW : XW + STATE]).astype(BF)
    c_t = jnp.transpose(active[:, XW + STATE : PROJ]).astype(BF)
    ku[...] = (xn[...] * keep_dt).astype(BF)
    gw[...] = (go[...].astype(F32) * crw[...]).astype(BF)
    end_state = mm(b_t, ku[...]).astype(BF)
    from_out = mm(c_t, gw[...]).astype(BF)
    note_row = lax.broadcasted_iota(jnp.int32, (16, 128), 0)
    high, low_part = split2(total[0:1])
    note = jnp.where(note_row == 0, high.astype(F32), jnp.where(note_row == 1, low_part.astype(F32), 0.0))
    note = mm(note.astype(BF), spreader[0:128, :]).astype(BF)
    for part in range(SPANS):
        at = slice(part % 4 * PART, part % 4 * PART + PART)
        pair = slice(part // 4 * 128, part // 4 * 128 + 128)
        xs[part, 0:PART, :] = end_state[at, pair]
        xs[part, PART : 2 * PART, :] = from_out[at, pair]
        xs[part, 2 * PART : 2 * PART + 16, :] = note[:, pair]

    def other(step):
        return lax.rem(span + step, SPANS)

    def out1(step):
        return pltpu.make_async_remote_copy(
            src_ref=xs.at[other(step)], dst_ref=xr.at[span],
            send_sem=x1s.at[other(step)], recv_sem=x1r.at[span],
            device_id={"context": other(step)}, device_id_type=MESH,
        )

    def in1(step):
        return pltpu.make_async_remote_copy(
            src_ref=xs.at[other(step)], dst_ref=xr.at[other(step)],
            send_sem=x1s.at[other(step)], recv_sem=x1r.at[other(step)],
            device_id={"context": other(step)}, device_id_type=MESH,
        )

    def out2(step):
        return pltpu.make_async_remote_copy(
            src_ref=os_.at[other(step)], dst_ref=or_.at[span],
            send_sem=x2s.at[other(step)], recv_sem=x2r.at[span],
            device_id={"context": other(step)}, device_id_type=MESH,
        )

    def in2(step):
        return pltpu.make_async_remote_copy(
            src_ref=os_.at[other(step)], dst_ref=or_.at[other(step)],
            send_sem=x2s.at[other(step)], recv_sem=x2r.at[other(step)],
            device_id={"context": other(step)}, device_id_type=MESH,
        )

    def every(action):
        for step in (10, 9, 11, 6, 14, 8, 2, 5, 7, 13, 15, 4, 12, 1, 3):
            action(step)

    every(lambda step: out1(step).start())
    xr[span] = xs[span]

    dte[...] = spread(dt, spreader[...])
    xk[...] = (xn[...] * spread(keep_w, spreader[...])).astype(BF)
    kdd[...] = keep_dt * dstn[:, 0:XW]
    ut[...] = jnp.transpose(xn[...] * dte[...]).astype(BF)
    cum_row = jnp.transpose(cum)
    scores = mm(c_nat, b_t)
    low = jnp.where(lax.broadcasted_iota(jnp.int32, (1, 128), 1) < HDIM, 1.0, 0.0).astype(BF)
    high_half = jnp.where(lax.broadcasted_iota(jnp.int32, (1, 128), 1) < HDIM, 0.0, 1.0).astype(BF)

    def inner(head):
        at = head_rows(head)
        pair = head // 2 * 128
        gap = cum[:, head : head + 1] - cum_row[head : head + 1, :] + bias_m[...]
        decay = jnp.exp(gap)
        mixing = (scores * decay).astype(BF)
        yt[at, :] = mm(ut[at, :], mixing, NT)
        dut[at, :] = mm(gyt[at, :], mixing)
        picked = go[:, pair : pair + 128] * (low if head % 2 == 0 else high_half)
        products = mm(picked, ut[pair : pair + 128, :])
        if head == 0:
            ds_[...] = products * decay
        else:
            ds_[...] += products * decay

    for head in range(HEADS // 2):
        inner(head)

    every(lambda step: in1(step).wait_recv())
    forward = jnp.zeros((PART, STATE), F32)
    back = jnp.zeros((PART, STATE), F32)
    for source in range(SPANS):
        os_[source, 0:PART, :] = forward.astype(BF)
        decays = xr[source, 2 * PART : 2 * PART + 16, :].astype(F32)
        forward = (decays[0:1] + decays[1:2]) * forward + xr[source, 0:PART, :].astype(F32)
        later = SPANS - 1 - source
        os_[later, PART : 2 * PART, :] = back.astype(BF)
        decays = xr[later, 2 * PART : 2 * PART + 16, :].astype(F32)
        back = (decays[0:1] + decays[1:2]) * back + xr[later, PART : 2 * PART, :].astype(F32)
    every(lambda step: out2(step).start())
    or_[span] = os_[span]

    for head in range(HEADS // 2, HEADS):
        inner(head)
    ds = ds_[...].astype(BF)
    dbc[:, 0:STATE] = mm(ds, c_nat, TN)
    dbc[:, STATE : 2 * STATE] = mm(ds, b_nat)
    gap_grad, direct = [], []
    for head in range(HEADS):
        at = head_rows(head)
        x_dt = ut[at, :].astype(F32)
        gap_grad.append(
            jnp.sum(gyt[at, :].astype(F32) * yt[at, :] - x_dt * dut[at, :], axis=0, keepdims=True)
        )
    yn[...] = jnp.transpose(yt[...])
    du_here = jnp.transpose(dut[...])
    skip_all = spread(skip, spreader[...])[0:1]
    x_here = xn[...]
    given = go[...].astype(F32)
    pre[...] = (du_here * dte[...] + given * skip_all) * dstn[:, 0:XW]
    yn[...] = yn[...] + x_here * skip_all
    direct = mm(
        jnp.concatenate(split2(x_here * du_here), axis=0), spreader[0:128, :], NT
    )
    direct = direct[0:SPAN] + direct[SPAN : 2 * SPAN]
    log_rows = sums(
        jnp.concatenate(gap_grad, axis=0), jnp.where(row >= lane, 1.0, 0.0).astype(BF)
    )
    log_here = jnp.transpose(
        jnp.concatenate([log_rows, jnp.zeros((120, SPAN), F32)], axis=0)
    )
    since_before = jnp.concatenate(
        [jnp.where(row <= lane, 1.0, 0.0).astype(BF), jnp.where(row > lane, 1.0, 0.0).astype(BF)],
        axis=1,
    )

    every(lambda step: in2(step).wait_recv())

    def gathered(first):
        return jnp.concatenate(
            [
                jnp.concatenate(
                    [or_[pair * 4 + part, first : first + PART, :] for part in range(4)], axis=0
                )
                for pair in range(4)
            ],
            axis=1,
        )

    state_in = gathered(0)
    state_grad = gathered(PART)
    carried = mm(c_nat, state_in)
    reach = mm(b_nat, state_grad)
    pgn[:, 0:XW] = (pre[...] + reach * kdd[...]).astype(BF)
    db = dbc[:, 0:STATE] + mm(ku[...], state_grad, NT)
    dc = dbc[:, STATE : 2 * STATE] + mm(gw[...], state_in, NT)
    pgn[:, XW : XW + STATE] = (db * dstn[:, XW : XW + STATE]).astype(BF)
    pgn[:, XW + STATE : PROJ] = (dc * dstn[:, XW + STATE : PROJ]).astype(BF)
    ends = jnp.sum(
        (state_in.astype(F32) * state_grad.astype(F32)).reshape(STATE // 8, 8, XW), axis=0
    )
    products = jnp.concatenate(
        [
            (gw[...].astype(F32) * carried).astype(BF),
            (ku[...].astype(F32) * reach).astype(BF),
            (xk[...].astype(F32) * reach).astype(BF),
            jnp.concatenate(split2(jnp.concatenate([ends, ends], axis=0)), axis=0),
        ],
        axis=0,
    )
    reduced = mm(products, spreader[0:128, :], NT)
    far_grad = mm(
        since_before, jnp.concatenate(split2(reduced[0 : 2 * SPAN]), axis=1)
    )
    far_grad = far_grad[:, 0:128] + far_grad[:, 128:256]
    end_grad = reduced[3 * SPAN : 3 * SPAN + 8] + reduced[3 * SPAN + 16 : 3 * SPAN + 24]
    end_grad = jnp.sum(end_grad, axis=0, keepdims=True)
    log_grad = log_here + far_grad + total[0:1] * end_grad
    dt_grad = (direct + reduced[2 * SPAN : 3 * SPAN] + rate[0:1] * log_grad) * dt_gate
    pgn[:, PROJ:WIDE] = dt_grad.astype(BF)
    yn[...] = yn[...] + carried * crw[...]

    for step in range(4):
        for unit in up_units[step]:
            to_up(step, *unit).wait_send()
        for unit in down_units[step]:
            to_down(step, *unit).wait_send()
    for place in range(PLANES):
        for unit in twin_units.get(place, halves):
            to_twin(place, *unit).wait_send()
    own, sbs = xb.at[0:128, :], xb.at[128:256, :]
    for place in range(PLANES):
        for half in range(2):
            at = half * 128 + SLOT[place] * 16
            pga[at : at + 16, :] = pgn[home(place, half), :]

    def multiply(quarter):
        term = mm(pga[...], wt[:, cols(quarter)]).astype(BF)
        own[:, cols(quarter)] = term[0:128]
        sbs[:, cols(quarter)] = term[128:256]

    def swap(quarter, first, last, sems):
        return pltpu.make_async_remote_copy(
            src_ref=sbs.at[first:last, cols(quarter)], dst_ref=sbr.at[first:last, cols(quarter)],
            send_sem=sems[0].at[quarter], recv_sem=sems[1].at[quarter],
            device_id={"tensor": twin}, device_id_type=MESH,
        )

    def swap_far(quarter):
        return swap(quarter, 112, 128, (bf_s, bf_r))

    def swap_next(quarter):
        return swap(quarter, 80, 112, (bn_s, bn_r))

    def swap_rest(quarter):
        return swap(quarter, 0, 80, (bb_s, bb_r))

    def place_rows(place):
        return pl.ds(SLOT[place % PLANES] * 16, 16)

    def pass_up(step, quarter, count):
        return pltpu.make_async_remote_copy(
            src_ref=own.at[place_rows(4 - step), cols(quarter, count)], dst_ref=ru_r.at[step, :, cols(quarter, count)],
            send_sem=bu_s.at[step, quarter], recv_sem=bu_r.at[step, quarter],
            device_id={"tensor": up}, device_id_type=MESH,
        )

    def pass_down(step, quarter, count):
        return pltpu.make_async_remote_copy(
            src_ref=own.at[place_rows(4 + step), cols(quarter, count)], dst_ref=rd_r.at[step, :, cols(quarter, count)],
            send_sem=bd_s.at[step, quarter], recv_sem=bd_r.at[step, quarter],
            device_id={"tensor": down}, device_id_type=MESH,
        )

    def pair_sum(place, quarter, count):
        at = place_rows(place)
        where = cols(quarter, count)
        return own[at, where].astype(F32) + sbr[at, where].astype(F32)

    def go_up(step, quarter, count):
        value = pair_sum(4 - step, quarter, count)
        if step > 1 or (step == 1 and quarter == 0):
            for unit in quarters[:2] if step == 1 else ((quarter, count),):
                pass_up(step - 1, *unit).wait_recv()
            value = value + ru_r[step - 1, :, cols(quarter, count)].astype(F32)
        own[place_rows(4 - step), cols(quarter, count)] = value.astype(BF)
        pass_up(step, quarter, count).start()

    def go_down(step, quarter, count):
        value = pair_sum(4 + step, quarter, count)
        if step > 1 or (step == 1 and quarter == 2):
            for unit in quarters[2:] if step == 1 else ((quarter, count),):
                pass_down(step - 1, *unit).wait_recv()
            value = value + rd_r[step - 1, :, cols(quarter, count)].astype(F32)
        own[place_rows(4 + step), cols(quarter, count)] = value.astype(BF)
        pass_down(step, quarter, count).start()

    def first_pass(quarter):
        swap_far(quarter).wait_recv()
        (go_up if quarter < 2 else go_down)(0, quarter, 1)

    for quarter in (0, 2, 1, 3):
        multiply(quarter)
        swap_far(quarter).start()
        swap_next(quarter).start()
    for quarter in (0, 2, 1, 3):
        swap_rest(quarter).start()
    for quarter in (0, 2, 1, 3):
        first_pass(quarter)
    for quarter in (2, 3):
        swap_next(quarter).wait_recv()
    go_up(1, 2, 2)
    for quarter in (0, 1):
        swap_next(quarter).wait_recv()
    go_down(1, 0, 2)
    go_up(1, 0, 2)
    go_down(1, 2, 2)
    for quarter in range(4):
        swap_rest(quarter).wait_recv()
    y_out[...] = yn[...].astype(BF)
    for step in (2, 3):
        go_up(step, 2, 2)
        go_down(step, 0, 2)
        go_up(step, 0, 2)
        go_down(step, 2, 2)

    def finish(quarter, up_here, down_here):
        value = pair_sum(0, quarter, 2)
        if up_here:
            pass_up(3, quarter, 2).wait_recv()
        if down_here:
            pass_down(3, quarter, 2).wait_recv()
        value = value + ru_r[3, :, cols(quarter, 2)].astype(F32)
        value = value + rd_r[3, :, cols(quarter, 2)].astype(F32)
        gh_out[:, cols(quarter, 2)] = value.astype(BF)

    finish(2, True, True)
    finish(0, True, True)

    for quarter in range(4):
        swap_far(quarter).wait_send()
        swap_next(quarter).wait_send()
        swap_rest(quarter).wait_send()
    for step in range(4):
        for unit in quarters[:2] if step == 0 else halves:
            pass_up(step, *unit).wait_send()
        for unit in quarters[2:] if step == 0 else halves:
            pass_down(step, *unit).wait_send()
    every(lambda step: out1(step).wait_send())
    every(lambda step: out2(step).wait_send())


def per_device(hidden, w_proj, w_dt, dt_bias, a_log, d_skip, doc_lengths, grad_out):
    vmem = pl.BlockSpec(memory_space=pltpu.VMEM)
    smem = pl.BlockSpec(memory_space=pltpu.SMEM)
    dma = pltpu.SemaphoreType.DMA
    whole = pl.BlockSpec(memory_space=pl.ANY)
    return pl.pallas_call(
        kernel,
        out_shape=(
            pltpu.VMEM((SPAN, XW), BF),
            pltpu.VMEM((ROWS, FEAT), BF),
        ),
        in_specs=[vmem, whole, vmem, smem, smem, smem, smem, vmem],
        out_specs=(vmem, vmem),
        scratch_shapes=[
            pltpu.VMEM((FEAT, WIDE), BF),
            pltpu.VMEM((WIDE, FEAT), BF),
            pltpu.VMEM((SPAN, FEAT), BF),
            pltpu.VMEM((SPAN, WIDE), F32),
            pltpu.VMEM((SPAN, SPAN), F32),
            pltpu.VMEM((2, SPAN, 128), F32),
            pltpu.VMEM((256, XW), BF),
            pltpu.VMEM((XW, SPAN), BF),
            pltpu.VMEM((SPAN, PROJ), F32),
            pltpu.VMEM((SPAN, 128), F32),
            pltpu.VMEM((SPAN, XW), F32),
            pltpu.VMEM((SPAN, PROJ), F32),
            pltpu.VMEM((SPAN, 2 * STATE), BF),
            pltpu.VMEM((SPAN, XW), F32),
            pltpu.VMEM((SPAN, XW), F32),
            pltpu.VMEM((SPAN, XW), F32),
            pltpu.VMEM((SPAN, XW), BF),
            pltpu.VMEM((SPAN, XW), BF),
            pltpu.VMEM((SPAN, XW), BF),
            pltpu.VMEM((XW, SPAN), BF),
            pltpu.VMEM((XW, SPAN), F32),
            pltpu.VMEM((XW, SPAN), F32),
            pltpu.VMEM((SPAN, SPAN), F32),
            pltpu.VMEM((SPAN, XW), F32),
            pltpu.VMEM((SPAN, XW), F32),
            pltpu.VMEM((SPAN, 2 * STATE), F32),
            pltpu.VMEM((SPANS, 2 * PART + 16, STATE), BF),
            pltpu.VMEM((SPANS, 2 * PART + 16, STATE), BF),
            pltpu.VMEM((SPANS, 2 * PART, STATE), BF),
            pltpu.VMEM((SPANS, 2 * PART, STATE), BF),
            pltpu.VMEM((SPAN, WIDE), BF),
            pltpu.VMEM((SPAN, WIDE), BF),
            pltpu.VMEM((128, FEAT), BF),
            pltpu.VMEM((4, ROWS, FEAT), BF),
            pltpu.VMEM((4, ROWS, FEAT), BF),
            dma,
            dma((4, 4)), dma((4, 4)), dma((4, 4)), dma((4, 4)),
            dma((PLANES, 4)), dma((PLANES, 4)),
            dma((SPANS,)), dma((SPANS,)), dma((SPANS,)), dma((SPANS,)),
            dma((4, 4)), dma((4, 4)), dma((4, 4)), dma((4, 4)),
            dma((4,)), dma((4,)), dma((4,)), dma((4,)), dma((4,)), dma((4,)),
            pltpu.SemaphoreType.REGULAR((3,)),
        ],
        compiler_params=pltpu.CompilerParams(
            collective_id=0, has_side_effects=True, vmem_limit_bytes=58 * 1024 * 1024
        ),
        name="layer",
    )(hidden, w_proj, w_dt, dt_bias, a_log, d_skip, doc_lengths, grad_out)


def solution(mesh):
    placed = (
        P(("context", "tensor"), None),
        P(None, "tensor"),
        P("tensor", None),
        P("tensor"),
        P("tensor"),
        P("tensor"),
        P(),
        P("context", "tensor"),
    )
    return jax.shard_map(
        per_device,
        mesh=mesh,
        in_specs=placed,
        out_specs=(P("context", "tensor"), P(("context", "tensor"), None)),
        check_vma=False,
    )
```

```python
import jax
import jax.numpy as jnp
from jax import lax
from jax.experimental import pallas as pl
from jax.experimental.pallas import tpu as pltpu
from jax.sharding import PartitionSpec as P

BF = jnp.bfloat16
F32 = jnp.float32
MESH = pl.DeviceIdType.MESH

PLANES = 8
SPANS = 16
ROWS = 16
SPAN = 256
FEAT = 8192
HEADS = 8
HDIM = 64
XW = HEADS * HDIM
STATE = 128
PROJ = XW + 2 * STATE
WIDE = PROJ + 128
QUARTER = FEAT // 4
PART = XW // SPANS
SLOT = {0: 0, 1: 1, 7: 2, 2: 3, 6: 4, 3: 5, 5: 6, 4: 7}
NEAR = 5 * 32

NN = (((1,), (0,)), ((), ()))
NT = (((1,), (1,)), ((), ()))
TN = (((0,), (0,)), ((), ()))


def mm(a, b, dims=NN):
    return lax.dot_general(a, b, dims, preferred_element_type=F32)


def cols(quarter, count=1):
    return pl.ds(quarter * QUARTER, count * QUARTER)


def quantize(rows):
    lane = lax.broadcasted_iota(jnp.int32, rows.shape, 1)
    largest = jnp.abs(rows)
    for step in (1, 2, 4, 8, 16):
        below = pltpu.roll(largest, step, 1)
        above = pltpu.roll(largest, 128 - step, 1)
        largest = jnp.maximum(largest, jnp.where((lane & step) != 0, below, above))
    power = jnp.exp2(jnp.floor(jnp.log2(jnp.maximum(largest, 2.0**-39)))).astype(BF).astype(F32)
    power = jnp.where(power > largest, power * 0.5, power)
    power = jnp.where(power * 2.0 <= largest, power * 2.0, power)
    scale = jnp.where(largest >= 2.0**-39, power * 2.0**-8, 2.0**-48)
    lifted = rows * 2.0**20
    normal = (rows + lifted) - lifted
    anchor = scale * (1.5 * 2.0**14)
    small = (rows + anchor) - anchor
    snapped = jnp.where(jnp.abs(rows) < scale * 2.0**-6, small, normal)
    bound = scale * 448.0
    return jnp.clip(snapped, -bound, bound)


def split3(values):
    first = values.astype(BF)
    rest = values - first.astype(F32)
    second = rest.astype(BF)
    third = (rest - second.astype(F32)).astype(BF)
    return first, second, third


def sums(values, chosen):
    first, second, third = split3(values)
    stacked = jnp.concatenate(
        [first.astype(F32), second.astype(F32), third.astype(F32), jnp.zeros_like(values)], axis=0
    ).astype(BF)
    out = mm(stacked, chosen)
    return out[0:8] + out[8:16] + out[16:24]


def head_lanes(scalars):
    lane = lax.broadcasted_iota(jnp.int32, (8, 128), 1)
    out = jnp.zeros((8, 128), F32)
    for head in range(HEADS):
        out = jnp.where(lane == head, scalars[head], out)
    return out


def split2(values):
    high = values.astype(BF)
    return high, (values - high.astype(F32)).astype(BF)


def spread(values, spreader):
    return mm(jnp.concatenate(split2(values), axis=1), spreader)


def head_rows(head):
    return pl.ds(head * HDIM, HDIM)


def kernel(
    hid, w_hbm, wdt_ref, bias_ref, alog_ref, skip_ref, docs, go,
    y_out, gh_out,
    w, wt, xb, acc, bias_m, masks, spreader, gyt, pn, dn_, xn, dstn, bc, dte, kdd, crw, xk, ku, gw,
    ut, yt, dut, ds_, yn, pre, dbc, xs, xr, os_, or_, pgn, pga, sbr, ru_r, rd_r,
    wsem, au_s, au_r, ad_s, ad_r, ab_s, ab_r, x1s, x1r, x2s, x2r,
    bu_s, bu_r, bd_s, bd_r, bb_s, bb_r, bf_s, bf_r, bn_s, bn_r, heard,
):
    me = lax.axis_index("tensor")
    span = lax.axis_index("context")
    z = me // 2
    core = me % 2
    up = lax.rem(z + 1, PLANES) * 2 + core
    down = lax.rem(z + PLANES - 1, PLANES) * 2 + core
    twin = z * 2 + (1 - core)

    w_copy = pltpu.make_async_copy(w_hbm, w.at[:, 0:PROJ], wsem)
    w_copy.start()

    barrier = pltpu.get_barrier_semaphore()
    for near in (up, down, twin):
        pl.semaphore_signal(barrier, inc=1, device_id={"tensor": near}, device_id_type=MESH)

    x, y = span % 4, span // 4
    beside = (y * 4 + lax.rem(x + 1, 4), y * 4 + lax.rem(x + 3, 4))
    across = (lax.rem(y + 1, 4) * 4 + x, lax.rem(y + 3, 4) * 4 + x)
    for near in beside + across:
        pl.semaphore_signal(barrier, inc=1, device_id={"context": near}, device_id_type=MESH)

    def tell(whom, sem):
        for near in whom:
            pl.semaphore_signal(sem, inc=1, device_id={"context": near}, device_id_type=MESH)

    def block(place, half, quarter, count):
        return xb.at[pl.ds(SLOT[place % PLANES] * 32 + half * 16, ROWS), cols(quarter, count)]

    def to_up(step, quarter, count):
        return pltpu.make_async_remote_copy(
            src_ref=block(-step, 0, quarter, count), dst_ref=block(-step - 1, 0, quarter, count),
            send_sem=au_s.at[step, quarter], recv_sem=au_r.at[step, quarter],
            device_id={"tensor": up}, device_id_type=MESH,
        )

    def to_down(step, quarter, count):
        return pltpu.make_async_remote_copy(
            src_ref=block(step, 0, quarter, count), dst_ref=block(step + 1, 0, quarter, count),
            send_sem=ad_s.at[step, quarter], recv_sem=ad_r.at[step, quarter],
            device_id={"tensor": down}, device_id_type=MESH,
        )

    def to_twin(place, quarter, count):
        place = place % PLANES
        return pltpu.make_async_remote_copy(
            src_ref=block(place, 0, quarter, count), dst_ref=block(place, 1, quarter, count),
            send_sem=ab_s.at[place, quarter], recv_sem=ab_r.at[place, quarter],
            device_id={"tensor": twin}, device_id_type=MESH,
        )

    quarters = ((0, 1), (1, 1), (2, 1), (3, 1))
    halves = ((0, 2), (2, 2))
    up_units = (quarters, halves, halves, quarters[:2])
    down_units = (quarters[2:] + quarters[:2], halves[::-1], halves[::-1], quarters[2:])
    twin_units = {0: ((0, 4),), 4: quarters}

    tiles = QUARTER // 128

    def encode(quarter):
        part = hid[:, quarter * QUARTER : (quarter + 1) * QUARTER].astype(F32)
        stacked = jnp.concatenate(
            [part[:, i * 128 : (i + 1) * 128] for i in range(tiles)], axis=0
        )
        snapped = quantize(stacked)
        flat = jnp.concatenate(
            [snapped[i * ROWS : (i + 1) * ROWS] for i in range(tiles)], axis=1
        )
        xb[0:ROWS, quarter * QUARTER : (quarter + 1) * QUARTER] = flat.astype(BF)

    encode(0)
    pl.semaphore_wait(barrier, 7)
    to_up(0, 0, 1).start()
    encode(2)
    to_down(0, 2, 1).start()
    encode(1)
    to_up(0, 1, 1).start()
    encode(3)
    to_down(0, 3, 1).start()
    to_up(0, 2, 1).start()
    to_down(0, 0, 1).start()
    to_up(0, 3, 1).start()
    to_down(0, 1, 1).start()
    to_twin(0, 0, 4).start()
    tell(beside, heard.at[0])

    first_token = span * SPAN

    def segment(positions):
        out = jnp.full(positions.shape, -1, jnp.int32)
        begin = jnp.int32(0)
        for doc in range(8):
            out = out + jnp.where(positions >= begin, 1, 0)
            begin = begin + docs[doc]
        return out

    row_pos = first_token + lax.broadcasted_iota(jnp.int32, (SPAN, SPAN), 0)
    col_pos = first_token + lax.broadcasted_iota(jnp.int32, (SPAN, SPAN), 1)
    bias_m[...] = jnp.where(
        (row_pos >= col_pos) & (segment(row_pos) == segment(col_pos)), 0.0, -1e30
    )
    token = first_token + lax.broadcasted_iota(jnp.int32, (SPAN, 128), 0)
    seg = segment(token)
    none = jnp.zeros((8, 128), jnp.int32)
    seg_before = segment(none + (first_token - 1))
    seg_last = segment(none + (first_token + SPAN - 1))
    masks[0] = jnp.where(seg == seg_before[0:1], 1.0, 0.0)
    masks[1] = jnp.where(seg == seg_last[0:1], 1.0, 0.0)
    through = jnp.where(seg_last == seg_before, 1.0, 0.0)
    head_of_row = lax.rem(lax.broadcasted_iota(jnp.int32, (256, XW), 0), 128)
    head_of_lane = lax.broadcasted_iota(jnp.int32, (256, XW), 1) // HDIM
    spreader[...] = jnp.where(head_of_row == head_of_lane, 1.0, 0.0).astype(BF)
    gyt[...] = jnp.transpose(go[...].astype(F32)).astype(BF)

    for quarter in range(4):
        steps_w = wdt_ref[:, quarter * QUARTER : (quarter + 1) * QUARTER].astype(F32)
        padded = jnp.concatenate([steps_w, jnp.zeros((120, QUARTER), F32)], axis=0)
        w[cols(quarter), PROJ:WIDE] = jnp.transpose(padded).astype(BF)
        wt[PROJ:WIDE, cols(quarter)] = padded.astype(BF)
    square_row = lax.broadcasted_iota(jnp.int32, (256, 256), 0)
    square_lane = lax.broadcasted_iota(jnp.int32, (256, 256), 1)
    same = jnp.where(square_row == square_lane, 1.0, 0.0).astype(BF)
    units = [(quarter, first) for quarter in (0, 2, 1, 3) for first in range(0, PROJ, 256)]

    def turn_weights(count):
        for _ in range(count):
            quarter, first = units.pop(0)
            at = slice(first, first + 256)
            wt[at, cols(quarter)] = mm(same, w[cols(quarter), at], NT).astype(BF)

    def project(first, last, quarter, begin):
        at = slice(quarter * QUARTER, (quarter + 1) * QUARTER)
        part = mm(xb[first:last, at], w[at, :])
        if begin:
            acc[first:last, :] = part
        else:
            acc[first:last, :] += part

    def arrived_twin(place):
        for unit in twin_units.get(place, halves):
            to_twin(place, *unit).wait_recv()

    def between(step, turn):
        if (step, turn) == (0, 0):
            pl.semaphore_wait(heard.at[0], 2)
            tell(across, heard.at[1])
            w_copy.wait()
            turn_weights(3)
        elif (step, turn) == (0, 1):
            pl.semaphore_wait(heard.at[1], 2)
            tell(across, heard.at[2])
            turn_weights(3)
        elif (step, turn) == (1, 0):
            pl.semaphore_wait(heard.at[2], 2)
            turn_weights(4)
        elif (step, turn) == (1, 1):
            turn_weights(2)
            for place in (0, 1, 7, 2, 6):
                arrived_twin(place)
            project(0, NEAR, 0, True)
            project(0, NEAR, 1, False)
        elif (step, turn) == (2, 0):
            project(0, NEAR, 2, False)
            project(0, NEAR, 3, False)

    for step in range(3):
        for turn in range(2):
            unit = halves[turn]
            for got in quarters[2 * turn : 2 * turn + 2] if step == 0 else (unit,):
                to_up(step, *got).wait_recv()
            if step < 2:
                to_up(step + 1, *unit).start()
            elif turn == 0:
                for part in up_units[3]:
                    to_up(3, *part).start()
            to_twin(-step - 1, *unit).start()
            unit = halves[1 - turn]
            for got in quarters[2 - 2 * turn : 4 - 2 * turn] if step == 0 else (unit,):
                to_down(step, *got).wait_recv()
            if step < 2:
                to_down(step + 1, *unit).start()
            elif turn == 0:
                for part in down_units[3]:
                    to_down(3, *part).start()
            to_twin(step + 1, *unit).start()
            between(step, turn)
    for at in range(2):
        to_up(3, *up_units[3][at]).wait_recv()
        to_twin(4, *up_units[3][at]).start()
        to_down(3, *down_units[3][at]).wait_recv()
        to_twin(4, *down_units[3][at]).start()
    arrived_twin(3)
    arrived_twin(5)
    for quarter in (0, 2, 1, 3):
        to_twin(4, quarter, 1).wait_recv()
        project(NEAR, SPAN, quarter, quarter == 0)

    def home(place, half):
        owner = lax.rem(z + place, PLANES) * 2 + (core if half == 0 else 1 - core)
        return pl.ds(pl.multiple_of(owner * ROWS, ROWS), ROWS)

    for place in range(PLANES):
        for half in range(2):
            at = SLOT[place] * 32 + half * 16
            pn[home(place, half), :] = acc[at : at + 16, 0:PROJ].astype(BF).astype(F32)
            dn_[home(place, half), :] = acc[at : at + 16, PROJ:WIDE]

    row = lax.broadcasted_iota(jnp.int32, (SPAN, SPAN), 0)
    lane = lax.broadcasted_iota(jnp.int32, (SPAN, SPAN), 1)
    rate = -jnp.exp(head_lanes(alog_ref))
    skip = head_lanes(skip_ref)
    dt_arg = dn_[...] + head_lanes(bias_ref)[0:1]
    dt = jnp.maximum(dt_arg, 0.0) + jnp.log1p(jnp.exp(-jnp.abs(dt_arg)))
    dt_gate = 1.0 / (1.0 + jnp.exp(-dt_arg))
    summed = mm(
        jnp.where(row >= lane, 1.0, 0.0).astype(BF),
        jnp.concatenate(split3(dt * rate[0:1]), axis=1),
    )
    cum = summed[:, 0:128] + summed[:, 128:256] + summed[:, 256:384]
    cum_last = cum[SPAN - 1 : SPAN]
    carry_w = jnp.exp(cum) * masks[0]
    keep_w = jnp.exp(cum_last - cum) * masks[1]
    total = jnp.exp(jnp.broadcast_to(cum_last, (8, 128))) * through
    keep_dt = spread(keep_w * dt, spreader[...])
    crw[...] = spread(carry_w, spreader[...])
    projected = pn[...]
    gate = 1.0 / (1.0 + jnp.exp(-projected))
    dstn[...] = gate * (1.0 + projected * (1.0 - gate))
    active = projected * gate
    xn[...] = active[:, 0:XW]
    bc[...] = active[:, XW:PROJ].astype(BF)
    b_nat = bc[:, 0:STATE]
    c_nat = bc[:, STATE : 2 * STATE]
    b_t = jnp.transpose(active[:, XW : XW + STATE]).astype(BF)
    c_t = jnp.transpose(active[:, XW + STATE : PROJ]).astype(BF)
    ku[...] = (xn[...] * keep_dt).astype(BF)
    gw[...] = (go[...].astype(F32) * crw[...]).astype(BF)
    end_state = mm(b_t, ku[...]).astype(BF)
    from_out = mm(c_t, gw[...]).astype(BF)
    note_row = lax.broadcasted_iota(jnp.int32, (16, 128), 0)
    high, low_part = split2(total[0:1])
    note = jnp.where(note_row == 0, high.astype(F32), jnp.where(note_row == 1, low_part.astype(F32), 0.0))
    note = mm(note.astype(BF), spreader[0:128, :]).astype(BF)
    for part in range(SPANS):
        at = slice(part % 4 * PART, part % 4 * PART + PART)
        pair = slice(part // 4 * 128, part // 4 * 128 + 128)
        xs[part, 0:PART, :] = end_state[at, pair]
        xs[part, PART : 2 * PART, :] = from_out[at, pair]
        xs[part, 2 * PART : 2 * PART + 16, :] = note[:, pair]

    def other(step):
        return lax.rem(span + step, SPANS)

    def out1(step):
        return pltpu.make_async_remote_copy(
            src_ref=xs.at[other(step)], dst_ref=xr.at[span],
            send_sem=x1s.at[other(step)], recv_sem=x1r.at[span],
            device_id={"context": other(step)}, device_id_type=MESH,
        )

    def in1(step):
        return pltpu.make_async_remote_copy(
            src_ref=xs.at[other(step)], dst_ref=xr.at[other(step)],
            send_sem=x1s.at[other(step)], recv_sem=x1r.at[other(step)],
            device_id={"context": other(step)}, device_id_type=MESH,
        )

    def out2(step):
        return pltpu.make_async_remote_copy(
            src_ref=os_.at[other(step)], dst_ref=or_.at[span],
            send_sem=x2s.at[other(step)], recv_sem=x2r.at[span],
            device_id={"context": other(step)}, device_id_type=MESH,
        )

    def in2(step):
        return pltpu.make_async_remote_copy(
            src_ref=os_.at[other(step)], dst_ref=or_.at[other(step)],
            send_sem=x2s.at[other(step)], recv_sem=x2r.at[other(step)],
            device_id={"context": other(step)}, device_id_type=MESH,
        )

    def every(action):
        for step in (10, 9, 11, 6, 14, 8, 2, 5, 7, 13, 15, 4, 12, 1, 3):
            action(step)

    every(lambda step: out1(step).start())
    xr[span] = xs[span]

    dte[...] = spread(dt, spreader[...])
    xk[...] = (xn[...] * spread(keep_w, spreader[...])).astype(BF)
    kdd[...] = keep_dt * dstn[:, 0:XW]
    ut[...] = jnp.transpose(xn[...] * dte[...]).astype(BF)
    cum_row = jnp.transpose(cum)
    scores = mm(c_nat, b_t)
    low = jnp.where(lax.broadcasted_iota(jnp.int32, (1, 128), 1) < HDIM, 1.0, 0.0).astype(BF)
    high_half = jnp.where(lax.broadcasted_iota(jnp.int32, (1, 128), 1) < HDIM, 0.0, 1.0).astype(BF)

    def inner(head):
        at = head_rows(head)
        pair = head // 2 * 128
        gap = cum[:, head : head + 1] - cum_row[head : head + 1, :] + bias_m[...]
        decay = jnp.exp(gap)
        mixing = (scores * decay).astype(BF)
        yt[at, :] = mm(ut[at, :], mixing, NT)
        dut[at, :] = mm(gyt[at, :], mixing)
        picked = go[:, pair : pair + 128] * (low if head % 2 == 0 else high_half)
        products = mm(picked, ut[pair : pair + 128, :])
        if head == 0:
            ds_[...] = products * decay
        else:
            ds_[...] += products * decay

    for head in range(HEADS // 2):
        inner(head)

    every(lambda step: in1(step).wait_recv())
    forward = jnp.zeros((PART, STATE), F32)
    back = jnp.zeros((PART, STATE), F32)
    for source in range(SPANS):
        os_[source, 0:PART, :] = forward.astype(BF)
        decays = xr[source, 2 * PART : 2 * PART + 16, :].astype(F32)
        forward = (decays[0:1] + decays[1:2]) * forward + xr[source, 0:PART, :].astype(F32)
        later = SPANS - 1 - source
        os_[later, PART : 2 * PART, :] = back.astype(BF)
        decays = xr[later, 2 * PART : 2 * PART + 16, :].astype(F32)
        back = (decays[0:1] + decays[1:2]) * back + xr[later, PART : 2 * PART, :].astype(F32)
    every(lambda step: out2(step).start())
    or_[span] = os_[span]

    for head in range(HEADS // 2, HEADS):
        inner(head)
    ds = ds_[...].astype(BF)
    dbc[:, 0:STATE] = mm(ds, c_nat, TN)
    dbc[:, STATE : 2 * STATE] = mm(ds, b_nat)
    gap_grad, direct = [], []
    for head in range(HEADS):
        at = head_rows(head)
        x_dt = ut[at, :].astype(F32)
        gap_grad.append(
            jnp.sum(gyt[at, :].astype(F32) * yt[at, :] - x_dt * dut[at, :], axis=0, keepdims=True)
        )
    yn[...] = jnp.transpose(yt[...])
    du_here = jnp.transpose(dut[...])
    skip_all = spread(skip, spreader[...])[0:1]
    x_here = xn[...]
    given = go[...].astype(F32)
    pre[...] = (du_here * dte[...] + given * skip_all) * dstn[:, 0:XW]
    yn[...] = yn[...] + x_here * skip_all
    direct = mm(
        jnp.concatenate(split2(x_here * du_here), axis=0), spreader[0:128, :], NT
    )
    direct = direct[0:SPAN] + direct[SPAN : 2 * SPAN]
    log_rows = sums(
        jnp.concatenate(gap_grad, axis=0), jnp.where(row >= lane, 1.0, 0.0).astype(BF)
    )
    log_here = jnp.transpose(
        jnp.concatenate([log_rows, jnp.zeros((120, SPAN), F32)], axis=0)
    )
    since_before = jnp.concatenate(
        [jnp.where(row <= lane, 1.0, 0.0).astype(BF), jnp.where(row > lane, 1.0, 0.0).astype(BF)],
        axis=1,
    )

    every(lambda step: in2(step).wait_recv())

    def gathered(first):
        return jnp.concatenate(
            [
                jnp.concatenate(
                    [or_[pair * 4 + part, first : first + PART, :] for part in range(4)], axis=0
                )
                for pair in range(4)
            ],
            axis=1,
        )

    state_in = gathered(0)
    state_grad = gathered(PART)
    carried = mm(c_nat, state_in)
    reach = mm(b_nat, state_grad)
    pgn[:, 0:XW] = (pre[...] + reach * kdd[...]).astype(BF)
    db = dbc[:, 0:STATE] + mm(ku[...], state_grad, NT)
    dc = dbc[:, STATE : 2 * STATE] + mm(gw[...], state_in, NT)
    pgn[:, XW : XW + STATE] = (db * dstn[:, XW : XW + STATE]).astype(BF)
    pgn[:, XW + STATE : PROJ] = (dc * dstn[:, XW + STATE : PROJ]).astype(BF)
    ends = jnp.sum(
        (state_in.astype(F32) * state_grad.astype(F32)).reshape(STATE // 8, 8, XW), axis=0
    )
    products = jnp.concatenate(
        [
            (gw[...].astype(F32) * carried).astype(BF),
            (ku[...].astype(F32) * reach).astype(BF),
            (xk[...].astype(F32) * reach).astype(BF),
            jnp.concatenate(split2(jnp.concatenate([ends, ends], axis=0)), axis=0),
        ],
        axis=0,
    )
    reduced = mm(products, spreader[0:128, :], NT)
    far_grad = mm(
        since_before, jnp.concatenate(split2(reduced[0 : 2 * SPAN]), axis=1)
    )
    far_grad = far_grad[:, 0:128] + far_grad[:, 128:256]
    end_grad = reduced[3 * SPAN : 3 * SPAN + 8] + reduced[3 * SPAN + 16 : 3 * SPAN + 24]
    end_grad = jnp.sum(end_grad, axis=0, keepdims=True)
    log_grad = log_here + far_grad + total[0:1] * end_grad
    dt_grad = (direct + reduced[2 * SPAN : 3 * SPAN] + rate[0:1] * log_grad) * dt_gate
    pgn[:, PROJ:WIDE] = dt_grad.astype(BF)
    yn[...] = yn[...] + carried * crw[...]

    for step in range(4):
        for unit in up_units[step]:
            to_up(step, *unit).wait_send()
        for unit in down_units[step]:
            to_down(step, *unit).wait_send()
    for place in range(PLANES):
        for unit in twin_units.get(place, halves):
            to_twin(place, *unit).wait_send()
    own, sbs = xb.at[0:128, :], xb.at[128:256, :]
    for place in range(PLANES):
        for half in range(2):
            slot = SLOT[place]
            if slot == 7:
                at = half * 16
            elif slot >= 5:
                at = 32 + half * 32 + (slot - 5) * 16
            else:
                at = 96 + half * 80 + slot * 16
            pga[at : at + 16, :] = pgn[home(place, half), :]

    def multiply(quarter, begin, first, last):
        count = last - first
        rows = pga[begin : begin + 2 * count, :]
        term = mm(rows, wt[:, cols(quarter)]).astype(BF)
        own[first:last, cols(quarter)] = term[0:count]
        sbs[first:last, cols(quarter)] = term[count : 2 * count]

    def multiply_far(quarter):
        multiply(quarter, 0, 112, 128)
        swap_far(quarter).start()

    def multiply_next(quarter):
        multiply(quarter, 32, 80, 112)
        swap_next(quarter).start()

    def multiply_rest(quarter):
        multiply(quarter, 96, 0, 80)
        swap_rest(quarter).start()

    def swap(quarter, first, last, sems):
        return pltpu.make_async_remote_copy(
            src_ref=sbs.at[first:last, cols(quarter)], dst_ref=sbr.at[first:last, cols(quarter)],
            send_sem=sems[0].at[quarter], recv_sem=sems[1].at[quarter],
            device_id={"tensor": twin}, device_id_type=MESH,
        )

    def swap_far(quarter):
        return swap(quarter, 112, 128, (bf_s, bf_r))

    def swap_next(quarter):
        return swap(quarter, 80, 112, (bn_s, bn_r))

    def swap_rest(quarter):
        return swap(quarter, 0, 80, (bb_s, bb_r))

    def place_rows(place):
        return pl.ds(SLOT[place % PLANES] * 16, 16)

    def pass_up(step, quarter, count):
        return pltpu.make_async_remote_copy(
            src_ref=own.at[place_rows(4 - step), cols(quarter, count)], dst_ref=ru_r.at[step, :, cols(quarter, count)],
            send_sem=bu_s.at[step, quarter], recv_sem=bu_r.at[step, quarter],
            device_id={"tensor": up}, device_id_type=MESH,
        )

    def pass_down(step, quarter, count):
        return pltpu.make_async_remote_copy(
            src_ref=own.at[place_rows(4 + step), cols(quarter, count)], dst_ref=rd_r.at[step, :, cols(quarter, count)],
            send_sem=bd_s.at[step, quarter], recv_sem=bd_r.at[step, quarter],
            device_id={"tensor": down}, device_id_type=MESH,
        )

    def pair_sum(place, quarter, count):
        at = place_rows(place)
        where = cols(quarter, count)
        return own[at, where].astype(F32) + sbr[at, where].astype(F32)

    def go_up(step, quarter):
        value = pair_sum(4 - step, quarter, 1)
        if step > 1 or (step == 1 and quarter < 2):
            pass_up(step - 1, quarter, 1).wait_recv()
            value = value + ru_r[step - 1, :, cols(quarter)].astype(F32)
        own[place_rows(4 - step), cols(quarter)] = value.astype(BF)
        pass_up(step, quarter, 1).start()

    def go_down(step, quarter):
        value = pair_sum(4 + step, quarter, 1)
        if step > 1 or (step == 1 and quarter >= 2):
            pass_down(step - 1, quarter, 1).wait_recv()
            value = value + rd_r[step - 1, :, cols(quarter)].astype(F32)
        own[place_rows(4 + step), cols(quarter)] = value.astype(BF)
        pass_down(step, quarter, 1).start()

    def first_pass(quarter):
        swap_far(quarter).wait_recv()
        (go_up if quarter < 2 else go_down)(0, quarter)

    for quarter in (0, 2, 1, 3):
        multiply_far(quarter)
    for quarter, ready in ((2, 0), (0, 2), (3, 1), (1, 3)):
        multiply_next(quarter)
        first_pass(ready)
    up_order, down_order = (2, 3, 0, 1), (0, 1, 2, 3)
    seen = set()
    for step in (1, 2, 3):
        for up_quarter, down_quarter in zip(up_order, down_order):
            for quarter in (up_quarter, down_quarter):
                if step == 1 and quarter not in seen:
                    swap_next(quarter).wait_recv()
                    seen.add(quarter)
            go_up(step, up_quarter)
            go_down(step, down_quarter)
            if step == 1:
                multiply_rest(up_quarter)
        if step == 1:
            for quarter in range(4):
                swap_rest(quarter).wait_recv()
            y_out[...] = yn[...].astype(BF)

    for up_quarter, down_quarter in zip(up_order, down_order):
        pass_up(3, up_quarter, 1).wait_recv()
        pass_down(3, down_quarter, 1).wait_recv()
        if up_quarter < 2:
            for quarter in (up_quarter, down_quarter):
                value = pair_sum(0, quarter, 1)
                value = value + ru_r[3, :, cols(quarter)].astype(F32)
                value = value + rd_r[3, :, cols(quarter)].astype(F32)
                gh_out[:, cols(quarter)] = value.astype(BF)

    for quarter in range(4):
        swap_far(quarter).wait_send()
        swap_next(quarter).wait_send()
        swap_rest(quarter).wait_send()
    for step in range(4):
        for unit in quarters[:2] if step == 0 else quarters:
            pass_up(step, *unit).wait_send()
        for unit in quarters[2:] if step == 0 else quarters:
            pass_down(step, *unit).wait_send()
    every(lambda step: out1(step).wait_send())
    every(lambda step: out2(step).wait_send())


def place_results(y_in, gh_in, y_out, gh_out, sems):
    y_copy = pltpu.make_async_copy(y_in, y_out, sems.at[0])
    gh_copy = pltpu.make_async_copy(gh_in, gh_out, sems.at[1])
    gh_copy.start()
    y_copy.start()
    gh_copy.wait()
    y_copy.wait()


def per_device(hidden, w_proj, w_dt, dt_bias, a_log, d_skip, doc_lengths, grad_out):
    vmem = pl.BlockSpec(memory_space=pltpu.VMEM)
    smem = pl.BlockSpec(memory_space=pltpu.SMEM)
    dma = pltpu.SemaphoreType.DMA
    whole = pl.BlockSpec(memory_space=pl.ANY)
    results = pl.pallas_call(
        kernel,
        out_shape=(
            pltpu.VMEM((SPAN, XW), BF),
            pltpu.VMEM((ROWS, FEAT), BF),
        ),
        in_specs=[vmem, whole, vmem, smem, smem, smem, smem, vmem],
        out_specs=(vmem, vmem),
        scratch_shapes=[
            pltpu.VMEM((FEAT, WIDE), BF),
            pltpu.VMEM((WIDE, FEAT), BF),
            pltpu.VMEM((SPAN, FEAT), BF),
            pltpu.VMEM((SPAN, WIDE), F32),
            pltpu.VMEM((SPAN, SPAN), F32),
            pltpu.VMEM((2, SPAN, 128), F32),
            pltpu.VMEM((256, XW), BF),
            pltpu.VMEM((XW, SPAN), BF),
            pltpu.VMEM((SPAN, PROJ), F32),
            pltpu.VMEM((SPAN, 128), F32),
            pltpu.VMEM((SPAN, XW), F32),
            pltpu.VMEM((SPAN, PROJ), F32),
            pltpu.VMEM((SPAN, 2 * STATE), BF),
            pltpu.VMEM((SPAN, XW), F32),
            pltpu.VMEM((SPAN, XW), F32),
            pltpu.VMEM((SPAN, XW), F32),
            pltpu.VMEM((SPAN, XW), BF),
            pltpu.VMEM((SPAN, XW), BF),
            pltpu.VMEM((SPAN, XW), BF),
            pltpu.VMEM((XW, SPAN), BF),
            pltpu.VMEM((XW, SPAN), F32),
            pltpu.VMEM((XW, SPAN), F32),
            pltpu.VMEM((SPAN, SPAN), F32),
            pltpu.VMEM((SPAN, XW), F32),
            pltpu.VMEM((SPAN, XW), F32),
            pltpu.VMEM((SPAN, 2 * STATE), F32),
            pltpu.VMEM((SPANS, 2 * PART + 16, STATE), BF),
            pltpu.VMEM((SPANS, 2 * PART + 16, STATE), BF),
            pltpu.VMEM((SPANS, 2 * PART, STATE), BF),
            pltpu.VMEM((SPANS, 2 * PART, STATE), BF),
            pltpu.VMEM((SPAN, WIDE), BF),
            pltpu.VMEM((SPAN, WIDE), BF),
            pltpu.VMEM((128, FEAT), BF),
            pltpu.VMEM((4, ROWS, FEAT), BF),
            pltpu.VMEM((4, ROWS, FEAT), BF),
            dma,
            dma((4, 4)), dma((4, 4)), dma((4, 4)), dma((4, 4)),
            dma((PLANES, 4)), dma((PLANES, 4)),
            dma((SPANS,)), dma((SPANS,)), dma((SPANS,)), dma((SPANS,)),
            dma((4, 4)), dma((4, 4)), dma((4, 4)), dma((4, 4)),
            dma((4,)), dma((4,)), dma((4,)), dma((4,)), dma((4,)), dma((4,)),
            pltpu.SemaphoreType.REGULAR((3,)),
        ],
        compiler_params=pltpu.CompilerParams(
            collective_id=0, has_side_effects=True, vmem_limit_bytes=58 * 1024 * 1024
        ),
        name="layer",
    )(hidden, w_proj, w_dt, dt_bias, a_log, d_skip, doc_lengths, grad_out)
    return pl.pallas_call(
        place_results,
        out_shape=(
            jax.ShapeDtypeStruct((SPAN, XW), BF),
            jax.ShapeDtypeStruct((ROWS, FEAT), BF),
        ),
        in_specs=[vmem, vmem],
        out_specs=(whole, whole),
        scratch_shapes=[dma((2,))],
        name="place_results",
    )(*(pltpu.with_memory_space_constraint(part, pltpu.VMEM) for part in results))


def solution(mesh):
    placed = (
        P(("context", "tensor"), None),
        P(None, "tensor"),
        P("tensor", None),
        P("tensor"),
        P("tensor"),
        P("tensor"),
        P(),
        P("context", "tensor"),
    )
    return jax.shard_map(
        per_device,
        mesh=mesh,
        in_specs=placed,
        out_specs=(P("context", "tensor"), P(("context", "tensor"), None)),
        check_vma=False,
    )
```

```python
import jax
import jax.numpy as jnp
from jax import lax
from jax.experimental import pallas as pl
from jax.experimental.pallas import tpu as pltpu
from jax.sharding import PartitionSpec as P

BF = jnp.bfloat16
F32 = jnp.float32
MESH = pl.DeviceIdType.MESH

PLANES = 8
SPANS = 16
ROWS = 16
SPAN = 256
FEAT = 8192
HEADS = 8
HDIM = 64
XW = HEADS * HDIM
STATE = 128
PROJ = XW + 2 * STATE
WIDE = PROJ + 128
QUARTER = FEAT // 4
PART = XW // SPANS
SLOT = {0: 0, 1: 1, 7: 2, 2: 3, 6: 4, 3: 5, 5: 6, 4: 7}
NEAR = 5 * 32

NN = (((1,), (0,)), ((), ()))
NT = (((1,), (1,)), ((), ()))
TN = (((0,), (0,)), ((), ()))


def mm(a, b, dims=NN):
    return lax.dot_general(a, b, dims, preferred_element_type=F32)


def cols(quarter, count=1):
    return pl.ds(quarter * QUARTER, count * QUARTER)


def quantize(rows):
    lane = lax.broadcasted_iota(jnp.int32, rows.shape, 1)
    largest = jnp.abs(rows)
    for step in (1, 2, 4, 8, 16):
        below = pltpu.roll(largest, step, 1)
        above = pltpu.roll(largest, 128 - step, 1)
        largest = jnp.maximum(largest, jnp.where((lane & step) != 0, below, above))
    power = jnp.exp2(jnp.floor(jnp.log2(jnp.maximum(largest, 2.0**-39)))).astype(BF).astype(F32)
    power = jnp.where(power > largest, power * 0.5, power)
    power = jnp.where(power * 2.0 <= largest, power * 2.0, power)
    scale = jnp.where(largest >= 2.0**-39, power * 2.0**-8, 2.0**-48)
    lifted = rows * 2.0**20
    normal = (rows + lifted) - lifted
    anchor = scale * (1.5 * 2.0**14)
    small = (rows + anchor) - anchor
    snapped = jnp.where(jnp.abs(rows) < scale * 2.0**-6, small, normal)
    bound = scale * 448.0
    return jnp.clip(snapped, -bound, bound)


def split3(values):
    first = values.astype(BF)
    rest = values - first.astype(F32)
    second = rest.astype(BF)
    third = (rest - second.astype(F32)).astype(BF)
    return first, second, third


def sums(values, chosen):
    first, second, third = split3(values)
    stacked = jnp.concatenate(
        [first.astype(F32), second.astype(F32), third.astype(F32), jnp.zeros_like(values)], axis=0
    ).astype(BF)
    out = mm(stacked, chosen)
    return out[0:8] + out[8:16] + out[16:24]


def head_lanes(scalars):
    lane = lax.broadcasted_iota(jnp.int32, (8, 128), 1)
    out = jnp.zeros((8, 128), F32)
    for head in range(HEADS):
        out = jnp.where(lane == head, scalars[head], out)
    return out


def split2(values):
    high = values.astype(BF)
    return high, (values - high.astype(F32)).astype(BF)


def spread(values, spreader):
    return mm(jnp.concatenate(split2(values), axis=1), spreader)


def head_rows(head):
    return pl.ds(head * HDIM, HDIM)


def kernel(
    hid_hbm, w_hbm, wdt_hbm, bias_hbm, alog_hbm, skip_hbm, docs_hbm, go_hbm,
    y_out, gh_out,
    hid, wdt_ref, go, bias_ref, alog_ref, skip_ref, docs, in_sems,
    w, wt, xb, acc, bias_m, masks, spreader, gyt, pn, dn_, xn, dstn, bc, dte, kdd, crw, xk, ku, gw,
    ut, yt, dut, ds_, yn, pre, dbc, xs, xr, os_, or_, pgn, pga, sbr, ru_r, rd_r,
    wsem, au_s, au_r, ad_s, ad_r, ab_s, ab_r, x1s, x1r, x2s, x2r,
    bu_s, bu_r, bd_s, bd_r, bb_s, bb_r, bf_s, bf_r, bn_s, bn_r, heard,
):
    me = lax.axis_index("tensor")
    span = lax.axis_index("context")
    z = me // 2
    core = me % 2
    up = lax.rem(z + 1, PLANES) * 2 + core
    down = lax.rem(z + PLANES - 1, PLANES) * 2 + core
    twin = z * 2 + (1 - core)

    hid_copy = pltpu.make_async_copy(hid_hbm, hid, in_sems.at[0])
    hid_copy.start()

    barrier = pltpu.get_barrier_semaphore()
    for near in (up, down, twin):
        pl.semaphore_signal(barrier, inc=1, device_id={"tensor": near}, device_id_type=MESH)

    x, y = span % 4, span // 4
    beside = (y * 4 + lax.rem(x + 1, 4), y * 4 + lax.rem(x + 3, 4))
    across = (lax.rem(y + 1, 4) * 4 + x, lax.rem(y + 3, 4) * 4 + x)
    for near in beside + across:
        pl.semaphore_signal(barrier, inc=1, device_id={"context": near}, device_id_type=MESH)

    def tell(whom, sem):
        for near in whom:
            pl.semaphore_signal(sem, inc=1, device_id={"context": near}, device_id_type=MESH)

    def block(place, half, quarter, count):
        return xb.at[pl.ds(SLOT[place % PLANES] * 32 + half * 16, ROWS), cols(quarter, count)]

    def to_up(step, quarter, count):
        return pltpu.make_async_remote_copy(
            src_ref=block(-step, 0, quarter, count), dst_ref=block(-step - 1, 0, quarter, count),
            send_sem=au_s.at[step, quarter], recv_sem=au_r.at[step, quarter],
            device_id={"tensor": up}, device_id_type=MESH,
        )

    def to_down(step, quarter, count):
        return pltpu.make_async_remote_copy(
            src_ref=block(step, 0, quarter, count), dst_ref=block(step + 1, 0, quarter, count),
            send_sem=ad_s.at[step, quarter], recv_sem=ad_r.at[step, quarter],
            device_id={"tensor": down}, device_id_type=MESH,
        )

    def to_twin(place, quarter, count):
        place = place % PLANES
        return pltpu.make_async_remote_copy(
            src_ref=block(place, 0, quarter, count), dst_ref=block(place, 1, quarter, count),
            send_sem=ab_s.at[place, quarter], recv_sem=ab_r.at[place, quarter],
            device_id={"tensor": twin}, device_id_type=MESH,
        )

    quarters = ((0, 1), (1, 1), (2, 1), (3, 1))
    halves = ((0, 2), (2, 2))
    up_units = (quarters, halves, halves, quarters[:2])
    down_units = (quarters[2:] + quarters[:2], halves[::-1], halves[::-1], quarters[2:])
    twin_units = {0: ((0, 4),), 4: quarters}

    tiles = QUARTER // 128

    def encode(quarter):
        part = hid[:, quarter * QUARTER : (quarter + 1) * QUARTER].astype(F32)
        stacked = jnp.concatenate(
            [part[:, i * 128 : (i + 1) * 128] for i in range(tiles)], axis=0
        )
        snapped = quantize(stacked)
        flat = jnp.concatenate(
            [snapped[i * ROWS : (i + 1) * ROWS] for i in range(tiles)], axis=1
        )
        xb[0:ROWS, quarter * QUARTER : (quarter + 1) * QUARTER] = flat.astype(BF)

    later_copies = [
        pltpu.make_async_copy(source, target, in_sems.at[1 + at])
        for at, (source, target) in enumerate(
            (
                (docs_hbm, docs),
                (wdt_hbm, wdt_ref),
                (go_hbm, go),
                (bias_hbm, bias_ref),
                (alog_hbm, alog_ref),
                (skip_hbm, skip_ref),
            )
        )
    ]
    for copy in later_copies:
        copy.start()
    w_copy = pltpu.make_async_copy(w_hbm, w.at[:, 0:PROJ], wsem)
    w_copy.start()
    hid_copy.wait()
    encode(0)
    pl.semaphore_wait(barrier, 7)
    to_up(0, 0, 1).start()
    encode(2)
    to_down(0, 2, 1).start()
    encode(1)
    to_up(0, 1, 1).start()
    encode(3)
    to_down(0, 3, 1).start()
    to_up(0, 2, 1).start()
    to_down(0, 0, 1).start()
    to_up(0, 3, 1).start()
    to_down(0, 1, 1).start()
    to_twin(0, 0, 4).start()
    tell(beside, heard.at[0])

    for copy in later_copies:
        copy.wait()
    first_token = span * SPAN

    def segment(positions):
        out = jnp.full(positions.shape, -1, jnp.int32)
        begin = jnp.int32(0)
        for doc in range(8):
            out = out + jnp.where(positions >= begin, 1, 0)
            begin = begin + docs[doc]
        return out

    row_pos = first_token + lax.broadcasted_iota(jnp.int32, (SPAN, SPAN), 0)
    col_pos = first_token + lax.broadcasted_iota(jnp.int32, (SPAN, SPAN), 1)
    bias_m[...] = jnp.where(
        (row_pos >= col_pos) & (segment(row_pos) == segment(col_pos)), 0.0, -1e30
    )
    token = first_token + lax.broadcasted_iota(jnp.int32, (SPAN, 128), 0)
    seg = segment(token)
    none = jnp.zeros((8, 128), jnp.int32)
    seg_before = segment(none + (first_token - 1))
    seg_last = segment(none + (first_token + SPAN - 1))
    masks[0] = jnp.where(seg == seg_before[0:1], 1.0, 0.0)
    masks[1] = jnp.where(seg == seg_last[0:1], 1.0, 0.0)
    through = jnp.where(seg_last == seg_before, 1.0, 0.0)
    head_of_row = lax.rem(lax.broadcasted_iota(jnp.int32, (256, XW), 0), 128)
    head_of_lane = lax.broadcasted_iota(jnp.int32, (256, XW), 1) // HDIM
    spreader[...] = jnp.where(head_of_row == head_of_lane, 1.0, 0.0).astype(BF)
    gyt[...] = jnp.transpose(go[...].astype(F32)).astype(BF)

    for quarter in range(4):
        steps_w = wdt_ref[:, quarter * QUARTER : (quarter + 1) * QUARTER].astype(F32)
        padded = jnp.concatenate([steps_w, jnp.zeros((120, QUARTER), F32)], axis=0)
        w[cols(quarter), PROJ:WIDE] = jnp.transpose(padded).astype(BF)
        wt[PROJ:WIDE, cols(quarter)] = padded.astype(BF)
    square_row = lax.broadcasted_iota(jnp.int32, (256, 256), 0)
    square_lane = lax.broadcasted_iota(jnp.int32, (256, 256), 1)
    same = jnp.where(square_row == square_lane, 1.0, 0.0).astype(BF)
    units = [(quarter, first) for quarter in (0, 2, 1, 3) for first in range(0, PROJ, 256)]

    def turn_weights(count):
        for _ in range(count):
            quarter, first = units.pop(0)
            at = slice(first, first + 256)
            wt[at, cols(quarter)] = mm(same, w[cols(quarter), at], NT).astype(BF)

    def project(first, last, quarter, begin):
        at = slice(quarter * QUARTER, (quarter + 1) * QUARTER)
        part = mm(xb[first:last, at], w[at, :])
        if begin:
            acc[first:last, :] = part
        else:
            acc[first:last, :] += part

    def arrived_twin(place):
        for unit in twin_units.get(place, halves):
            to_twin(place, *unit).wait_recv()

    def between(step, turn):
        if (step, turn) == (0, 0):
            pl.semaphore_wait(heard.at[0], 2)
            tell(across, heard.at[1])
            w_copy.wait()
            turn_weights(3)
        elif (step, turn) == (0, 1):
            pl.semaphore_wait(heard.at[1], 2)
            tell(across, heard.at[2])
            turn_weights(3)
        elif (step, turn) == (1, 0):
            pl.semaphore_wait(heard.at[2], 2)
            turn_weights(4)
        elif (step, turn) == (1, 1):
            turn_weights(2)
            for place in (0, 1, 7, 2, 6):
                arrived_twin(place)
            project(0, NEAR, 0, True)
            project(0, NEAR, 1, False)
        elif (step, turn) == (2, 0):
            project(0, NEAR, 2, False)
            project(0, NEAR, 3, False)

    for step in range(3):
        for turn in range(2):
            unit = halves[turn]
            for got in quarters[2 * turn : 2 * turn + 2] if step == 0 else (unit,):
                to_up(step, *got).wait_recv()
            if step < 2:
                to_up(step + 1, *unit).start()
            elif turn == 0:
                for part in up_units[3]:
                    to_up(3, *part).start()
            to_twin(-step - 1, *unit).start()
            unit = halves[1 - turn]
            for got in quarters[2 - 2 * turn : 4 - 2 * turn] if step == 0 else (unit,):
                to_down(step, *got).wait_recv()
            if step < 2:
                to_down(step + 1, *unit).start()
            elif turn == 0:
                for part in down_units[3]:
                    to_down(3, *part).start()
            to_twin(step + 1, *unit).start()
            between(step, turn)
    for at in range(2):
        to_up(3, *up_units[3][at]).wait_recv()
        to_twin(4, *up_units[3][at]).start()
        to_down(3, *down_units[3][at]).wait_recv()
        to_twin(4, *down_units[3][at]).start()
    arrived_twin(3)
    arrived_twin(5)
    for quarter in (0, 2, 1, 3):
        to_twin(4, quarter, 1).wait_recv()
        project(NEAR, SPAN, quarter, quarter == 0)

    def home(place, half):
        owner = lax.rem(z + place, PLANES) * 2 + (core if half == 0 else 1 - core)
        return pl.ds(pl.multiple_of(owner * ROWS, ROWS), ROWS)

    for place in range(PLANES):
        for half in range(2):
            at = SLOT[place] * 32 + half * 16
            pn[home(place, half), :] = acc[at : at + 16, 0:PROJ].astype(BF).astype(F32)
            dn_[home(place, half), :] = acc[at : at + 16, PROJ:WIDE]

    row = lax.broadcasted_iota(jnp.int32, (SPAN, SPAN), 0)
    lane = lax.broadcasted_iota(jnp.int32, (SPAN, SPAN), 1)
    rate = -jnp.exp(head_lanes(alog_ref))
    skip = head_lanes(skip_ref)
    dt_arg = dn_[...] + head_lanes(bias_ref)[0:1]
    dt = jnp.maximum(dt_arg, 0.0) + jnp.log1p(jnp.exp(-jnp.abs(dt_arg)))
    dt_gate = 1.0 / (1.0 + jnp.exp(-dt_arg))
    summed = mm(
        jnp.where(row >= lane, 1.0, 0.0).astype(BF),
        jnp.concatenate(split3(dt * rate[0:1]), axis=1),
    )
    cum = summed[:, 0:128] + summed[:, 128:256] + summed[:, 256:384]
    cum_last = cum[SPAN - 1 : SPAN]
    carry_w = jnp.exp(cum) * masks[0]
    keep_w = jnp.exp(cum_last - cum) * masks[1]
    total = jnp.exp(jnp.broadcast_to(cum_last, (8, 128))) * through
    keep_dt = spread(keep_w * dt, spreader[...])
    crw[...] = spread(carry_w, spreader[...])
    projected = pn[...]
    gate = 1.0 / (1.0 + jnp.exp(-projected))
    dstn[...] = gate * (1.0 + projected * (1.0 - gate))
    active = projected * gate
    xn[...] = active[:, 0:XW]
    bc[...] = active[:, XW:PROJ].astype(BF)
    b_nat = bc[:, 0:STATE]
    c_nat = bc[:, STATE : 2 * STATE]
    b_t = jnp.transpose(active[:, XW : XW + STATE]).astype(BF)
    c_t = jnp.transpose(active[:, XW + STATE : PROJ]).astype(BF)
    ku[...] = (xn[...] * keep_dt).astype(BF)
    gw[...] = (go[...].astype(F32) * crw[...]).astype(BF)
    end_state = mm(b_t, ku[...]).astype(BF)
    from_out = mm(c_t, gw[...]).astype(BF)
    note_row = lax.broadcasted_iota(jnp.int32, (16, 128), 0)
    high, low_part = split2(total[0:1])
    note = jnp.where(note_row == 0, high.astype(F32), jnp.where(note_row == 1, low_part.astype(F32), 0.0))
    note = mm(note.astype(BF), spreader[0:128, :]).astype(BF)
    for part in range(SPANS):
        at = slice(part % 4 * PART, part % 4 * PART + PART)
        pair = slice(part // 4 * 128, part // 4 * 128 + 128)
        xs[part, 0:PART, :] = end_state[at, pair]
        xs[part, PART : 2 * PART, :] = from_out[at, pair]
        xs[part, 2 * PART : 2 * PART + 16, :] = note[:, pair]

    def other(step):
        return lax.rem(span + step, SPANS)

    def out1(step):
        return pltpu.make_async_remote_copy(
            src_ref=xs.at[other(step)], dst_ref=xr.at[span],
            send_sem=x1s.at[other(step)], recv_sem=x1r.at[span],
            device_id={"context": other(step)}, device_id_type=MESH,
        )

    def in1(step):
        return pltpu.make_async_remote_copy(
            src_ref=xs.at[other(step)], dst_ref=xr.at[other(step)],
            send_sem=x1s.at[other(step)], recv_sem=x1r.at[other(step)],
            device_id={"context": other(step)}, device_id_type=MESH,
        )

    def out2(step):
        return pltpu.make_async_remote_copy(
            src_ref=os_.at[other(step)], dst_ref=or_.at[span],
            send_sem=x2s.at[other(step)], recv_sem=x2r.at[span],
            device_id={"context": other(step)}, device_id_type=MESH,
        )

    def in2(step):
        return pltpu.make_async_remote_copy(
            src_ref=os_.at[other(step)], dst_ref=or_.at[other(step)],
            send_sem=x2s.at[other(step)], recv_sem=x2r.at[other(step)],
            device_id={"context": other(step)}, device_id_type=MESH,
        )

    def every(action):
        for step in (10, 9, 11, 6, 14, 8, 2, 5, 7, 13, 15, 4, 12, 1, 3):
            action(step)

    every(lambda step: out1(step).start())
    xr[span] = xs[span]

    dte[...] = spread(dt, spreader[...])
    xk[...] = (xn[...] * spread(keep_w, spreader[...])).astype(BF)
    kdd[...] = keep_dt * dstn[:, 0:XW]
    ut[...] = jnp.transpose(xn[...] * dte[...]).astype(BF)
    cum_row = jnp.transpose(cum)
    scores = mm(c_nat, b_t)
    low = jnp.where(lax.broadcasted_iota(jnp.int32, (1, 128), 1) < HDIM, 1.0, 0.0).astype(BF)
    high_half = jnp.where(lax.broadcasted_iota(jnp.int32, (1, 128), 1) < HDIM, 0.0, 1.0).astype(BF)

    def inner(head):
        at = head_rows(head)
        pair = head // 2 * 128
        gap = cum[:, head : head + 1] - cum_row[head : head + 1, :] + bias_m[...]
        decay = jnp.exp(gap)
        mixing = (scores * decay).astype(BF)
        yt[at, :] = mm(ut[at, :], mixing, NT)
        dut[at, :] = mm(gyt[at, :], mixing)
        picked = go[:, pair : pair + 128] * (low if head % 2 == 0 else high_half)
        products = mm(picked, ut[pair : pair + 128, :])
        if head == 0:
            ds_[...] = products * decay
        else:
            ds_[...] += products * decay

    for head in range(HEADS // 2):
        inner(head)

    every(lambda step: in1(step).wait_recv())
    forward = jnp.zeros((PART, STATE), F32)
    back = jnp.zeros((PART, STATE), F32)
    for source in range(SPANS):
        os_[source, 0:PART, :] = forward.astype(BF)
        decays = xr[source, 2 * PART : 2 * PART + 16, :].astype(F32)
        forward = (decays[0:1] + decays[1:2]) * forward + xr[source, 0:PART, :].astype(F32)
        later = SPANS - 1 - source
        os_[later, PART : 2 * PART, :] = back.astype(BF)
        decays = xr[later, 2 * PART : 2 * PART + 16, :].astype(F32)
        back = (decays[0:1] + decays[1:2]) * back + xr[later, PART : 2 * PART, :].astype(F32)
    every(lambda step: out2(step).start())
    or_[span] = os_[span]

    for head in range(HEADS // 2, HEADS):
        inner(head)
    ds = ds_[...].astype(BF)
    dbc[:, 0:STATE] = mm(ds, c_nat, TN)
    dbc[:, STATE : 2 * STATE] = mm(ds, b_nat)
    gap_grad, direct = [], []
    for head in range(HEADS):
        at = head_rows(head)
        x_dt = ut[at, :].astype(F32)
        gap_grad.append(
            jnp.sum(gyt[at, :].astype(F32) * yt[at, :] - x_dt * dut[at, :], axis=0, keepdims=True)
        )
    yn[...] = jnp.transpose(yt[...])
    du_here = jnp.transpose(dut[...])
    skip_all = spread(skip, spreader[...])[0:1]
    x_here = xn[...]
    given = go[...].astype(F32)
    pre[...] = (du_here * dte[...] + given * skip_all) * dstn[:, 0:XW]
    yn[...] = yn[...] + x_here * skip_all
    direct = mm(
        jnp.concatenate(split2(x_here * du_here), axis=0), spreader[0:128, :], NT
    )
    direct = direct[0:SPAN] + direct[SPAN : 2 * SPAN]
    log_rows = sums(
        jnp.concatenate(gap_grad, axis=0), jnp.where(row >= lane, 1.0, 0.0).astype(BF)
    )
    log_here = jnp.transpose(
        jnp.concatenate([log_rows, jnp.zeros((120, SPAN), F32)], axis=0)
    )
    since_before = jnp.concatenate(
        [jnp.where(row <= lane, 1.0, 0.0).astype(BF), jnp.where(row > lane, 1.0, 0.0).astype(BF)],
        axis=1,
    )

    every(lambda step: in2(step).wait_recv())

    def gathered(first):
        return jnp.concatenate(
            [
                jnp.concatenate(
                    [or_[pair * 4 + part, first : first + PART, :] for part in range(4)], axis=0
                )
                for pair in range(4)
            ],
            axis=1,
        )

    state_in = gathered(0)
    state_grad = gathered(PART)
    carried = mm(c_nat, state_in)
    reach = mm(b_nat, state_grad)
    pgn[:, 0:XW] = (pre[...] + reach * kdd[...]).astype(BF)
    db = dbc[:, 0:STATE] + mm(ku[...], state_grad, NT)
    dc = dbc[:, STATE : 2 * STATE] + mm(gw[...], state_in, NT)
    pgn[:, XW : XW + STATE] = (db * dstn[:, XW : XW + STATE]).astype(BF)
    pgn[:, XW + STATE : PROJ] = (dc * dstn[:, XW + STATE : PROJ]).astype(BF)
    ends = jnp.sum(
        (state_in.astype(F32) * state_grad.astype(F32)).reshape(STATE // 8, 8, XW), axis=0
    )
    products = jnp.concatenate(
        [
            (gw[...].astype(F32) * carried).astype(BF),
            (ku[...].astype(F32) * reach).astype(BF),
            (xk[...].astype(F32) * reach).astype(BF),
            jnp.concatenate(split2(jnp.concatenate([ends, ends], axis=0)), axis=0),
        ],
        axis=0,
    )
    reduced = mm(products, spreader[0:128, :], NT)
    far_grad = mm(
        since_before, jnp.concatenate(split2(reduced[0 : 2 * SPAN]), axis=1)
    )
    far_grad = far_grad[:, 0:128] + far_grad[:, 128:256]
    end_grad = reduced[3 * SPAN : 3 * SPAN + 8] + reduced[3 * SPAN + 16 : 3 * SPAN + 24]
    end_grad = jnp.sum(end_grad, axis=0, keepdims=True)
    log_grad = log_here + far_grad + total[0:1] * end_grad
    dt_grad = (direct + reduced[2 * SPAN : 3 * SPAN] + rate[0:1] * log_grad) * dt_gate
    pgn[:, PROJ:WIDE] = dt_grad.astype(BF)
    yn[...] = yn[...] + carried * crw[...]

    for step in range(4):
        for unit in up_units[step]:
            to_up(step, *unit).wait_send()
        for unit in down_units[step]:
            to_down(step, *unit).wait_send()
    for place in range(PLANES):
        for unit in twin_units.get(place, halves):
            to_twin(place, *unit).wait_send()
    own, sbs = xb.at[0:128, :], xb.at[128:256, :]
    for place in range(PLANES):
        for half in range(2):
            slot = SLOT[place]
            if slot == 7:
                at = half * 16
            elif slot >= 5:
                at = 32 + half * 32 + (slot - 5) * 16
            else:
                at = 96 + half * 80 + slot * 16
            pga[at : at + 16, :] = pgn[home(place, half), :]

    def multiply(quarter, begin, first, last):
        count = last - first
        rows = pga[begin : begin + 2 * count, :]
        term = mm(rows, wt[:, cols(quarter)]).astype(BF)
        own[first:last, cols(quarter)] = term[0:count]
        sbs[first:last, cols(quarter)] = term[count : 2 * count]

    def multiply_far(quarter):
        multiply(quarter, 0, 112, 128)
        swap_far(quarter).start()

    def multiply_next(quarter):
        multiply(quarter, 32, 80, 112)
        swap_next(quarter).start()

    def multiply_rest(quarter):
        multiply(quarter, 96, 0, 80)
        swap_rest(quarter).start()

    def swap(quarter, first, last, sems):
        return pltpu.make_async_remote_copy(
            src_ref=sbs.at[first:last, cols(quarter)], dst_ref=sbr.at[first:last, cols(quarter)],
            send_sem=sems[0].at[quarter], recv_sem=sems[1].at[quarter],
            device_id={"tensor": twin}, device_id_type=MESH,
        )

    def swap_far(quarter):
        return swap(quarter, 112, 128, (bf_s, bf_r))

    def swap_next(quarter):
        return swap(quarter, 80, 112, (bn_s, bn_r))

    def swap_rest(quarter):
        return swap(quarter, 0, 80, (bb_s, bb_r))

    def place_rows(place):
        return pl.ds(SLOT[place % PLANES] * 16, 16)

    def pass_up(step, quarter, count):
        return pltpu.make_async_remote_copy(
            src_ref=own.at[place_rows(4 - step), cols(quarter, count)], dst_ref=ru_r.at[step, :, cols(quarter, count)],
            send_sem=bu_s.at[step, quarter], recv_sem=bu_r.at[step, quarter],
            device_id={"tensor": up}, device_id_type=MESH,
        )

    def pass_down(step, quarter, count):
        return pltpu.make_async_remote_copy(
            src_ref=own.at[place_rows(4 + step), cols(quarter, count)], dst_ref=rd_r.at[step, :, cols(quarter, count)],
            send_sem=bd_s.at[step, quarter], recv_sem=bd_r.at[step, quarter],
            device_id={"tensor": down}, device_id_type=MESH,
        )

    def pair_sum(place, quarter, count):
        at = place_rows(place)
        where = cols(quarter, count)
        return own[at, where].astype(F32) + sbr[at, where].astype(F32)

    def go_up(step, quarter):
        value = pair_sum(4 - step, quarter, 1)
        if step > 1 or (step == 1 and quarter < 2):
            pass_up(step - 1, quarter, 1).wait_recv()
            value = value + ru_r[step - 1, :, cols(quarter)].astype(F32)
        own[place_rows(4 - step), cols(quarter)] = value.astype(BF)
        pass_up(step, quarter, 1).start()

    def go_down(step, quarter):
        value = pair_sum(4 + step, quarter, 1)
        if step > 1 or (step == 1 and quarter >= 2):
            pass_down(step - 1, quarter, 1).wait_recv()
            value = value + rd_r[step - 1, :, cols(quarter)].astype(F32)
        own[place_rows(4 + step), cols(quarter)] = value.astype(BF)
        pass_down(step, quarter, 1).start()

    def first_pass(quarter):
        swap_far(quarter).wait_recv()
        (go_up if quarter < 2 else go_down)(0, quarter)

    for quarter in (0, 2, 1, 3):
        multiply_far(quarter)
    for quarter, ready in ((2, 0), (0, 2), (3, 1), (1, 3)):
        multiply_next(quarter)
        first_pass(ready)
    up_order, down_order = (2, 3, 0, 1), (0, 1, 2, 3)
    seen = set()
    for step in (1, 2, 3):
        for up_quarter, down_quarter in zip(up_order, down_order):
            for quarter in (up_quarter, down_quarter):
                if step == 1 and quarter not in seen:
                    swap_next(quarter).wait_recv()
                    seen.add(quarter)
            go_up(step, up_quarter)
            go_down(step, down_quarter)
            if step == 1:
                multiply_rest(up_quarter)
        if step == 1:
            for quarter in range(4):
                swap_rest(quarter).wait_recv()
            y_out[...] = yn[...].astype(BF)

    for up_quarter, down_quarter in zip(up_order, down_order):
        pass_up(3, up_quarter, 1).wait_recv()
        pass_down(3, down_quarter, 1).wait_recv()
        if up_quarter < 2:
            for quarter in (up_quarter, down_quarter):
                value = pair_sum(0, quarter, 1)
                value = value + ru_r[3, :, cols(quarter)].astype(F32)
                value = value + rd_r[3, :, cols(quarter)].astype(F32)
                gh_out[:, cols(quarter)] = value.astype(BF)

    for quarter in range(4):
        swap_far(quarter).wait_send()
        swap_next(quarter).wait_send()
        swap_rest(quarter).wait_send()
    for step in range(4):
        for unit in quarters[:2] if step == 0 else quarters:
            pass_up(step, *unit).wait_send()
        for unit in quarters[2:] if step == 0 else quarters:
            pass_down(step, *unit).wait_send()
    every(lambda step: out1(step).wait_send())
    every(lambda step: out2(step).wait_send())


def place_results(y_in, gh_in, y_out, gh_out, sems):
    y_copy = pltpu.make_async_copy(y_in, y_out, sems.at[0])
    gh_copy = pltpu.make_async_copy(gh_in, gh_out, sems.at[1])
    gh_copy.start()
    y_copy.start()
    gh_copy.wait()
    y_copy.wait()


def per_device(hidden, w_proj, w_dt, dt_bias, a_log, d_skip, doc_lengths, grad_out):
    vmem = pl.BlockSpec(memory_space=pltpu.VMEM)
    dma = pltpu.SemaphoreType.DMA
    whole = pl.BlockSpec(memory_space=pl.ANY)
    results = pl.pallas_call(
        kernel,
        out_shape=(
            pltpu.VMEM((SPAN, XW), BF),
            pltpu.VMEM((ROWS, FEAT), BF),
        ),
        in_specs=[whole] * 8,
        out_specs=(vmem, vmem),
        scratch_shapes=[
            pltpu.VMEM((ROWS, FEAT), BF),
            pltpu.VMEM((HEADS, FEAT), BF),
            pltpu.VMEM((SPAN, XW), BF),
            pltpu.SMEM((HEADS,), F32),
            pltpu.SMEM((HEADS,), F32),
            pltpu.SMEM((HEADS,), F32),
            pltpu.SMEM((8,), jnp.int32),
            dma((7,)),
            pltpu.VMEM((FEAT, WIDE), BF),
            pltpu.VMEM((WIDE, FEAT), BF),
            pltpu.VMEM((SPAN, FEAT), BF),
            pltpu.VMEM((SPAN, WIDE), F32),
            pltpu.VMEM((SPAN, SPAN), F32),
            pltpu.VMEM((2, SPAN, 128), F32),
            pltpu.VMEM((256, XW), BF),
            pltpu.VMEM((XW, SPAN), BF),
            pltpu.VMEM((SPAN, PROJ), F32),
            pltpu.VMEM((SPAN, 128), F32),
            pltpu.VMEM((SPAN, XW), F32),
            pltpu.VMEM((SPAN, PROJ), F32),
            pltpu.VMEM((SPAN, 2 * STATE), BF),
            pltpu.VMEM((SPAN, XW), F32),
            pltpu.VMEM((SPAN, XW), F32),
            pltpu.VMEM((SPAN, XW), F32),
            pltpu.VMEM((SPAN, XW), BF),
            pltpu.VMEM((SPAN, XW), BF),
            pltpu.VMEM((SPAN, XW), BF),
            pltpu.VMEM((XW, SPAN), BF),
            pltpu.VMEM((XW, SPAN), F32),
            pltpu.VMEM((XW, SPAN), F32),
            pltpu.VMEM((SPAN, SPAN), F32),
            pltpu.VMEM((SPAN, XW), F32),
            pltpu.VMEM((SPAN, XW), F32),
            pltpu.VMEM((SPAN, 2 * STATE), F32),
            pltpu.VMEM((SPANS, 2 * PART + 16, STATE), BF),
            pltpu.VMEM((SPANS, 2 * PART + 16, STATE), BF),
            pltpu.VMEM((SPANS, 2 * PART, STATE), BF),
            pltpu.VMEM((SPANS, 2 * PART, STATE), BF),
            pltpu.VMEM((SPAN, WIDE), BF),
            pltpu.VMEM((SPAN, WIDE), BF),
            pltpu.VMEM((128, FEAT), BF),
            pltpu.VMEM((4, ROWS, FEAT), BF),
            pltpu.VMEM((4, ROWS, FEAT), BF),
            dma,
            dma((4, 4)), dma((4, 4)), dma((4, 4)), dma((4, 4)),
            dma((PLANES, 4)), dma((PLANES, 4)),
            dma((SPANS,)), dma((SPANS,)), dma((SPANS,)), dma((SPANS,)),
            dma((4, 4)), dma((4, 4)), dma((4, 4)), dma((4, 4)),
            dma((4,)), dma((4,)), dma((4,)), dma((4,)), dma((4,)), dma((4,)),
            pltpu.SemaphoreType.REGULAR((3,)),
        ],
        compiler_params=pltpu.CompilerParams(
            collective_id=0, has_side_effects=True, vmem_limit_bytes=58 * 1024 * 1024
        ),
        name="layer",
    )(hidden, w_proj, w_dt, dt_bias, a_log, d_skip, doc_lengths, grad_out)
    return pl.pallas_call(
        place_results,
        out_shape=(
            jax.ShapeDtypeStruct((SPAN, XW), BF),
            jax.ShapeDtypeStruct((ROWS, FEAT), BF),
        ),
        in_specs=[vmem, vmem],
        out_specs=(whole, whole),
        scratch_shapes=[dma((2,))],
        name="place_results",
    )(*(pltpu.with_memory_space_constraint(part, pltpu.VMEM) for part in results))


def solution(mesh):
    placed = (
        P(("context", "tensor"), None),
        P(None, "tensor"),
        P("tensor", None),
        P("tensor"),
        P("tensor"),
        P("tensor"),
        P(),
        P("context", "tensor"),
    )
    return jax.shard_map(
        per_device,
        mesh=mesh,
        in_specs=placed,
        out_specs=(P("context", "tensor"), P(("context", "tensor"), None)),
        check_vma=False,
    )
```

```python
import jax
import jax.numpy as jnp
from jax import lax
from jax.experimental import pallas as pl
from jax.experimental.pallas import tpu as pltpu
from jax.sharding import PartitionSpec as P

BF = jnp.bfloat16
F32 = jnp.float32
MESH = pl.DeviceIdType.MESH

PLANES = 8
SPANS = 16
ROWS = 16
SPAN = 256
FEAT = 8192
HEADS = 8
HDIM = 64
XW = HEADS * HDIM
STATE = 128
PROJ = XW + 2 * STATE
WIDE = PROJ + 128
QUARTER = FEAT // 4
PART = XW // SPANS
SLOT = {0: 0, 1: 1, 7: 2, 2: 3, 6: 4, 3: 5, 5: 6, 4: 7}
NEAR = 5 * 32

NN = (((1,), (0,)), ((), ()))
NT = (((1,), (1,)), ((), ()))
TN = (((0,), (0,)), ((), ()))


def mm(a, b, dims=NN):
    return lax.dot_general(a, b, dims, preferred_element_type=F32)


def cols(quarter, count=1):
    return pl.ds(quarter * QUARTER, count * QUARTER)


def quantize(rows):
    lane = lax.broadcasted_iota(jnp.int32, rows.shape, 1)
    largest = jnp.abs(rows)
    for step in (1, 2, 4, 8, 16):
        below = pltpu.roll(largest, step, 1)
        above = pltpu.roll(largest, 128 - step, 1)
        largest = jnp.maximum(largest, jnp.where((lane & step) != 0, below, above))
    power = jnp.exp2(jnp.floor(jnp.log2(jnp.maximum(largest, 2.0**-39)))).astype(BF).astype(F32)
    power = jnp.where(power > largest, power * 0.5, power)
    power = jnp.where(power * 2.0 <= largest, power * 2.0, power)
    scale = jnp.where(largest >= 2.0**-39, power * 2.0**-8, 2.0**-48)
    lifted = rows * 2.0**20
    normal = (rows + lifted) - lifted
    anchor = scale * (1.5 * 2.0**14)
    small = (rows + anchor) - anchor
    snapped = jnp.where(jnp.abs(rows) < scale * 2.0**-6, small, normal)
    bound = scale * 448.0
    return jnp.clip(snapped, -bound, bound)


def split3(values):
    first = values.astype(BF)
    rest = values - first.astype(F32)
    second = rest.astype(BF)
    third = (rest - second.astype(F32)).astype(BF)
    return first, second, third


def sums(values, chosen):
    first, second, third = split3(values)
    stacked = jnp.concatenate(
        [first.astype(F32), second.astype(F32), third.astype(F32), jnp.zeros_like(values)], axis=0
    ).astype(BF)
    out = mm(stacked, chosen)
    return out[0:8] + out[8:16] + out[16:24]


def head_lanes(scalars):
    lane = lax.broadcasted_iota(jnp.int32, (8, 128), 1)
    out = jnp.zeros((8, 128), F32)
    for head in range(HEADS):
        out = jnp.where(lane == head, scalars[head], out)
    return out


def split2(values):
    high = values.astype(BF)
    return high, (values - high.astype(F32)).astype(BF)


def spread(values, spreader):
    return mm(jnp.concatenate(split2(values), axis=1), spreader)


def head_rows(head):
    return pl.ds(head * HDIM, HDIM)


def kernel(
    hid_hbm, w_hbm, wdt_ref, bias_hbm, alog_hbm, skip_hbm, docs_hbm, go_hbm,
    y_out, gh_out,
    hid, go, bias_ref, alog_ref, skip_ref, docs, in_sems,
    w, wt, xb, acc, bias_m, masks, spreader, gyt, pn, dn_, xn, dstn, bc, dte, kdd, crw, xk, ku, gw,
    ut, yt, dut, ds_, yn, pre, dbc, xs, xr, os_, or_, pgn, pga, sbr, ru_r, rd_r,
    wsem, au_s, au_r, ad_s, ad_r, ab_s, ab_r, x1s, x1r, x2s, x2r,
    bu_s, bu_r, bd_s, bd_r, bb_s, bb_r, bf_s, bf_r, bn_s, bn_r, heard,
):
    me = lax.axis_index("tensor")
    span = lax.axis_index("context")
    z = me // 2
    core = me % 2
    up = lax.rem(z + 1, PLANES) * 2 + core
    down = lax.rem(z + PLANES - 1, PLANES) * 2 + core
    twin = z * 2 + (1 - core)

    hid_copy = pltpu.make_async_copy(hid_hbm, hid, in_sems.at[0])
    hid_copy.start()

    barrier = pltpu.get_barrier_semaphore()
    for near in (up, down, twin):
        pl.semaphore_signal(barrier, inc=1, device_id={"tensor": near}, device_id_type=MESH)

    x, y = span % 4, span // 4
    beside = (y * 4 + lax.rem(x + 1, 4), y * 4 + lax.rem(x + 3, 4))
    across = (lax.rem(y + 1, 4) * 4 + x, lax.rem(y + 3, 4) * 4 + x)
    for near in beside + across:
        pl.semaphore_signal(barrier, inc=1, device_id={"context": near}, device_id_type=MESH)

    def tell(whom, sem):
        for near in whom:
            pl.semaphore_signal(sem, inc=1, device_id={"context": near}, device_id_type=MESH)

    def block(place, half, quarter, count):
        return xb.at[pl.ds(SLOT[place % PLANES] * 32 + half * 16, ROWS), cols(quarter, count)]

    def to_up(step, quarter, count):
        return pltpu.make_async_remote_copy(
            src_ref=block(-step, 0, quarter, count), dst_ref=block(-step - 1, 0, quarter, count),
            send_sem=au_s.at[step, quarter], recv_sem=au_r.at[step, quarter],
            device_id={"tensor": up}, device_id_type=MESH,
        )

    def to_down(step, quarter, count):
        return pltpu.make_async_remote_copy(
            src_ref=block(step, 0, quarter, count), dst_ref=block(step + 1, 0, quarter, count),
            send_sem=ad_s.at[step, quarter], recv_sem=ad_r.at[step, quarter],
            device_id={"tensor": down}, device_id_type=MESH,
        )

    def to_twin(place, quarter, count):
        place = place % PLANES
        return pltpu.make_async_remote_copy(
            src_ref=block(place, 0, quarter, count), dst_ref=block(place, 1, quarter, count),
            send_sem=ab_s.at[place, quarter], recv_sem=ab_r.at[place, quarter],
            device_id={"tensor": twin}, device_id_type=MESH,
        )

    quarters = ((0, 1), (1, 1), (2, 1), (3, 1))
    halves = ((0, 2), (2, 2))
    up_units = (quarters, halves, halves, quarters[:2])
    down_units = (quarters[2:] + quarters[:2], halves[::-1], halves[::-1], quarters[2:])
    twin_units = {0: ((0, 4),), 4: quarters}

    tiles = QUARTER // 128

    def encode(quarter):
        part = hid[:, quarter * QUARTER : (quarter + 1) * QUARTER].astype(F32)
        stacked = jnp.concatenate(
            [part[:, i * 128 : (i + 1) * 128] for i in range(tiles)], axis=0
        )
        snapped = quantize(stacked)
        flat = jnp.concatenate(
            [snapped[i * ROWS : (i + 1) * ROWS] for i in range(tiles)], axis=1
        )
        xb[0:ROWS, quarter * QUARTER : (quarter + 1) * QUARTER] = flat.astype(BF)

    later_copies = [
        pltpu.make_async_copy(source, target, in_sems.at[1 + at])
        for at, (source, target) in enumerate(
            (
                (docs_hbm, docs),
                (go_hbm, go),
                (bias_hbm, bias_ref),
                (alog_hbm, alog_ref),
                (skip_hbm, skip_ref),
            )
        )
    ]
    for copy in later_copies:
        copy.start()
    w_copy = pltpu.make_async_copy(w_hbm, w.at[:, 0:PROJ], wsem)
    w_copy.start()
    hid_copy.wait()
    encode(0)
    pl.semaphore_wait(barrier, 7)
    to_up(0, 0, 1).start()
    encode(2)
    to_down(0, 2, 1).start()
    encode(1)
    to_up(0, 1, 1).start()
    encode(3)
    to_down(0, 3, 1).start()
    to_up(0, 2, 1).start()
    to_down(0, 0, 1).start()
    to_up(0, 3, 1).start()
    to_down(0, 1, 1).start()
    to_twin(0, 0, 4).start()
    tell(beside, heard.at[0])

    for copy in later_copies:
        copy.wait()
    first_token = span * SPAN

    def segment(positions):
        out = jnp.full(positions.shape, -1, jnp.int32)
        begin = jnp.int32(0)
        for doc in range(8):
            out = out + jnp.where(positions >= begin, 1, 0)
            begin = begin + docs[doc]
        return out

    row_pos = first_token + lax.broadcasted_iota(jnp.int32, (SPAN, SPAN), 0)
    col_pos = first_token + lax.broadcasted_iota(jnp.int32, (SPAN, SPAN), 1)
    bias_m[...] = jnp.where(
        (row_pos >= col_pos) & (segment(row_pos) == segment(col_pos)), 0.0, -1e30
    )
    token = first_token + lax.broadcasted_iota(jnp.int32, (SPAN, 128), 0)
    seg = segment(token)
    none = jnp.zeros((8, 128), jnp.int32)
    seg_before = segment(none + (first_token - 1))
    seg_last = segment(none + (first_token + SPAN - 1))
    masks[0] = jnp.where(seg == seg_before[0:1], 1.0, 0.0)
    masks[1] = jnp.where(seg == seg_last[0:1], 1.0, 0.0)
    through = jnp.where(seg_last == seg_before, 1.0, 0.0)
    head_of_row = lax.rem(lax.broadcasted_iota(jnp.int32, (256, XW), 0), 128)
    head_of_lane = lax.broadcasted_iota(jnp.int32, (256, XW), 1) // HDIM
    spreader[...] = jnp.where(head_of_row == head_of_lane, 1.0, 0.0).astype(BF)
    gyt[...] = jnp.transpose(go[...].astype(F32)).astype(BF)

    for quarter in range(4):
        steps_w = wdt_ref[:, quarter * QUARTER : (quarter + 1) * QUARTER].astype(F32)
        padded = jnp.concatenate([steps_w, jnp.zeros((120, QUARTER), F32)], axis=0)
        w[cols(quarter), PROJ:WIDE] = jnp.transpose(padded).astype(BF)
        wt[PROJ:WIDE, cols(quarter)] = padded.astype(BF)
    square_row = lax.broadcasted_iota(jnp.int32, (256, 256), 0)
    square_lane = lax.broadcasted_iota(jnp.int32, (256, 256), 1)
    same = jnp.where(square_row == square_lane, 1.0, 0.0).astype(BF)
    units = [(quarter, first) for quarter in (0, 2, 1, 3) for first in range(0, PROJ, 256)]

    def turn_weights(count):
        for _ in range(count):
            quarter, first = units.pop(0)
            at = slice(first, first + 256)
            wt[at, cols(quarter)] = mm(same, w[cols(quarter), at], NT).astype(BF)

    def project(first, last, quarter, begin):
        at = slice(quarter * QUARTER, (quarter + 1) * QUARTER)
        part = mm(xb[first:last, at], w[at, :])
        if begin:
            acc[first:last, :] = part
        else:
            acc[first:last, :] += part

    def arrived_twin(place):
        for unit in twin_units.get(place, halves):
            to_twin(place, *unit).wait_recv()

    def between(step, turn):
        if (step, turn) == (0, 0):
            pl.semaphore_wait(heard.at[0], 2)
            tell(across, heard.at[1])
            w_copy.wait()
            turn_weights(3)
        elif (step, turn) == (0, 1):
            pl.semaphore_wait(heard.at[1], 2)
            tell(across, heard.at[2])
            turn_weights(3)
        elif (step, turn) == (1, 0):
            pl.semaphore_wait(heard.at[2], 2)
            turn_weights(4)
        elif (step, turn) == (1, 1):
            turn_weights(2)
            for place in (0, 1, 7, 2, 6):
                arrived_twin(place)
            project(0, NEAR, 0, True)
            project(0, NEAR, 1, False)
        elif (step, turn) == (2, 0):
            project(0, NEAR, 2, False)
            project(0, NEAR, 3, False)

    for step in range(3):
        for turn in range(2):
            unit = halves[turn]
            for got in quarters[2 * turn : 2 * turn + 2] if step == 0 else (unit,):
                to_up(step, *got).wait_recv()
            if step < 2:
                to_up(step + 1, *unit).start()
            elif turn == 0:
                for part in up_units[3]:
                    to_up(3, *part).start()
            to_twin(-step - 1, *unit).start()
            unit = halves[1 - turn]
            for got in quarters[2 - 2 * turn : 4 - 2 * turn] if step == 0 else (unit,):
                to_down(step, *got).wait_recv()
            if step < 2:
                to_down(step + 1, *unit).start()
            elif turn == 0:
                for part in down_units[3]:
                    to_down(3, *part).start()
            to_twin(step + 1, *unit).start()
            between(step, turn)
    for at in range(2):
        to_up(3, *up_units[3][at]).wait_recv()
        to_twin(4, *up_units[3][at]).start()
        to_down(3, *down_units[3][at]).wait_recv()
        to_twin(4, *down_units[3][at]).start()
    arrived_twin(3)
    arrived_twin(5)
    for quarter in (0, 2, 1, 3):
        to_twin(4, quarter, 1).wait_recv()
        project(NEAR, SPAN, quarter, quarter == 0)

    def home(place, half):
        owner = lax.rem(z + place, PLANES) * 2 + (core if half == 0 else 1 - core)
        return pl.ds(pl.multiple_of(owner * ROWS, ROWS), ROWS)

    for place in range(PLANES):
        for half in range(2):
            at = SLOT[place] * 32 + half * 16
            pn[home(place, half), :] = acc[at : at + 16, 0:PROJ].astype(BF).astype(F32)
            dn_[home(place, half), :] = acc[at : at + 16, PROJ:WIDE]

    row = lax.broadcasted_iota(jnp.int32, (SPAN, SPAN), 0)
    lane = lax.broadcasted_iota(jnp.int32, (SPAN, SPAN), 1)
    rate = -jnp.exp(head_lanes(alog_ref))
    skip = head_lanes(skip_ref)
    dt_arg = dn_[...] + head_lanes(bias_ref)[0:1]
    dt = jnp.maximum(dt_arg, 0.0) + jnp.log1p(jnp.exp(-jnp.abs(dt_arg)))
    dt_gate = 1.0 / (1.0 + jnp.exp(-dt_arg))
    summed = mm(
        jnp.where(row >= lane, 1.0, 0.0).astype(BF),
        jnp.concatenate(split3(dt * rate[0:1]), axis=1),
    )
    cum = summed[:, 0:128] + summed[:, 128:256] + summed[:, 256:384]
    cum_last = cum[SPAN - 1 : SPAN]
    carry_w = jnp.exp(cum) * masks[0]
    keep_w = jnp.exp(cum_last - cum) * masks[1]
    total = jnp.exp(jnp.broadcast_to(cum_last, (8, 128))) * through
    keep_dt = spread(keep_w * dt, spreader[...])
    crw[...] = spread(carry_w, spreader[...])
    projected = pn[...]
    gate = 1.0 / (1.0 + jnp.exp(-projected))
    dstn[...] = gate * (1.0 + projected * (1.0 - gate))
    active = projected * gate
    xn[...] = active[:, 0:XW]
    bc[...] = active[:, XW:PROJ].astype(BF)
    b_nat = bc[:, 0:STATE]
    c_nat = bc[:, STATE : 2 * STATE]
    b_t = jnp.transpose(active[:, XW : XW + STATE]).astype(BF)
    c_t = jnp.transpose(active[:, XW + STATE : PROJ]).astype(BF)
    ku[...] = (xn[...] * keep_dt).astype(BF)
    gw[...] = (go[...].astype(F32) * crw[...]).astype(BF)
    end_state = mm(b_t, ku[...]).astype(BF)
    from_out = mm(c_t, gw[...]).astype(BF)
    note_row = lax.broadcasted_iota(jnp.int32, (16, 128), 0)
    high, low_part = split2(total[0:1])
    note = jnp.where(note_row == 0, high.astype(F32), jnp.where(note_row == 1, low_part.astype(F32), 0.0))
    note = mm(note.astype(BF), spreader[0:128, :]).astype(BF)
    for part in range(SPANS):
        at = slice(part % 4 * PART, part % 4 * PART + PART)
        pair = slice(part // 4 * 128, part // 4 * 128 + 128)
        xs[part, 0:PART, :] = end_state[at, pair]
        xs[part, PART : 2 * PART, :] = from_out[at, pair]
        xs[part, 2 * PART : 2 * PART + 16, :] = note[:, pair]

    def other(step):
        return lax.rem(span + step, SPANS)

    def out1(step):
        return pltpu.make_async_remote_copy(
            src_ref=xs.at[other(step)], dst_ref=xr.at[span],
            send_sem=x1s.at[other(step)], recv_sem=x1r.at[span],
            device_id={"context": other(step)}, device_id_type=MESH,
        )

    def in1(step):
        return pltpu.make_async_remote_copy(
            src_ref=xs.at[other(step)], dst_ref=xr.at[other(step)],
            send_sem=x1s.at[other(step)], recv_sem=x1r.at[other(step)],
            device_id={"context": other(step)}, device_id_type=MESH,
        )

    def out2(step):
        return pltpu.make_async_remote_copy(
            src_ref=os_.at[other(step)], dst_ref=or_.at[span],
            send_sem=x2s.at[other(step)], recv_sem=x2r.at[span],
            device_id={"context": other(step)}, device_id_type=MESH,
        )

    def in2(step):
        return pltpu.make_async_remote_copy(
            src_ref=os_.at[other(step)], dst_ref=or_.at[other(step)],
            send_sem=x2s.at[other(step)], recv_sem=x2r.at[other(step)],
            device_id={"context": other(step)}, device_id_type=MESH,
        )

    def every(action):
        for step in (10, 9, 11, 6, 14, 8, 2, 5, 7, 13, 15, 4, 12, 1, 3):
            action(step)

    every(lambda step: out1(step).start())
    xr[span] = xs[span]

    dte[...] = spread(dt, spreader[...])
    xk[...] = (xn[...] * spread(keep_w, spreader[...])).astype(BF)
    kdd[...] = keep_dt * dstn[:, 0:XW]
    ut[...] = jnp.transpose(xn[...] * dte[...]).astype(BF)
    cum_row = jnp.transpose(cum)
    scores = mm(c_nat, b_t)
    low = jnp.where(lax.broadcasted_iota(jnp.int32, (1, 128), 1) < HDIM, 1.0, 0.0).astype(BF)
    high_half = jnp.where(lax.broadcasted_iota(jnp.int32, (1, 128), 1) < HDIM, 0.0, 1.0).astype(BF)

    def inner(head):
        at = head_rows(head)
        pair = head // 2 * 128
        gap = cum[:, head : head + 1] - cum_row[head : head + 1, :] + bias_m[...]
        decay = jnp.exp(gap)
        mixing = (scores * decay).astype(BF)
        yt[at, :] = mm(ut[at, :], mixing, NT)
        dut[at, :] = mm(gyt[at, :], mixing)
        picked = go[:, pair : pair + 128] * (low if head % 2 == 0 else high_half)
        products = mm(picked, ut[pair : pair + 128, :])
        if head == 0:
            ds_[...] = products * decay
        else:
            ds_[...] += products * decay

    for head in range(HEADS // 2):
        inner(head)

    every(lambda step: in1(step).wait_recv())
    forward = jnp.zeros((PART, STATE), F32)
    back = jnp.zeros((PART, STATE), F32)
    for source in range(SPANS):
        os_[source, 0:PART, :] = forward.astype(BF)
        decays = xr[source, 2 * PART : 2 * PART + 16, :].astype(F32)
        forward = (decays[0:1] + decays[1:2]) * forward + xr[source, 0:PART, :].astype(F32)
        later = SPANS - 1 - source
        os_[later, PART : 2 * PART, :] = back.astype(BF)
        decays = xr[later, 2 * PART : 2 * PART + 16, :].astype(F32)
        back = (decays[0:1] + decays[1:2]) * back + xr[later, PART : 2 * PART, :].astype(F32)
    every(lambda step: out2(step).start())
    or_[span] = os_[span]

    for head in range(HEADS // 2, HEADS):
        inner(head)
    ds = ds_[...].astype(BF)
    dbc[:, 0:STATE] = mm(ds, c_nat, TN)
    dbc[:, STATE : 2 * STATE] = mm(ds, b_nat)
    gap_grad, direct = [], []
    for head in range(HEADS):
        at = head_rows(head)
        x_dt = ut[at, :].astype(F32)
        gap_grad.append(
            jnp.sum(gyt[at, :].astype(F32) * yt[at, :] - x_dt * dut[at, :], axis=0, keepdims=True)
        )
    yn[...] = jnp.transpose(yt[...])
    du_here = jnp.transpose(dut[...])
    skip_all = spread(skip, spreader[...])[0:1]
    x_here = xn[...]
    given = go[...].astype(F32)
    pre[...] = (du_here * dte[...] + given * skip_all) * dstn[:, 0:XW]
    yn[...] = yn[...] + x_here * skip_all
    direct = mm(
        jnp.concatenate(split2(x_here * du_here), axis=0), spreader[0:128, :], NT
    )
    direct = direct[0:SPAN] + direct[SPAN : 2 * SPAN]
    log_rows = sums(
        jnp.concatenate(gap_grad, axis=0), jnp.where(row >= lane, 1.0, 0.0).astype(BF)
    )
    log_here = jnp.transpose(
        jnp.concatenate([log_rows, jnp.zeros((120, SPAN), F32)], axis=0)
    )
    since_before = jnp.concatenate(
        [jnp.where(row <= lane, 1.0, 0.0).astype(BF), jnp.where(row > lane, 1.0, 0.0).astype(BF)],
        axis=1,
    )

    every(lambda step: in2(step).wait_recv())

    def gathered(first):
        return jnp.concatenate(
            [
                jnp.concatenate(
                    [or_[pair * 4 + part, first : first + PART, :] for part in range(4)], axis=0
                )
                for pair in range(4)
            ],
            axis=1,
        )

    state_in = gathered(0)
    state_grad = gathered(PART)
    carried = mm(c_nat, state_in)
    reach = mm(b_nat, state_grad)
    pgn[:, 0:XW] = (pre[...] + reach * kdd[...]).astype(BF)
    db = dbc[:, 0:STATE] + mm(ku[...], state_grad, NT)
    dc = dbc[:, STATE : 2 * STATE] + mm(gw[...], state_in, NT)
    pgn[:, XW : XW + STATE] = (db * dstn[:, XW : XW + STATE]).astype(BF)
    pgn[:, XW + STATE : PROJ] = (dc * dstn[:, XW + STATE : PROJ]).astype(BF)
    ends = jnp.sum(
        (state_in.astype(F32) * state_grad.astype(F32)).reshape(STATE // 8, 8, XW), axis=0
    )
    products = jnp.concatenate(
        [
            (gw[...].astype(F32) * carried).astype(BF),
            (ku[...].astype(F32) * reach).astype(BF),
            (xk[...].astype(F32) * reach).astype(BF),
            jnp.concatenate(split2(jnp.concatenate([ends, ends], axis=0)), axis=0),
        ],
        axis=0,
    )
    reduced = mm(products, spreader[0:128, :], NT)
    far_grad = mm(
        since_before, jnp.concatenate(split2(reduced[0 : 2 * SPAN]), axis=1)
    )
    far_grad = far_grad[:, 0:128] + far_grad[:, 128:256]
    end_grad = reduced[3 * SPAN : 3 * SPAN + 8] + reduced[3 * SPAN + 16 : 3 * SPAN + 24]
    end_grad = jnp.sum(end_grad, axis=0, keepdims=True)
    log_grad = log_here + far_grad + total[0:1] * end_grad
    dt_grad = (direct + reduced[2 * SPAN : 3 * SPAN] + rate[0:1] * log_grad) * dt_gate
    pgn[:, PROJ:WIDE] = dt_grad.astype(BF)
    yn[...] = yn[...] + carried * crw[...]

    for step in range(4):
        for unit in up_units[step]:
            to_up(step, *unit).wait_send()
        for unit in down_units[step]:
            to_down(step, *unit).wait_send()
    for place in range(PLANES):
        for unit in twin_units.get(place, halves):
            to_twin(place, *unit).wait_send()
    own, sbs = xb.at[0:128, :], xb.at[128:256, :]
    for place in range(PLANES):
        for half in range(2):
            slot = SLOT[place]
            if slot == 7:
                at = half * 16
            elif slot >= 5:
                at = 32 + half * 32 + (slot - 5) * 16
            else:
                at = 96 + half * 80 + slot * 16
            pga[at : at + 16, :] = pgn[home(place, half), :]

    def multiply(quarter, begin, first, last):
        count = last - first
        rows = pga[begin : begin + 2 * count, :]
        term = mm(rows, wt[:, cols(quarter)]).astype(BF)
        own[first:last, cols(quarter)] = term[0:count]
        sbs[first:last, cols(quarter)] = term[count : 2 * count]

    def multiply_far(quarter):
        multiply(quarter, 0, 112, 128)
        swap_far(quarter).start()

    def multiply_next(quarter):
        multiply(quarter, 32, 80, 112)
        swap_next(quarter).start()

    def multiply_rest(quarter):
        multiply(quarter, 96, 0, 80)
        swap_rest(quarter).start()

    def swap(quarter, first, last, sems):
        return pltpu.make_async_remote_copy(
            src_ref=sbs.at[first:last, cols(quarter)], dst_ref=sbr.at[first:last, cols(quarter)],
            send_sem=sems[0].at[quarter], recv_sem=sems[1].at[quarter],
            device_id={"tensor": twin}, device_id_type=MESH,
        )

    def swap_far(quarter):
        return swap(quarter, 112, 128, (bf_s, bf_r))

    def swap_next(quarter):
        return swap(quarter, 80, 112, (bn_s, bn_r))

    def swap_rest(quarter):
        return swap(quarter, 0, 80, (bb_s, bb_r))

    def place_rows(place):
        return pl.ds(SLOT[place % PLANES] * 16, 16)

    def pass_up(step, quarter, count):
        return pltpu.make_async_remote_copy(
            src_ref=own.at[place_rows(4 - step), cols(quarter, count)], dst_ref=ru_r.at[step, :, cols(quarter, count)],
            send_sem=bu_s.at[step, quarter], recv_sem=bu_r.at[step, quarter],
            device_id={"tensor": up}, device_id_type=MESH,
        )

    def pass_down(step, quarter, count):
        return pltpu.make_async_remote_copy(
            src_ref=own.at[place_rows(4 + step), cols(quarter, count)], dst_ref=rd_r.at[step, :, cols(quarter, count)],
            send_sem=bd_s.at[step, quarter], recv_sem=bd_r.at[step, quarter],
            device_id={"tensor": down}, device_id_type=MESH,
        )

    def pair_sum(place, quarter, count):
        at = place_rows(place)
        where = cols(quarter, count)
        return own[at, where].astype(F32) + sbr[at, where].astype(F32)

    def go_up(step, quarter):
        value = pair_sum(4 - step, quarter, 1)
        if step > 1 or (step == 1 and quarter < 2):
            pass_up(step - 1, quarter, 1).wait_recv()
            value = value + ru_r[step - 1, :, cols(quarter)].astype(F32)
        own[place_rows(4 - step), cols(quarter)] = value.astype(BF)
        pass_up(step, quarter, 1).start()

    def go_down(step, quarter):
        value = pair_sum(4 + step, quarter, 1)
        if step > 1 or (step == 1 and quarter >= 2):
            pass_down(step - 1, quarter, 1).wait_recv()
            value = value + rd_r[step - 1, :, cols(quarter)].astype(F32)
        own[place_rows(4 + step), cols(quarter)] = value.astype(BF)
        pass_down(step, quarter, 1).start()

    def first_pass(quarter):
        swap_far(quarter).wait_recv()
        (go_up if quarter < 2 else go_down)(0, quarter)

    for quarter in (0, 2, 1, 3):
        multiply_far(quarter)
    for quarter, ready in ((2, 0), (0, 2), (3, 1), (1, 3)):
        multiply_next(quarter)
        first_pass(ready)
    up_order, down_order = (2, 3, 0, 1), (0, 1, 2, 3)
    seen = set()
    for step in (1, 2, 3):
        for up_quarter, down_quarter in zip(up_order, down_order):
            for quarter in (up_quarter, down_quarter):
                if step == 1 and quarter not in seen:
                    swap_next(quarter).wait_recv()
                    seen.add(quarter)
            go_up(step, up_quarter)
            go_down(step, down_quarter)
            if step == 1:
                multiply_rest(up_quarter)
        if step == 1:
            for quarter in range(4):
                swap_rest(quarter).wait_recv()
            y_out[...] = yn[...].astype(BF)

    for up_quarter, down_quarter in zip(up_order, down_order):
        pass_up(3, up_quarter, 1).wait_recv()
        pass_down(3, down_quarter, 1).wait_recv()
        if up_quarter < 2:
            for quarter in (up_quarter, down_quarter):
                value = pair_sum(0, quarter, 1)
                value = value + ru_r[3, :, cols(quarter)].astype(F32)
                value = value + rd_r[3, :, cols(quarter)].astype(F32)
                gh_out[:, cols(quarter)] = value.astype(BF)

    for quarter in range(4):
        swap_far(quarter).wait_send()
        swap_next(quarter).wait_send()
        swap_rest(quarter).wait_send()
    for step in range(4):
        for unit in quarters[:2] if step == 0 else quarters:
            pass_up(step, *unit).wait_send()
        for unit in quarters[2:] if step == 0 else quarters:
            pass_down(step, *unit).wait_send()
    every(lambda step: out1(step).wait_send())
    every(lambda step: out2(step).wait_send())


def place_results(y_in, gh_in, y_out, gh_out, sems):
    y_copy = pltpu.make_async_copy(y_in, y_out, sems.at[0])
    gh_copy = pltpu.make_async_copy(gh_in, gh_out, sems.at[1])
    gh_copy.start()
    y_copy.start()
    gh_copy.wait()
    y_copy.wait()


def per_device(hidden, w_proj, w_dt, dt_bias, a_log, d_skip, doc_lengths, grad_out):
    vmem = pl.BlockSpec(memory_space=pltpu.VMEM)
    dma = pltpu.SemaphoreType.DMA
    whole = pl.BlockSpec(memory_space=pl.ANY)
    results = pl.pallas_call(
        kernel,
        out_shape=(
            pltpu.VMEM((SPAN, XW), BF),
            pltpu.VMEM((ROWS, FEAT), BF),
        ),
        in_specs=[whole, whole, vmem, whole, whole, whole, whole, whole],
        out_specs=(vmem, vmem),
        scratch_shapes=[
            pltpu.VMEM((ROWS, FEAT), BF),
            pltpu.VMEM((SPAN, XW), BF),
            pltpu.SMEM((HEADS,), F32),
            pltpu.SMEM((HEADS,), F32),
            pltpu.SMEM((HEADS,), F32),
            pltpu.SMEM((8,), jnp.int32),
            dma((6,)),
            pltpu.VMEM((FEAT, WIDE), BF),
            pltpu.VMEM((WIDE, FEAT), BF),
            pltpu.VMEM((SPAN, FEAT), BF),
            pltpu.VMEM((SPAN, WIDE), F32),
            pltpu.VMEM((SPAN, SPAN), F32),
            pltpu.VMEM((2, SPAN, 128), F32),
            pltpu.VMEM((256, XW), BF),
            pltpu.VMEM((XW, SPAN), BF),
            pltpu.VMEM((SPAN, PROJ), F32),
            pltpu.VMEM((SPAN, 128), F32),
            pltpu.VMEM((SPAN, XW), F32),
            pltpu.VMEM((SPAN, PROJ), F32),
            pltpu.VMEM((SPAN, 2 * STATE), BF),
            pltpu.VMEM((SPAN, XW), F32),
            pltpu.VMEM((SPAN, XW), F32),
            pltpu.VMEM((SPAN, XW), F32),
            pltpu.VMEM((SPAN, XW), BF),
            pltpu.VMEM((SPAN, XW), BF),
            pltpu.VMEM((SPAN, XW), BF),
            pltpu.VMEM((XW, SPAN), BF),
            pltpu.VMEM((XW, SPAN), F32),
            pltpu.VMEM((XW, SPAN), F32),
            pltpu.VMEM((SPAN, SPAN), F32),
            pltpu.VMEM((SPAN, XW), F32),
            pltpu.VMEM((SPAN, XW), F32),
            pltpu.VMEM((SPAN, 2 * STATE), F32),
            pltpu.VMEM((SPANS, 2 * PART + 16, STATE), BF),
            pltpu.VMEM((SPANS, 2 * PART + 16, STATE), BF),
            pltpu.VMEM((SPANS, 2 * PART, STATE), BF),
            pltpu.VMEM((SPANS, 2 * PART, STATE), BF),
            pltpu.VMEM((SPAN, WIDE), BF),
            pltpu.VMEM((SPAN, WIDE), BF),
            pltpu.VMEM((128, FEAT), BF),
            pltpu.VMEM((4, ROWS, FEAT), BF),
            pltpu.VMEM((4, ROWS, FEAT), BF),
            dma,
            dma((4, 4)), dma((4, 4)), dma((4, 4)), dma((4, 4)),
            dma((PLANES, 4)), dma((PLANES, 4)),
            dma((SPANS,)), dma((SPANS,)), dma((SPANS,)), dma((SPANS,)),
            dma((4, 4)), dma((4, 4)), dma((4, 4)), dma((4, 4)),
            dma((4,)), dma((4,)), dma((4,)), dma((4,)), dma((4,)), dma((4,)),
            pltpu.SemaphoreType.REGULAR((3,)),
        ],
        compiler_params=pltpu.CompilerParams(
            collective_id=0, has_side_effects=True, vmem_limit_bytes=58 * 1024 * 1024
        ),
        name="layer",
    )(hidden, w_proj, w_dt, dt_bias, a_log, d_skip, doc_lengths, grad_out)
    return pl.pallas_call(
        place_results,
        out_shape=(
            jax.ShapeDtypeStruct((SPAN, XW), BF),
            jax.ShapeDtypeStruct((ROWS, FEAT), BF),
        ),
        in_specs=[vmem, vmem],
        out_specs=(whole, whole),
        scratch_shapes=[dma((2,))],
        name="place_results",
    )(*(pltpu.with_memory_space_constraint(part, pltpu.VMEM) for part in results))


def solution(mesh):
    placed = (
        P(("context", "tensor"), None),
        P(None, "tensor"),
        P("tensor", None),
        P("tensor"),
        P("tensor"),
        P("tensor"),
        P(),
        P("context", "tensor"),
    )
    return jax.shard_map(
        per_device,
        mesh=mesh,
        in_specs=placed,
        out_specs=(P("context", "tensor"), P(("context", "tensor"), None)),
        check_vma=False,
    )
```
